256 devices in a mesh: gx: 8 (over y, core), gy: 32 (over x, z).
Axes of the slice: x: 4, y: 4, z: 8, core: 2. Of those that a mesh axis runs over, the one named last changes fastest.
Arguments:
- features: bfloat16 [131072, 128], P(('gx', 'gy')), may hold values from -6 to 6
- point_slab: int32 [131072, 1], P(('gx', 'gy')), may hold values from 0 to 31; in each aligned block of 512 rows (0 to 511, 512 to 1023, ...) at most 48 rows name the same one
- base_cell: int32 [131072], P(('gx', 'gy')), may hold values from 0 to 366, as said below
- nearest: int32 [131072], P(('gx', 'gy')), may hold values from 0 to 7
- offsets: bfloat16 [3, 131072], P(None, ('gx', 'gy')), may hold values from 0 to 1
- conv_weight: bfloat16 [27, 128, 128], replicated, may hold values from -0.109375 to 0.109375
- mlp_weight: bfloat16 [128, 128], replicated, may hold values from -0.5 to 0.5
- cotangent: bfloat16 [131072, 128], P(('gx', 'gy')), may hold values from -6 to 6
Outputs:
- output: bfloat16 [131072, 128], P(('gx', 'gy'))
- grad_features: bfloat16 [131072, 128], P(('gx', 'gy'))
- grad_conv: float32 [27, 128, 128], replicated
- grad_mlp: float32 [128, 128], replicated
The draws below stay inside these ranges and needn't reach their ends.
Inputs may be any that keep to these rules, and one draw needn't show every extreme that they name: `point_slab`: in the rows of one device at most 48 points name the same slab, a bound that some block reaches of them. `base_cell`: each entry is (a * 8 + b) * 16 + c with a < 3, b < 7, c < 15.
All inputs are finite; a program needn't handle non-finite values.
Results may differ from the reference program's by a relative error of at most 0.0058.
Values may be sent and summed in bfloat16 or wider, within the bound.
No kernel may reach another device: no remote copies, remote signals or barrier semaphores. Data moves between devices by JAX's collectives and lax.ppermute only.
A program may use at most 64 MiB of HBM per device.

```python
import math
import jax
import jax.numpy as jnp
import numpy as np
from jax import lax

C = 128
VX_DEV = 4
VY_DEV = 8
Z = 16
PTS_DEV = 512
CAP = 48
POINTS = 131072
GRID_X = 32
GRID_Y = 256
N_GY = 32


def draw_base_cell(key, part):
    key = jax.random.fold_in(key, 11)
    subkeys = jax.random.split(key, 5)
    point_count = POINTS
    x_local = jax.random.randint(subkeys[0], (point_count,), 0, VX_DEV - 1)
    y_local = jax.random.randint(subkeys[1], (point_count,), 0, VY_DEV - 1)
    z_local = jax.random.randint(subkeys[2], (point_count,), 0, Z - 1)
    flattened = (x_local * VY_DEV + y_local) * Z + z_local
    highest = ((VX_DEV - 2) * VY_DEV + VY_DEV - 2) * Z + Z - 2
    first_row = jax.random.randint(subkeys[3], (), 0, point_count)
    second_row = (first_row + 1 + jax.random.randint(subkeys[4], (), 0, point_count - 1)) % point_count
    row_index = jnp.arange(point_count, dtype=jnp.int32)
    flattened = jnp.where(row_index == first_row, highest, flattened)
    flattened = jnp.where(row_index == second_row, 0, flattened)
    return flattened.astype(jnp.int32)


def set_ends(drawn, rng, least, top_value):
    extent = drawn.shape
    index_at = [jax.random.randint(jax.random.fold_in(rng, axis), (), 0, extent[axis]) for axis in range(len(extent))]
    drawn = drawn.at[tuple(index_at)].set(least)
    longest = extent.index(max(extent))
    index_at[longest] = (index_at[longest] + 1) % extent[longest]
    return drawn.at[tuple(index_at)].set(top_value)


def levels(key, extent, cuts, low, largest):
    gain = 1.0
    for position, shards_of in cuts:
        steps = jax.random.uniform(jax.random.fold_in(jax.random.fold_in(key, 6), position), (shards_of,), jnp.float32, low / len(cuts), largest / len(cuts))
        gain = gain * jnp.repeat(jnp.exp(steps), extent[position] // shards_of).reshape((-1,) + (1,) * (len(extent) - 1 - position))
    return gain


def routed_block(key, own, number, rows, amount, top, bound, lean):
    order = jax.random.permutation(key, amount)
    crowded, usual = shares(amount, rows * top, bound, lean, True), shares(amount, rows * top, bound, lean, False)
    places = jnp.arange(amount)

    def named(tallies, offset_by):
        used = int((tallies > 0).sum())
        fixed = max(1, used // 4)
        passed = fixed + (places - fixed + offset_by * (used - fixed)) % max(1, amount - fixed)
        return jnp.zeros((amount,), jnp.int32).at[order[jnp.where(places < fixed, places, passed)]].set(jnp.asarray(tallies, jnp.int32))

    tallies = jnp.where(number % 4 == 0, named(crowded, number // 4), named(usual, number - number // 4 - 1))
    mixed = jax.random.permutation(jax.random.fold_in(own, 3), amount)
    source_of, sink = mixed[0:amount // 2 * 2:2], mixed[1:amount // 2 * 2:2]
    room = jnp.minimum(tallies[source_of] - 1, bound - tallies[sink]) // 2
    room = jnp.where((source_of == order[0]) | (sink == order[0]) | (tallies[sink] == 0), 0, jnp.maximum(room, 0))
    passed = jax.random.randint(jax.random.fold_in(own, 4), (amount // 2,), 0, 1 << 20) % (room + 1)
    tallies = tallies.at[source_of].add(-passed).at[sink].add(passed)
    members = jnp.searchsorted(jnp.cumsum(tallies), jnp.arange(rows * top), side="right").astype(jnp.int32)
    grid = members.reshape(top, rows).T
    grid = grid[jax.random.permutation(jax.random.fold_in(own, 1), rows)]
    offset_by = jax.random.randint(jax.random.fold_in(own, 2), (rows, 1), 0, top)
    return jnp.take_along_axis(grid, (jnp.arange(top)[None, :] + offset_by) % top, axis=1)


def shares(count, total, bound, lean, full):
    weights = [(1 << 20) // math.isqrt(rank ** lean) + 1 for rank in range(1, count + 1)]
    largest = bound if full else min(bound, max(-(-total // count), total * weights[0] // sum(weights)))
    least = 1 if total - largest >= count - 1 else 0
    given, spare = [largest] + [least] * (count - 1), total - largest - least * (count - 1)
    while spare > 0:
        movable = [i for i in range(1, count) if given[i] < largest] or [i for i in range(1, count) if given[i] < bound]
        whole, left = sum([weights[i] for i in movable]), spare
        for i in movable:
            extra = min(bound - given[i], max(1, left * weights[i] // whole), spare)
            given[i] = given[i] + extra
            spare = spare - extra
    return np.array(given)


def centred(key, dims, scale, reach, cuts=(), held_as=jnp.bfloat16):
    gain = levels(key, dims, cuts, -0.22, 0.18) if cuts else 1.0
    entries = jax.random.normal(key, dims, jnp.float32) * scale * gain
    return jnp.minimum(jnp.maximum(entries, -reach), reach).astype(held_as)


def setup_inputs(seed: int = 0) -> dict:
    streams_of = jax.random.split(jax.random.key(seed), 9)
    features = centred(streams_of[0], (POINTS, C), 1.0, 6.0, ((0, 256),))
    point_slab_keys = jax.random.split(jax.random.fold_in(streams_of[1], 1), POINTS // PTS_DEV)
    point_slab_turns = jax.random.permutation(jax.random.fold_in(streams_of[1], 3), POINTS // PTS_DEV)
    point_slab = jax.vmap(lambda own, number: routed_block(jax.random.fold_in(streams_of[1], 2), own, number, PTS_DEV, N_GY, 1, CAP, 2))(point_slab_keys, point_slab_turns).reshape((POINTS, 1))
    base_cell = draw_base_cell(jax.random.fold_in(streams_of[8], 71), 0)
    nearest = set_ends(jax.random.randint(streams_of[3], (POINTS,), 0, 8), jax.random.fold_in(streams_of[3], 1), 0, 7).astype(jnp.int32)
    offsets = jnp.clip(1.0 * jax.random.uniform(streams_of[4], (3, POINTS), jnp.float32) ** levels(streams_of[4], (3, POINTS), ((1, 256),), -0.2, 0.2), 0.0, 1.0).astype(jnp.bfloat16)
    conv_weight = centred(streams_of[5], (27, C, C), (27 * C) ** -0.5, 0.109375)
    mlp_weight = centred(streams_of[6], (C, C), C ** -0.5, 0.5)
    cotangent = centred(streams_of[7], (POINTS, C), 1.0, 6.0, ((0, 256),))
    return {"features": features, "point_slab": point_slab, "base_cell": base_cell, "nearest": nearest, "offsets": offsets, "conv_weight": conv_weight, "mlp_weight": mlp_weight, "cotangent": cotangent}


def sigmoid_slope(pre_act):
    sigmoid_value = jax.nn.sigmoid(pre_act)
    return sigmoid_value * (1.0 + pre_act * (1.0 - sigmoid_value))

def convolve(padded, kernel_stack, block_shape, flipped):
    x_cells, y_cells, z_cells = block_shape
    channels = padded.shape[3]
    accumulated = jnp.zeros((x_cells * y_cells * z_cells, kernel_stack.shape[2]), jnp.float32)
    for offset in range(27):
        x_shift = offset // 9
        y_shift = offset // 3 % 3
        z_shift = offset % 3
        if flipped:
            starts = (2 - x_shift, 2 - y_shift, 2 - z_shift)
            kernel = kernel_stack[offset].T
        else:
            starts = (x_shift, y_shift, z_shift)
            kernel = kernel_stack[offset]
        window = lax.slice(padded, (starts[0], starts[1], starts[2], 0), (starts[0] + x_cells, starts[1] + y_cells, starts[2] + z_cells, channels))
        accumulated = accumulated + jnp.dot(window.reshape(-1, channels), kernel, preferred_element_type=jnp.float32)
    return accumulated

def weight_gradient(padded, grad_hidden, block_shape):
    x_cells, y_cells, z_cells = block_shape
    channels = padded.shape[3]
    pieces = []
    for offset in range(27):
        x_shift = offset // 9
        y_shift = offset // 3 % 3
        z_shift = offset % 3
        window = lax.slice(padded, (x_shift, y_shift, z_shift, 0), (x_shift + x_cells, y_shift + y_cells, z_shift + z_cells, channels))
        pieces.append(lax.dot_general(window.reshape(-1, channels), grad_hidden, (((0,), (0,)), ((), ())), preferred_element_type=jnp.float32))
    return jnp.stack(pieces)

def trilinear(offsets, base_cell, plane_cells, z_cells):
    fraction = offsets.astype(jnp.float32)
    weights = []
    corners = []
    for corner in range(8):
        x_bit = corner // 4
        y_bit = corner // 2 % 2
        z_bit = corner % 2
        factor = fraction[0] if x_bit else 1.0 - fraction[0]
        factor = factor * (fraction[1] if y_bit else 1.0 - fraction[1])
        factor = factor * (fraction[2] if z_bit else 1.0 - fraction[2])
        factor = lax.optimization_barrier(factor.astype(jnp.bfloat16)).astype(jnp.float32)
        weights.append(factor)
        corners.append(base_cell + x_bit * plane_cells + y_bit * z_cells + z_bit)
    return (weights, corners)

def reference(features, point_slab, base_cell, nearest, offsets, conv_weight, mlp_weight, cotangent):
    point_count = features.shape[0]
    row_index = jnp.arange(point_count, dtype=jnp.int32)
    strip_index = row_index // (PTS_DEV * N_GY)
    target = point_slab[:, 0]
    plane_cells = VY_DEV * Z

    def global_cell(local_cell):
        x_local = local_cell // plane_cells
        y_local = local_cell // Z % VY_DEV
        z_local = local_cell % Z
        return ((strip_index * VX_DEV + x_local) * GRID_Y + target * VY_DEV + y_local) * Z + z_local
    cells_all = GRID_X * GRID_Y * Z
    own_cell = base_cell + nearest // 4 * plane_cells + nearest // 2 % 2 * Z + nearest % 2
    voxel_ids = global_cell(own_cell)
    voxel_sums = jax.ops.segment_sum(features.astype(jnp.float32), voxel_ids, cells_all)
    counts = jax.ops.segment_sum(jnp.ones((point_count,), jnp.float32), voxel_ids, cells_all)
    divisor = jnp.maximum(counts, 1.0)
    voxels = (voxel_sums / divisor[:, None]).astype(jnp.bfloat16).reshape(GRID_X, GRID_Y, Z, C)
    padded = jnp.pad(voxels, ((1, 1), (1, 1), (1, 1), (0, 0)))
    block_shape = (GRID_X, GRID_Y, Z)
    hidden = convolve(padded, conv_weight, block_shape, False)
    conv_out = jax.nn.silu(hidden).astype(jnp.bfloat16)
    weights, corners = trilinear(offsets, base_cell, plane_cells, Z)
    corner_ids = [global_cell(corners[corner]) for corner in range(8)]
    sampled = jnp.zeros((point_count, C), jnp.float32)
    for corner in range(8):
        sampled = sampled + weights[corner][:, None] * conv_out[corner_ids[corner]].astype(jnp.float32)
    sampled = sampled.astype(jnp.bfloat16)
    pre_mlp = jnp.dot(features, mlp_weight, preferred_element_type=jnp.float32)
    output = (sampled.astype(jnp.float32) + jax.nn.silu(pre_mlp)).astype(jnp.bfloat16)
    upstream = cotangent.astype(jnp.float32)
    grad_pre = (upstream * sigmoid_slope(pre_mlp)).astype(jnp.bfloat16)
    grad_mlp = lax.dot_general(features, grad_pre, (((0,), (0,)), ((), ())), preferred_element_type=jnp.float32) * (1.0 / math.sqrt(point_count))
    grad_conv_out = jnp.zeros((cells_all, C), jnp.float32)
    for corner in range(8):
        grad_conv_out = grad_conv_out + jax.ops.segment_sum(weights[corner][:, None] * upstream, corner_ids[corner], cells_all)
    grad_hidden = (grad_conv_out * sigmoid_slope(hidden)).astype(jnp.bfloat16)
    grad_conv = weight_gradient(padded, grad_hidden, block_shape) * (1.0 / math.sqrt(cells_all))
    grad_padded = jnp.pad(grad_hidden.reshape(GRID_X, GRID_Y, Z, C), ((1, 1), (1, 1), (1, 1), (0, 0)))
    grad_voxels = convolve(grad_padded, conv_weight, block_shape, True)
    from_voxels = (grad_voxels[voxel_ids] / divisor[voxel_ids][:, None]).astype(jnp.bfloat16)
    grad_features = (jnp.dot(grad_pre, mlp_weight.T, preferred_element_type=jnp.float32) + from_voxels.astype(jnp.float32)).astype(jnp.bfloat16)
    return (output, grad_features, grad_conv, grad_mlp)
```

```python
import functools
import math

import jax
import jax.numpy as jnp
from jax import lax
from jax.experimental import pallas as pl
from jax.experimental.pallas import tpu as pltpu
from jax.sharding import Mesh, PartitionSpec as P

C = 128
VX = 4
VY = 8
Z = 16
CELLS = VX * VY * Z
PTS = 512
CAP = 48
GY = 32
SLOTS = GY * CAP
GX = 8
KINDS = 16
HALF = 14
SHARE = HALF * C // GY
SHARE_PAD = 64
BF = jnp.bfloat16
F32 = jnp.float32
VMEM = pl.BlockSpec(memory_space=pltpu.VMEM)
SMEM = pl.BlockSpec(memory_space=pltpu.SMEM)
PARAMS = pltpu.CompilerParams(vmem_limit_bytes=48 * 1024 * 1024)
LEFT = (((0,), (0,)), ((), ()))
RIGHT = (((1,), (1,)), ((), ()))


def sds(shape, dtype):
    return jax.ShapeDtypeStruct(shape, dtype)


def call(kernel, out_shape, args, scratch=(), smem=0):
    return pl.pallas_call(
        kernel,
        out_shape=out_shape,
        in_specs=[SMEM] * smem + [VMEM] * (len(args) - smem),
        out_specs=jax.tree.map(lambda _: VMEM, out_shape),
        scratch_shapes=list(scratch),
        compiler_params=PARAMS,
    )(*args)


def iota(shape, dim):
    return lax.broadcasted_iota(jnp.int32, shape, dim)


def dot(a, b, dims=(((1,), (0,)), ((), ()))):
    return lax.dot_general(a, b, dims, preferred_element_type=F32)


def onehot(mask):
    return jnp.where(mask, 1.0, 0.0).astype(BF)


def sigmoid(v):
    return 1.0 / (1.0 + jnp.exp(-v))


def pack_kernel(feat_ref, cot_ref, slab_ref, base_ref, near_ref, off_ref, sent_ref, pos_ref):
    slab = slab_ref[...]
    named = iota((GY, PTS), 0) == slab
    earlier = onehot(iota((PTS, PTS), 0) < iota((PTS, PTS), 1))
    before = dot(onehot(named), earlier)
    rank = jnp.sum(jnp.where(named, before, 0.0), axis=0, keepdims=True)
    position = slab * CAP + rank.astype(jnp.int32)
    spread = jnp.broadcast_to(position.astype(F32), (C, PTS))
    pos_ref[...] = spread.T.astype(jnp.int32)
    base = base_ref[...]
    near = near_ref[...]
    a = base // (VY * Z)
    b = base // Z % VY
    c = base % Z
    fraction = off_ref[...].astype(F32)
    rows = [a + 2, b, c, a + near // 4 + 2, b + near // 2 % 2, c + near % 2]
    meta = jnp.concatenate(
        [r.astype(F32) for r in rows] + [fraction, jnp.zeros((KINDS - 9, PTS), F32)], axis=0
    ).astype(BF)
    both = jnp.concatenate([feat_ref[...], cot_ref[...]], axis=1)
    group = 8
    for g in range(GY // group):
        span = group * CAP
        chosen = onehot(iota((span, PTS), 0) + g * span == position)
        packed = dot(chosen, both).astype(BF).reshape(group, CAP, 2 * C)
        here = pl.ds(g * group, group)
        sent_ref[here, 0:CAP, :] = packed[:, :, :C]
        sent_ref[here, CAP : 2 * CAP, :] = packed[:, :, C:]
        lanes = dot(meta, chosen, RIGHT)
        for i in range(group):
            piece = lanes[:, i * CAP : (i + 1) * CAP]
            wide = jnp.concatenate([piece, jnp.zeros((KINDS, C - CAP), F32)], axis=1)
            sent_ref[g * group + i, 2 * CAP : 2 * CAP + KINDS, :] = wide.astype(BF)


def mlp_kernel(feat_ref, cot_ref, mlp_ref, act_ref, back_ref, grad_ref):
    feat = feat_ref[...]
    weight = mlp_ref[...]
    pre = dot(feat, weight)
    s = sigmoid(pre)
    act_ref[...] = pre * s
    grad_pre = (cot_ref[...].astype(F32) * (s * (1.0 + pre * (1.0 - s)))).astype(BF)
    back_ref[...] = dot(grad_pre, weight, RIGHT)
    grad_ref[...] = dot(grad_pre, feat, LEFT)


def voxel_kernel(got_ref, vox_ref, div_ref, own_ref, meta_ref):
    meta = jnp.concatenate(
        [got_ref[t, 2 * CAP : 2 * CAP + KINDS, :].astype(F32)[:, :CAP] for t in range(GY)], axis=1
    )
    meta_ref[...] = meta
    own = ((meta[3:4] - 2.0) * (VY * Z) + meta[4:5] * Z + meta[5:6]).astype(jnp.int32)
    own_hot = onehot(iota((CELLS, SLOTS), 0) == own)
    own_ref[...] = own_hot
    rows = got_ref[:, 0:CAP, :].reshape(SLOTS, C)
    both = jnp.concatenate([rows, jnp.ones((SLOTS, C), BF)], axis=1)
    total = dot(own_hot, both)
    divisor = jnp.maximum(total[:, C:], 1.0)
    div_ref[...] = divisor
    vox_ref[...] = (total[:, :C] / divisor).astype(BF).reshape(VX, VY, Z, C)


def spread_kernel(got_ref, meta_ref, matrix_ref, grad_ref):
    meta = meta_ref[...]
    a, b, c = meta[0:1] - 2.0, meta[1:2], meta[2:3]
    fx, fy, fz = meta[6:7], meta[7:8], meta[8:9]

    def side(distance, fraction):
        return jnp.where(distance == 0.0, 1.0 - fraction, jnp.where(distance == 1.0, fraction, 0.0))

    plane = VY * Z
    place = iota((plane, SLOTS), 0)
    wy = side((place // Z).astype(F32) - b, fy)
    wz = side((place % Z).astype(F32) - c, fz)
    for x in range(VX):
        wx = side(x - a, fx)
        matrix_ref[x * plane : (x + 1) * plane, :] = ((wx * wy) * wz).astype(BF)
    cots = got_ref[:, CAP : 2 * CAP, :].reshape(SLOTS, C)
    grad_ref[...] = dot(matrix_ref[...], cots)


def assemble(wide_ref, own_ref, xlo_ref, xhi_ref, ylo_ref, yhi_ref):
    def put(x, y, block):
        nx, ny = block.shape[0], block.shape[1]
        flat = block.reshape(nx * ny * Z, C).astype(F32)
        z = iota(flat.shape, 0) % Z
        blank = jnp.zeros((8, C), F32)
        down = jnp.concatenate([blank, flat], axis=0)[7 : 7 + flat.shape[0]]
        up = jnp.concatenate([flat, blank], axis=0)[1 : 1 + flat.shape[0]]
        down = jnp.where(z == 0, 0.0, down)
        up = jnp.where(z == Z - 1, 0.0, up)
        shape = (nx, ny, Z, C)
        wide_ref[x : x + nx, y : y + ny, :, 0:C] = down.astype(BF).reshape(shape)
        wide_ref[x : x + nx, y : y + ny, :, C : 2 * C] = block
        wide_ref[x : x + nx, y : y + ny, :, 2 * C :] = up.astype(BF).reshape(shape)

    put(1, 1, own_ref[...])
    put(0, 1, xlo_ref[...])
    put(VX + 1, 1, xhi_ref[...])
    put(0, 0, ylo_ref[...])
    put(0, VY + 1, yhi_ref[...])


def window(wide_ref, x, y):
    return wide_ref[x : x + VX, y : y + VY, :, :].reshape(CELLS, 3 * C)


def conv_kernel(core_ref, vox_ref, xlo_ref, xhi_ref, ylo_ref, yhi_ref, weight_ref, matrix_ref, gout_ref,
                mlp_ref, keep_ref, send_ref, sampled_ref, hid_ref, wide_ref, all_ref):
    assemble(wide_ref, vox_ref, xlo_ref, xhi_ref, ylo_ref, yhi_ref)
    hidden = jnp.zeros((CELLS, C), F32)
    for k in range(9):
        taps = weight_ref[3 * k : 3 * k + 3].reshape(3 * C, C)
        hidden = hidden + dot(window(wide_ref, k // 3, k % 3), taps)
    s = sigmoid(hidden)
    conv_out = (hidden * s).astype(BF)
    grad = gout_ref[...] * (s * (1.0 + hidden * (1.0 - s)))
    grad_hidden = grad.astype(BF)
    hid_ref[...] = grad_hidden.reshape(VX, VY, Z, C)
    turned = grad_hidden.astype(F32).T.astype(BF)
    for k in range(9):
        part = dot(turned, window(wide_ref, k // 3, k % 3))
        for j in range(3):
            all_ref[3 * k + j] = part[:, j * C : (j + 1) * C]
    all_ref[27] = mlp_ref[...]
    core = core_ref[0]
    keep_ref[...] = all_ref[pl.ds(core * HALF, HALF)]
    send_ref[...] = all_ref[pl.ds((1 - core) * HALF, HALF)].astype(BF)
    sampled_ref[...] = dot(matrix_ref[...], conv_out, LEFT).astype(BF).reshape(GY, CAP, C)


def join_kernel(keep_ref, got_ref, sampled_ref, out_ref):
    total = (keep_ref[...] + got_ref[...].astype(F32)).reshape(GY, SHARE, C)
    blank = jnp.zeros((GY, SHARE_PAD - SHARE, C), F32)
    out_ref[:, 0:SHARE_PAD, :] = jnp.concatenate([total, blank], axis=1).astype(BF)
    out_ref[:, SHARE_PAD:, :] = sampled_ref[...]


def share_kernel(got_ref, out_ref):
    total = jnp.sum(got_ref[:, 0:SHARE_PAD, :].astype(F32), axis=0)
    out_ref[...] = jnp.broadcast_to(total.astype(BF)[None], out_ref.shape)


def back_kernel(hid_ref, xlo_ref, xhi_ref, ylo_ref, yhi_ref, weight_ref, own_ref, div_ref, from_ref, wide_ref):
    assemble(wide_ref, hid_ref, xlo_ref, xhi_ref, ylo_ref, yhi_ref)
    total = jnp.zeros((CELLS, C), F32)
    for k in range(9):
        taps = jnp.concatenate([weight_ref[3 * k + 2 - j] for j in range(3)], axis=1)
        total = total + dot(window(wide_ref, 2 - k // 3, 2 - k % 3), taps, RIGHT)
    mean = (total / div_ref[...]).astype(BF)
    from_ref[...] = dot(own_ref[...], mean, LEFT).astype(BF).reshape(GY, CAP, C)


def spread_share_kernel(got_ref, from_ref, out_ref):
    total = jnp.sum(got_ref[...].astype(F32), axis=0)
    out_ref[:, 0:SHARE_PAD, :] = jnp.broadcast_to(total.astype(BF)[None], (GY, SHARE_PAD, C))
    out_ref[:, SHARE_PAD:, :] = from_ref[...]


def unpack(pos, rows):
    chosen = jnp.concatenate(
        [onehot(iota((PTS, C), 1) + i * C == pos) for i in range(SLOTS // C)], axis=1
    )
    return dot(chosen, rows)


def points_kernel(second, pos_ref, got_ref, base_ref, out_ref):
    rows = got_ref[:, SHARE_PAD:, :].reshape(SLOTS, C)
    out_ref[...] = (unpack(pos_ref[...], rows) + base_ref[...]).astype(BF)


def weights_kernel(half_ref, conv_ref, mlp_ref):
    for o in range(27):
        conv_ref[o] = half_ref[o].astype(F32).T * (1.0 / math.sqrt(GX * GY * CELLS))
    mlp_ref[...] = half_ref[27].astype(F32).T * (1.0 / math.sqrt(GX * GY * PTS))


def halo(cells):
    up = [(i, i + 1) for i in range(GX - 1)]
    down = [(i + 1, i) for i in range(GX - 1)]
    xlo = lax.ppermute(cells[VX - 1 :], ("y", "c"), up)
    xhi = lax.ppermute(cells[:1], ("y", "c"), down)
    tail = jnp.concatenate([xlo[:, VY - 1 :], cells[:, VY - 1 :], xhi[:, VY - 1 :]], axis=0)
    head = jnp.concatenate([xlo[:, :1], cells[:, :1], xhi[:, :1]], axis=0)
    up = [(i, i + 1) for i in range(GY - 1)]
    down = [(i + 1, i) for i in range(GY - 1)]
    ylo = lax.ppermute(tail, ("x", "z"), up)
    yhi = lax.ppermute(head, ("x", "z"), down)
    return xlo, xhi, ylo, yhi


def exchange(rows):
    return lax.all_to_all(rows, ("x", "z"), split_axis=0, concat_axis=0, tiled=True)


def body(features, point_slab, base_cell, nearest, offsets, conv_weight, mlp_weight, cotangent):
    core = lax.axis_index("c").reshape(1)
    sent, position = call(
        pack_kernel,
        (sds((GY, 2 * CAP + KINDS, C), BF), sds((PTS, C), jnp.int32)),
        (features, cotangent, point_slab.reshape(1, PTS), base_cell.reshape(1, PTS), nearest.reshape(1, PTS), offsets),
    )
    got = exchange(sent)
    act, mlp_back, mlp_grad = call(
        mlp_kernel,
        (sds((PTS, C), F32), sds((PTS, C), F32), sds((C, C), F32)),
        (features, cotangent, mlp_weight),
    )
    voxels, divisor, own_hot, meta = call(
        voxel_kernel,
        (sds((VX, VY, Z, C), BF), sds((CELLS, C), F32), sds((CELLS, SLOTS), BF), sds((KINDS, SLOTS), F32)),
        (got,),
    )
    faces = halo(voxels)
    matrix, grad_out = call(
        spread_kernel, (sds((CELLS, SLOTS), BF), sds((CELLS, C), F32)), (got, meta)
    )
    wide = pltpu.VMEM((VX + 2, VY + 2, Z, 3 * C), BF)
    keep, send, sampled, grad_hidden = call(
        conv_kernel,
        (
            sds((HALF, C, C), F32),
            sds((HALF, C, C), BF),
            sds((GY, CAP, C), BF),
            sds((VX, VY, Z, C), BF),
        ),
        (core, voxels) + faces + (conv_weight, matrix, grad_out, mlp_grad),
        scratch=(wide, pltpu.VMEM((2 * HALF, C, C), F32)),
        smem=1,
    )
    arrived = lax.ppermute(send, "c", [(0, 1), (1, 0)])
    joined = call(join_kernel, sds((GY, SHARE_PAD + CAP, C), BF), (keep, arrived, sampled))
    first = exchange(joined)
    grad_faces = halo(grad_hidden)
    from_voxels = call(
        back_kernel,
        sds((GY, CAP, C), BF),
        (grad_hidden,) + grad_faces + (conv_weight, own_hot, divisor),
        scratch=(wide,),
    )
    shares = call(share_kernel, sds((4, SHARE_PAD, C), BF), (first,))
    shares = lax.all_to_all(shares, "y", split_axis=0, concat_axis=0, tiled=True)
    second_rows = call(spread_share_kernel, sds((GY, SHARE_PAD + CAP, C), BF), (shares, from_voxels))
    second = exchange(second_rows)
    output = call(
        functools.partial(points_kernel, False), sds((PTS, C), BF), (position, first, act)
    )
    half = second[:, :SHARE, :].reshape(1, HALF, C, C)
    whole = lax.all_gather(half, "c", axis=0, tiled=True).reshape(2 * HALF, C, C)
    grad_features = call(
        functools.partial(points_kernel, True), sds((PTS, C), BF), (position, second, mlp_back)
    )
    grad_conv, grad_mlp = call(weights_kernel, (sds((27, C, C), F32), sds((C, C), F32)), (whole,))
    return (output, grad_features, grad_conv, grad_mlp)


def solution(mesh):
    fine = Mesh(mesh.devices.reshape(4, 2, 4, 8), ("y", "c", "x", "z"))
    rows = ("y", "c", "x", "z")
    in_specs = (P(rows, None), P(rows, None), P(rows), P(rows), P(None, rows), P(), P(), P(rows, None))
    out_specs = (P(rows, None), P(rows, None), P(), P())
    return jax.shard_map(body, mesh=fine, in_specs=in_specs, out_specs=out_specs, check_vma=False)
```

```python
import math

import jax
import jax.numpy as jnp
from jax import lax
from jax.experimental import pallas as pl
from jax.experimental.pallas import tpu as pltpu
from jax.sharding import Mesh, PartitionSpec as P

C = 128
VX = 4
VY = 8
Z = 16
CELLS = VX * VY * Z
PTS = 512
CAP = 48
GY = 32
SLOTS = GY * CAP
GX = 8
KINDS = 8
HALF = 14
SHARE = HALF * C // GY
ROWS = CAP + SHARE
BF = jnp.bfloat16
F32 = jnp.float32
VMEM = pl.BlockSpec(memory_space=pltpu.VMEM)
SMEM = pl.BlockSpec(memory_space=pltpu.SMEM)
HBM = pl.BlockSpec(memory_space=pltpu.HBM)
LEFT = (((0,), (0,)), ((), ()))
RIGHT = (((1,), (1,)), ((), ()))


def sds(shape, dtype):
    return jax.ShapeDtypeStruct(shape, dtype)


def call(kernel, out_shape, args, scratch=(), smem=0, hbm=0, mib=12):
    return pl.pallas_call(
        kernel,
        out_shape=out_shape,
        in_specs=[SMEM] * smem + [HBM] * hbm + [VMEM] * (len(args) - smem - hbm),
        out_specs=jax.tree.map(lambda _: VMEM, out_shape),
        scratch_shapes=list(scratch),
        compiler_params=pltpu.CompilerParams(vmem_limit_bytes=mib * 1024 * 1024),
    )(*args)


def iota(shape, dim):
    return lax.broadcasted_iota(jnp.int32, shape, dim)


def dot(a, b, dims=(((1,), (0,)), ((), ()))):
    return lax.dot_general(a, b, dims, preferred_element_type=F32)


def onehot(mask):
    return jnp.where(mask, 1.0, 0.0).astype(BF)


def sigmoid(v):
    return 1.0 / (1.0 + jnp.exp(-v))


def places(slab):
    named = iota((GY, PTS), 0) == slab
    earlier = onehot(iota((PTS, PTS), 0) < iota((PTS, PTS), 1))
    before = dot(onehot(named), earlier)
    rank = jnp.sum(jnp.where(named, before, 0.0), axis=0, keepdims=True)
    return slab * CAP + rank.astype(jnp.int32)


def pack_kernel(feat_hbm, cot_hbm, slab_hbm, base_hbm, near_hbm, off_hbm, sent_ref,
                both_ref, slab_ref, base_ref, near_ref, off_ref, sems):
    moves = [
        pltpu.make_async_copy(slab_hbm, slab_ref, sems.at[0]),
        pltpu.make_async_copy(base_hbm, base_ref, sems.at[1]),
        pltpu.make_async_copy(near_hbm, near_ref, sems.at[2]),
        pltpu.make_async_copy(off_hbm, off_ref, sems.at[3]),
        pltpu.make_async_copy(feat_hbm, both_ref.at[:, 0:C], sems.at[4]),
        pltpu.make_async_copy(cot_hbm, both_ref.at[:, C : 2 * C], sems.at[5]),
    ]
    for move in moves:
        move.start()
    for move in moves:
        move.wait()
    position = places(slab_ref[...])
    base = base_ref[...]
    near = near_ref[...]
    a = base // (VY * Z)
    b = base // Z % VY
    c = base % Z
    fraction = off_ref[...].astype(F32)
    rows = [a + 2, b, c, near]
    meta = jnp.concatenate(
        [r.astype(F32) for r in rows] + [fraction, jnp.zeros((KINDS - 7, PTS), F32)], axis=0
    ).astype(BF)
    both = both_ref[...]
    group = 8
    for g in range(GY // group):
        span = group * CAP
        chosen = onehot(iota((span, PTS), 0) + g * span == position)
        packed = dot(chosen, both).astype(BF).reshape(group, CAP, 2 * C)
        here = pl.ds(g * group, group)
        sent_ref[here, 0:CAP, :] = packed[:, :, :C]
        sent_ref[here, CAP : 2 * CAP, :] = packed[:, :, C:]
        lanes = dot(meta, chosen, RIGHT)
        for i in range(group):
            piece = lanes[:, i * CAP : (i + 1) * CAP]
            wide = jnp.concatenate([piece, jnp.zeros((KINDS, C - CAP), F32)], axis=1)
            sent_ref[g * group + i, 2 * CAP : 2 * CAP + KINDS, :] = wide.astype(BF)


def slope(v, s):
    return s * (1.0 + v * (1.0 - s))


def mlp_kernel(feat_ref, cot_ref, mlp_ref, grad_ref):
    feat = feat_ref[...]
    pre = dot(feat, mlp_ref[...])
    grad_pre = (cot_ref[...].astype(F32) * slope(pre, sigmoid(pre))).astype(BF)
    grad_ref[...] = dot(grad_pre, feat, LEFT)


def arrived_meta(got_ref):
    return jnp.concatenate(
        [got_ref[t, 2 * CAP : 2 * CAP + KINDS, :].astype(F32)[:, :CAP] for t in range(GY)], axis=1
    )


def own_matrix(meta):
    near = meta[3:4].astype(jnp.int32)
    base = (meta[0:1] - 2.0) * (VY * Z) + meta[1:2] * Z + meta[2:3]
    own = base.astype(jnp.int32) + near // 4 * (VY * Z) + near // 2 % 2 * Z + near % 2
    return onehot(iota((CELLS, SLOTS), 0) == own)


def voxel_kernel(got_ref, vox_ref, lo_ref, hi_ref, div_ref, meta_ref):
    meta = arrived_meta(got_ref)
    meta_ref[...] = meta
    own_hot = own_matrix(meta)
    rows = got_ref[:, 0:CAP, :].reshape(SLOTS, C)
    both = jnp.concatenate([rows, jnp.ones((SLOTS, C), BF)], axis=1)
    total = dot(own_hot, both)
    divisor = jnp.maximum(total[:, C:], 1.0)
    div_ref[...] = divisor
    voxels = (total[:, :C] / divisor).astype(BF).reshape(VX, VY, Z, C)
    vox_ref[...] = voxels
    lo_ref[...] = voxels[:1]
    hi_ref[...] = voxels[VX - 1 :]


def spread_kernel(got_ref, meta_ref, matrix_ref, grad_ref):
    meta = meta_ref[...]
    a, b, c = meta[0:1] - 2.0, meta[1:2], meta[2:3]
    fx, fy, fz = meta[4:5], meta[5:6], meta[6:7]

    def side(distance, fraction):
        return jnp.where(distance == 0.0, 1.0 - fraction, jnp.where(distance == 1.0, fraction, 0.0))

    plane = VY * Z
    place = iota((plane, SLOTS), 0)
    wy = side((place // Z).astype(F32) - b, fy)
    wz = side((place % Z).astype(F32) - c, fz)
    for x in range(VX):
        wx = side(x - a, fx)
        matrix_ref[x * plane : (x + 1) * plane, :] = ((wx * wy) * wz).astype(BF)
    cots = got_ref[:, CAP : 2 * CAP, :].reshape(SLOTS, C)
    grad_ref[...] = dot(matrix_ref[...], cots)


def edge_kernel(xlo_ref, own_ref, xhi_ref, tail_ref, head_ref):
    for ref, y in ((tail_ref, VY - 1), (head_ref, 0)):
        ref[0] = xlo_ref[0, y : y + 1]
        ref[1 : VX + 1] = own_ref[:, y : y + 1]
        ref[VX + 1] = xhi_ref[0, y : y + 1]


def assemble(wide_ref, own_ref, xlo_ref, xhi_ref, ylo_ref, yhi_ref):
    def put(x, y, block):
        nx, ny = block.shape[0], block.shape[1]
        flat = block.reshape(nx * ny * Z, C).astype(F32)
        z = iota(flat.shape, 0) % Z
        blank = jnp.zeros((8, C), F32)
        down = jnp.concatenate([blank, flat], axis=0)[7 : 7 + flat.shape[0]]
        up = jnp.concatenate([flat, blank], axis=0)[1 : 1 + flat.shape[0]]
        down = jnp.where(z == 0, 0.0, down)
        up = jnp.where(z == Z - 1, 0.0, up)
        shape = (nx, ny, Z, C)
        wide_ref[x : x + nx, y : y + ny, :, 0:C] = down.astype(BF).reshape(shape)
        wide_ref[x : x + nx, y : y + ny, :, C : 2 * C] = block
        wide_ref[x : x + nx, y : y + ny, :, 2 * C :] = up.astype(BF).reshape(shape)

    put(1, 1, own_ref[...])
    put(0, 1, xlo_ref[...])
    put(VX + 1, 1, xhi_ref[...])
    put(0, 0, ylo_ref[...])
    put(0, VY + 1, yhi_ref[...])


def window(wide_ref, x, y):
    return wide_ref[x : x + VX, y : y + VY, :, :].reshape(CELLS, 3 * C)


def conv_kernel(core_ref, vox_ref, xlo_ref, xhi_ref, ylo_ref, yhi_ref, weight_ref, gout_ref,
                mlp_ref, keep_ref, send_ref, act_ref, hid_ref, lo_ref, hi_ref, wide_ref, all_ref):
    assemble(wide_ref, vox_ref, xlo_ref, xhi_ref, ylo_ref, yhi_ref)
    hidden = jnp.zeros((CELLS, C), F32)
    for k in range(9):
        taps = weight_ref[3 * k : 3 * k + 3].reshape(3 * C, C)
        hidden = hidden + dot(window(wide_ref, k // 3, k % 3), taps)
    s = sigmoid(hidden)
    act_ref[...] = (hidden * s).astype(BF)
    grad_hidden = (gout_ref[...] * slope(hidden, s)).astype(BF)
    shaped = grad_hidden.reshape(VX, VY, Z, C)
    hid_ref[...] = shaped
    lo_ref[...] = shaped[:1]
    hi_ref[...] = shaped[VX - 1 :]
    turned = grad_hidden.astype(F32).T.astype(BF)
    for k in range(9):
        part = dot(turned, window(wide_ref, k // 3, k % 3))
        for j in range(3):
            all_ref[3 * k + j] = part[:, j * C : (j + 1) * C]
    all_ref[27] = mlp_ref[...]
    core = core_ref[0]
    keep_ref[...] = all_ref[pl.ds(core * HALF, HALF)]
    send_ref[...] = all_ref[pl.ds((1 - core) * HALF, HALF)].astype(BF)


def sample_kernel(matrix_ref, act_ref, out_ref):
    out_ref[...] = dot(matrix_ref[...], act_ref[...], LEFT).astype(BF).reshape(GY, CAP, C)


def join_kernel(keep_ref, got_ref, filled_ref, out_ref):
    total = keep_ref[...] + got_ref[...].astype(F32)
    out_ref[:, CAP:, :] = total.reshape(GY, SHARE, C).astype(BF)
    out_ref[:, 0:CAP, :] = filled_ref[...]


def share_kernel(got_ref, out_ref):
    total = jnp.sum(got_ref[:, CAP:, :].astype(F32), axis=0)
    out_ref[...] = jnp.broadcast_to(total.astype(BF)[None], out_ref.shape)


def back_kernel(hid_ref, xlo_ref, xhi_ref, ylo_ref, yhi_ref, weight_ref, meta_ref, div_ref, out_ref, wide_ref):
    assemble(wide_ref, hid_ref, xlo_ref, xhi_ref, ylo_ref, yhi_ref)
    total = jnp.zeros((CELLS, C), F32)
    for k in range(9):
        taps = jnp.concatenate([weight_ref[3 * k + 2 - j] for j in range(3)], axis=1)
        total = total + dot(window(wide_ref, 2 - k // 3, 2 - k % 3), taps, RIGHT)
    mean = (total / div_ref[...]).astype(BF)
    out_ref[...] = dot(own_matrix(meta_ref[...]), mean, LEFT).astype(BF).reshape(GY, CAP, C)


def spread_share_kernel(got_ref, filled_ref, out_ref):
    total = jnp.sum(got_ref[...].astype(F32), axis=0)
    out_ref[:, CAP:, :] = jnp.broadcast_to(total.astype(BF)[None], (GY, SHARE, C))
    out_ref[:, 0:CAP, :] = filled_ref[...]


def unpack(pos, got_ref):
    rows = got_ref[:, 0:CAP, :].reshape(SLOTS, C)
    chosen = jnp.concatenate(
        [onehot(iota((PTS, C), 1) + i * C == pos) for i in range(SLOTS // C)], axis=1
    )
    return dot(chosen, rows)


def forward_kernel(got_ref, slab_ref, feat_ref, cot_ref, mlp_ref, out_ref, pos_ref, back_ref):
    spread = jnp.broadcast_to(places(slab_ref[...]).astype(F32), (C, PTS))
    pos = spread.T.astype(jnp.int32)
    pos_ref[...] = pos
    weight = mlp_ref[...]
    pre = dot(feat_ref[...], weight)
    s = sigmoid(pre)
    grad_pre = (cot_ref[...].astype(F32) * slope(pre, s)).astype(BF)
    back_ref[...] = dot(grad_pre, weight, RIGHT)
    sampled = unpack(pos, got_ref).astype(BF).astype(F32)
    out_ref[...] = (sampled + pre * s).astype(BF)


def take_kernel(got_ref, out_ref):
    out_ref[...] = got_ref[:, CAP:, :].astype(F32).reshape(HALF, C, C).astype(BF)


def backward_kernel(got_ref, pos_ref, back_ref, out_ref):
    out_ref[...] = (unpack(pos_ref[...], got_ref) + back_ref[...]).astype(BF)


def weights_kernel(core_ref, mine_ref, other_ref, conv_ref, mlp_ref):
    def fill(first_ref, second_ref):
        for o in range(27):
            half = first_ref[o] if o < HALF else second_ref[o - HALF]
            conv_ref[o] = half.astype(F32).T * (1.0 / math.sqrt(GX * GY * CELLS))
        mlp_ref[...] = second_ref[HALF - 1].astype(F32).T * (1.0 / math.sqrt(GX * GY * PTS))

    @pl.when(core_ref[0] == 0)
    def _():
        fill(mine_ref, other_ref)

    @pl.when(core_ref[0] == 1)
    def _():
        fill(other_ref, mine_ref)


FACE = sds((1, VY, Z, C), BF)
EDGE = sds((VX + 2, 1, Z, C), BF)


def halo(cells, lo, hi):
    up = [(i, i + 1) for i in range(GX - 1)]
    down = [(i + 1, i) for i in range(GX - 1)]
    xlo = lax.ppermute(hi, ("y", "c"), up)
    xhi = lax.ppermute(lo, ("y", "c"), down)
    tail, head = call(edge_kernel, (EDGE, EDGE), (xlo, cells, xhi), mib=2)
    up = [(i, i + 1) for i in range(GY - 1)]
    down = [(i + 1, i) for i in range(GY - 1)]
    ylo = lax.ppermute(tail, ("x", "z"), up)
    yhi = lax.ppermute(head, ("x", "z"), down)
    return xlo, xhi, ylo, yhi


def exchange(rows):
    return lax.all_to_all(rows, ("x", "z"), split_axis=0, concat_axis=0, tiled=True)


def swap(half):
    return lax.ppermute(half, "c", [(0, 1), (1, 0)])


def body(features, point_slab, base_cell, nearest, offsets, conv_weight, mlp_weight, cotangent):
    core = lax.axis_index("c").reshape(1)
    point_slab, core = lax.optimization_barrier((point_slab, core))
    slab = point_slab.reshape(1, PTS)
    line = pltpu.VMEM((1, PTS), jnp.int32)
    sent = call(
        pack_kernel,
        sds((GY, 2 * CAP + KINDS, C), BF),
        (features, cotangent, slab, base_cell.reshape(1, PTS), nearest.reshape(1, PTS), offsets),
        scratch=(
            pltpu.VMEM((PTS, 2 * C), BF),
            line,
            line,
            line,
            pltpu.VMEM((3, PTS), BF),
            pltpu.SemaphoreType.DMA((6,)),
        ),
        hbm=6,
        mib=60,
    )
    got = exchange(sent)
    mlp_grad = call(mlp_kernel, sds((C, C), F32), (features, cotangent, mlp_weight))
    got, mlp_grad = lax.optimization_barrier((got, mlp_grad))
    cells = sds((VX, VY, Z, C), BF)
    voxels, lo, hi, divisor, meta = call(
        voxel_kernel,
        (cells, FACE, FACE, sds((CELLS, C), F32), sds((KINDS, SLOTS), F32)),
        (got,),
    )
    faces = halo(voxels, lo, hi)
    matrix, grad_out = call(
        spread_kernel, (sds((CELLS, SLOTS), BF), sds((CELLS, C), F32)), (got, meta)
    )
    wide = pltpu.VMEM((VX + 2, VY + 2, Z, 3 * C), BF)
    block = sds((GY, ROWS, C), BF)
    rows = sds((GY, CAP, C), BF)
    keep, send, act, grad_hidden, lo, hi = call(
        conv_kernel,
        (sds((HALF, C, C), F32), sds((HALF, C, C), BF), sds((CELLS, C), BF), cells, FACE, FACE),
        (core, voxels) + faces + (conv_weight, grad_out, mlp_grad),
        scratch=(wide, pltpu.VMEM((2 * HALF, C, C), F32)),
        smem=1,
    )
    arrived = swap(send)
    filled = call(sample_kernel, rows, (matrix, act))
    joined = call(join_kernel, block, (keep, arrived, filled))
    first = exchange(joined)
    grad_faces = halo(grad_hidden, lo, hi)
    filled = call(
        back_kernel,
        rows,
        (grad_hidden,) + grad_faces + (conv_weight, meta, divisor),
        scratch=(wide,),
    )
    first, filled = lax.optimization_barrier((first, filled))
    shares = call(share_kernel, sds((4, SHARE, C), BF), (first,), mib=4)
    shares = lax.all_to_all(shares, "y", split_axis=0, concat_axis=0, tiled=True)
    joined = call(spread_share_kernel, block, (shares, filled))
    second = exchange(joined)
    output, position, back = call(
        forward_kernel,
        (sds((PTS, C), BF), sds((PTS, C), jnp.int32), sds((PTS, C), F32)),
        (first, slab, features, cotangent, mlp_weight),
    )
    second, back = lax.optimization_barrier((second, back))
    mine = call(take_kernel, sds((HALF, C, C), BF), (second,), mib=4)
    other = swap(mine)
    grad_features = call(backward_kernel, sds((PTS, C), BF), (second, position, back))
    grad_conv, grad_mlp = call(
        weights_kernel, (sds((27, C, C), F32), sds((C, C), F32)), (core, mine, other), smem=1
    )
    return (output, grad_features, grad_conv, grad_mlp)


def solution(mesh):
    fine = Mesh(mesh.devices.reshape(4, 2, 4, 8), ("y", "c", "x", "z"))
    rows = ("y", "c", "x", "z")
    in_specs = (P(rows, None), P(rows, None), P(rows), P(rows), P(None, rows), P(), P(), P(rows, None))
    out_specs = (P(rows, None), P(rows, None), P(), P())
    return jax.shard_map(body, mesh=fine, in_specs=in_specs, out_specs=out_specs, check_vma=False)
```

```python
import math

import jax
import jax.numpy as jnp
from jax import lax
from jax.experimental import pallas as pl
from jax.experimental.pallas import tpu as pltpu
from jax.sharding import Mesh, PartitionSpec as P

C = 128
VX = 4
VY = 8
Z = 16
CELLS = VX * VY * Z
PTS = 512
CAP = 48
GY = 32
SLOTS = GY * CAP
GX = 8
KINDS = 8
HALF = 14
SHARE = HALF * C // GY
ROWS = CAP + SHARE
BF = jnp.bfloat16
F32 = jnp.float32
VMEM = pl.BlockSpec(memory_space=pltpu.VMEM)
SMEM = pl.BlockSpec(memory_space=pltpu.SMEM)
HBM = pl.BlockSpec(memory_space=pltpu.HBM)
LEFT = (((0,), (0,)), ((), ()))
RIGHT = (((1,), (1,)), ((), ()))


def sds(shape, dtype):
    return jax.ShapeDtypeStruct(shape, dtype)


def call(kernel, out_shape, args, scratch=(), smem=0, hbm=0, mib=12, out=VMEM):
    return pl.pallas_call(
        kernel,
        out_shape=out_shape,
        in_specs=[SMEM] * smem + [HBM] * hbm + [VMEM] * (len(args) - smem - hbm),
        out_specs=jax.tree.map(lambda _: out, out_shape),
        scratch_shapes=list(scratch),
        compiler_params=pltpu.CompilerParams(vmem_limit_bytes=mib * 1024 * 1024),
    )(*args)


def iota(shape, dim):
    return lax.broadcasted_iota(jnp.int32, shape, dim)


def dot(a, b, dims=(((1,), (0,)), ((), ()))):
    return lax.dot_general(a, b, dims, preferred_element_type=F32)


def onehot(mask):
    return jnp.where(mask, 1.0, 0.0).astype(BF)


def sigmoid(v):
    return 1.0 / (1.0 + jnp.exp(-v))


def places(slab):
    named = iota((GY, PTS), 0) == slab
    earlier = onehot(iota((PTS, PTS), 0) < iota((PTS, PTS), 1))
    before = dot(onehot(named), earlier)
    rank = jnp.sum(jnp.where(named, before, 0.0), axis=0, keepdims=True)
    return slab * CAP + rank.astype(jnp.int32)


def pack_kernel(feat_hbm, cot_hbm, slab_hbm, base_hbm, near_hbm, off_hbm, sent_hbm,
                both_ref, slab_ref, base_ref, near_ref, off_ref, sent_ref, sems, out_sems):
    moves = [
        pltpu.make_async_copy(slab_hbm, slab_ref, sems.at[0]),
        pltpu.make_async_copy(base_hbm, base_ref, sems.at[1]),
        pltpu.make_async_copy(near_hbm, near_ref, sems.at[2]),
        pltpu.make_async_copy(off_hbm, off_ref, sems.at[3]),
        pltpu.make_async_copy(feat_hbm, both_ref.at[:, 0:C], sems.at[4]),
        pltpu.make_async_copy(cot_hbm, both_ref.at[:, C : 2 * C], sems.at[5]),
    ]
    for move in moves:
        move.start()
    for move in moves[:4]:
        move.wait()
    position = places(slab_ref[...])
    base = base_ref[...]
    near = near_ref[...]
    a = base // (VY * Z)
    b = base // Z % VY
    c = base % Z
    fraction = off_ref[...].astype(F32)
    rows = [a + 2, b, c, near]
    meta = jnp.concatenate(
        [r.astype(F32) for r in rows] + [fraction, jnp.zeros((KINDS - 7, PTS), F32)], axis=0
    ).astype(BF)
    moves[4].wait()
    moves[5].wait()
    both = both_ref[...]
    group = 8
    sends = []
    for g in range(GY // group):
        span = group * CAP
        chosen = onehot(iota((span, PTS), 0) + g * span == position)
        packed = dot(chosen, both).astype(BF).reshape(group, CAP, 2 * C)
        here = pl.ds(g * group, group)
        sent_ref[here, 0:CAP, :] = packed[:, :, :C]
        sent_ref[here, CAP : 2 * CAP, :] = packed[:, :, C:]
        lanes = dot(meta, chosen, RIGHT)
        for i in range(group):
            piece = lanes[:, i * CAP : (i + 1) * CAP]
            wide = jnp.concatenate([piece, jnp.zeros((KINDS, C - CAP), F32)], axis=1)
            sent_ref[g * group + i, 2 * CAP : 2 * CAP + KINDS, :] = wide.astype(BF)
        sends.append(pltpu.make_async_copy(sent_ref.at[here], sent_hbm.at[here], out_sems.at[g]))
        sends[g].start()
    for send in sends:
        send.wait()


def slope(v, s):
    return s * (1.0 + v * (1.0 - s))


def mlp_kernel(feat_ref, cot_ref, mlp_ref, grad_ref):
    feat = feat_ref[...]
    pre = dot(feat, mlp_ref[...])
    grad_pre = (cot_ref[...].astype(F32) * slope(pre, sigmoid(pre))).astype(BF)
    grad_ref[...] = dot(grad_pre, feat, LEFT)


def arrived_meta(got_ref):
    return jnp.concatenate(
        [got_ref[t, 2 * CAP : 2 * CAP + KINDS, :].astype(F32)[:, :CAP] for t in range(GY)], axis=1
    )


def own_matrix(meta):
    near = meta[3:4].astype(jnp.int32)
    base = (meta[0:1] - 2.0) * (VY * Z) + meta[1:2] * Z + meta[2:3]
    own = base.astype(jnp.int32) + near // 4 * (VY * Z) + near // 2 % 2 * Z + near % 2
    return onehot(iota((CELLS, SLOTS), 0) == own)


def voxel_kernel(core_ref, got_ref, vox_ref, near_ref, far_ref, div_ref, meta_ref):
    meta = arrived_meta(got_ref)
    meta_ref[...] = meta
    own_hot = own_matrix(meta)
    rows = got_ref[:, 0:CAP, :].reshape(SLOTS, C)
    both = jnp.concatenate([rows, jnp.ones((SLOTS, C), BF)], axis=1)
    total = dot(own_hot, both)
    divisor = jnp.maximum(total[:, C:], 1.0)
    div_ref[...] = divisor
    vox_ref[...] = (total[:, :C] / divisor).astype(BF).reshape(VX, VY, Z, C)
    core = core_ref[0]
    near_ref[...] = vox_ref[pl.ds((VX - 1) * (1 - core), 1)]
    far_ref[...] = vox_ref[pl.ds((VX - 1) * core, 1)]


def spread_kernel(got_ref, meta_ref, matrix_ref, grad_ref):
    meta = meta_ref[...]
    a, b, c = meta[0:1] - 2.0, meta[1:2], meta[2:3]
    fx, fy, fz = meta[4:5], meta[5:6], meta[6:7]

    def side(distance, fraction):
        return jnp.where(distance == 0.0, 1.0 - fraction, jnp.where(distance == 1.0, fraction, 0.0))

    plane = VY * Z
    place = iota((plane, SLOTS), 0)
    wy = side((place // Z).astype(F32) - b, fy)
    wz = side((place % Z).astype(F32) - c, fz)
    for x in range(VX):
        wx = side(x - a, fx)
        matrix_ref[x * plane : (x + 1) * plane, :] = ((wx * wy) * wz).astype(BF)
    cots = got_ref[:, CAP : 2 * CAP, :].reshape(SLOTS, C)
    grad_ref[...] = dot(matrix_ref[...], cots)


def edge_kernel(core_ref, near_ref, own_ref, far_ref, tail_ref, head_ref):
    core = core_ref[0]
    for ref, y in ((tail_ref, VY - 1), (head_ref, 0)):
        ref[pl.ds((VX + 1) * (1 - core), 1)] = near_ref[:, y : y + 1]
        ref[1 : VX + 1] = own_ref[:, y : y + 1]
        ref[pl.ds((VX + 1) * core, 1)] = far_ref[:, y : y + 1]


def assemble(core, wide_ref, own_ref, near_ref, far_ref, ylo_ref, yhi_ref):
    def put(x, y, block):
        nx, ny = block.shape[0], block.shape[1]
        flat = block.reshape(nx * ny * Z, C).astype(F32)
        z = iota(flat.shape, 0) % Z
        blank = jnp.zeros((8, C), F32)
        down = jnp.concatenate([blank, flat], axis=0)[7 : 7 + flat.shape[0]]
        up = jnp.concatenate([flat, blank], axis=0)[1 : 1 + flat.shape[0]]
        down = jnp.where(z == 0, 0.0, down)
        up = jnp.where(z == Z - 1, 0.0, up)
        shape = (nx, ny, Z, C)
        planes = pl.ds(x, nx)
        wide_ref[planes, y : y + ny, :, 0:C] = down.astype(BF).reshape(shape)
        wide_ref[planes, y : y + ny, :, C : 2 * C] = block
        wide_ref[planes, y : y + ny, :, 2 * C :] = up.astype(BF).reshape(shape)

    put(1, 1, own_ref[...])
    put((VX + 1) * (1 - core), 1, near_ref[...])
    put((VX + 1) * core, 1, far_ref[...])
    put(0, 0, ylo_ref[...])
    put(0, VY + 1, yhi_ref[...])


def window(wide_ref, x, y):
    return wide_ref[x : x + VX, y : y + VY, :, :].reshape(CELLS, 3 * C)


def conv_kernel(core_ref, vox_ref, near_ref, far_ref, ylo_ref, yhi_ref, weight_ref, gout_ref,
                mlp_ref, keep_ref, send_ref, act_ref, hid_ref, in_ref, out_ref, wide_ref, all_ref):
    core = core_ref[0]
    assemble(core, wide_ref, vox_ref, near_ref, far_ref, ylo_ref, yhi_ref)
    hidden = jnp.zeros((CELLS, C), F32)
    for k in range(9):
        taps = weight_ref[3 * k : 3 * k + 3].reshape(3 * C, C)
        hidden = hidden + dot(window(wide_ref, k // 3, k % 3), taps)
    s = sigmoid(hidden)
    act_ref[...] = (hidden * s).astype(BF)
    grad_hidden = (gout_ref[...] * slope(hidden, s)).astype(BF)
    hid_ref[...] = grad_hidden.reshape(VX, VY, Z, C)
    in_ref[...] = hid_ref[pl.ds((VX - 1) * (1 - core), 1)]
    out_ref[...] = hid_ref[pl.ds((VX - 1) * core, 1)]
    turned = grad_hidden.astype(F32).T.astype(BF)
    for k in range(9):
        part = dot(turned, window(wide_ref, k // 3, k % 3))
        for j in range(3):
            all_ref[3 * k + j] = part[:, j * C : (j + 1) * C]
    all_ref[27] = mlp_ref[...]
    keep_ref[...] = all_ref[pl.ds(core * HALF, HALF)]
    send_ref[...] = all_ref[pl.ds((1 - core) * HALF, HALF)].astype(BF)


def sample_kernel(matrix_ref, act_ref, out_ref):
    out_ref[...] = dot(matrix_ref[...], act_ref[...], LEFT).astype(BF).reshape(GY, CAP, C)


def join_kernel(keep_ref, got_ref, filled_ref, out_ref):
    total = keep_ref[...] + got_ref[...].astype(F32)
    out_ref[:, CAP:, :] = total.reshape(GY, SHARE, C).astype(BF)
    out_ref[:, 0:CAP, :] = filled_ref[...]


def share_kernel(got_ref, out_ref):
    total = jnp.sum(got_ref[:, CAP:, :].astype(F32), axis=0)
    out_ref[...] = jnp.broadcast_to(total.astype(BF)[None], out_ref.shape)


def back_kernel(core_ref, hid_ref, near_ref, far_ref, ylo_ref, yhi_ref, weight_ref, meta_ref, div_ref, out_ref, wide_ref):
    assemble(core_ref[0], wide_ref, hid_ref, near_ref, far_ref, ylo_ref, yhi_ref)
    total = jnp.zeros((CELLS, C), F32)
    for k in range(9):
        taps = jnp.concatenate([weight_ref[3 * k + 2 - j] for j in range(3)], axis=1)
        total = total + dot(window(wide_ref, 2 - k // 3, 2 - k % 3), taps, RIGHT)
    mean = (total / div_ref[...]).astype(BF)
    out_ref[...] = dot(own_matrix(meta_ref[...]), mean, LEFT).astype(BF).reshape(GY, CAP, C)


def spread_share_kernel(got_ref, filled_ref, out_ref):
    total = jnp.sum(got_ref[...].astype(F32), axis=0)
    out_ref[:, CAP:, :] = jnp.broadcast_to(total.astype(BF)[None], (GY, SHARE, C))
    out_ref[:, 0:CAP, :] = filled_ref[...]


def unpack(pos, got_ref):
    rows = got_ref[:, 0:CAP, :].reshape(SLOTS, C)
    chosen = jnp.concatenate(
        [onehot(iota((PTS, C), 1) + i * C == pos) for i in range(SLOTS // C)], axis=1
    )
    return dot(chosen, rows)


def forward_kernel(got_ref, slab_ref, feat_ref, cot_ref, mlp_ref, out_ref, pos_ref, back_ref):
    spread = jnp.broadcast_to(places(slab_ref[...]).astype(F32), (C, PTS))
    pos = spread.T.astype(jnp.int32)
    pos_ref[...] = pos
    weight = mlp_ref[...]
    pre = dot(feat_ref[...], weight)
    s = sigmoid(pre)
    grad_pre = (cot_ref[...].astype(F32) * slope(pre, s)).astype(BF)
    back_ref[...] = dot(grad_pre, weight, RIGHT)
    sampled = unpack(pos, got_ref).astype(BF).astype(F32)
    out_ref[...] = (sampled + pre * s).astype(BF)


def take_kernel(got_ref, out_ref):
    out_ref[...] = got_ref[:, CAP:, :].astype(F32).reshape(HALF, C, C).astype(BF)


def backward_kernel(got_ref, pos_ref, back_ref, out_ref):
    out_ref[...] = (unpack(pos_ref[...], got_ref) + back_ref[...]).astype(BF)


def weights_kernel(core_ref, mine_ref, other_ref, conv_ref, mlp_ref):
    def fill(first_ref, second_ref):
        for o in range(27):
            half = first_ref[o] if o < HALF else second_ref[o - HALF]
            conv_ref[o] = half.astype(F32).T * (1.0 / math.sqrt(GX * GY * CELLS))
        mlp_ref[...] = second_ref[HALF - 1].astype(F32).T * (1.0 / math.sqrt(GX * GY * PTS))

    @pl.when(core_ref[0] == 0)
    def _():
        fill(mine_ref, other_ref)

    @pl.when(core_ref[0] == 1)
    def _():
        fill(other_ref, mine_ref)


FACE = sds((1, VY, Z, C), BF)
EDGE = sds((VX + 2, 1, Z, C), BF)


def chips(face):
    pairs = [(i, i + 1) for i in range(1, GX - 1, 2)]
    return lax.ppermute(face, ("y", "c"), pairs + [(j, i) for i, j in pairs])


def edges(core, near, cells, far):
    tail, head = call(edge_kernel, (EDGE, EDGE), (core, near, cells, far), smem=1, mib=2)
    up = [(i, i + 1) for i in range(GY - 1)]
    down = [(i + 1, i) for i in range(GY - 1)]
    return lax.ppermute(tail, ("x", "z"), up), lax.ppermute(head, ("x", "z"), down)


def exchange(rows):
    return lax.all_to_all(rows, ("x", "z"), split_axis=0, concat_axis=0, tiled=True)


def swap(half):
    return lax.ppermute(half, "c", [(0, 1), (1, 0)])


def body(features, point_slab, base_cell, nearest, offsets, conv_weight, mlp_weight, cotangent):
    core = lax.axis_index("c").reshape(1)
    point_slab, core = lax.optimization_barrier((point_slab, core))
    slab = point_slab.reshape(1, PTS)
    line = pltpu.VMEM((1, PTS), jnp.int32)
    sent = call(
        pack_kernel,
        sds((GY, 2 * CAP + KINDS, C), BF),
        (features, cotangent, slab, base_cell.reshape(1, PTS), nearest.reshape(1, PTS), offsets),
        scratch=(
            pltpu.VMEM((PTS, 2 * C), BF),
            line,
            line,
            line,
            pltpu.VMEM((3, PTS), BF),
            pltpu.VMEM((GY, 2 * CAP + KINDS, C), BF),
            pltpu.SemaphoreType.DMA((6,)),
            pltpu.SemaphoreType.DMA((4,)),
        ),
        hbm=6,
        mib=60,
        out=HBM,
    )
    got = exchange(sent)
    mlp_grad = call(mlp_kernel, sds((C, C), F32), (features, cotangent, mlp_weight))
    got, mlp_grad = lax.optimization_barrier((got, mlp_grad))
    cells = sds((VX, VY, Z, C), BF)
    voxels, near, far, divisor, meta = call(
        voxel_kernel,
        (cells, FACE, FACE, sds((CELLS, C), F32), sds((KINDS, SLOTS), F32)),
        (core, got),
        smem=1,
    )
    near, far = swap(near), chips(far)
    faces = (near, far) + edges(core, near, voxels, far)
    matrix, grad_out = call(
        spread_kernel, (sds((CELLS, SLOTS), BF), sds((CELLS, C), F32)), (got, meta)
    )
    wide = pltpu.VMEM((VX + 2, VY + 2, Z, 3 * C), BF)
    block = sds((GY, ROWS, C), BF)
    rows = sds((GY, CAP, C), BF)
    keep, send, act, grad_hidden, near, far = call(
        conv_kernel,
        (sds((HALF, C, C), F32), sds((HALF, C, C), BF), sds((CELLS, C), BF), cells, FACE, FACE),
        (core, voxels) + faces + (conv_weight, grad_out, mlp_grad),
        scratch=(wide, pltpu.VMEM((2 * HALF, C, C), F32)),
        smem=1,
    )
    arrived = swap(send)
    filled = call(sample_kernel, rows, (matrix, act))
    joined = call(join_kernel, block, (keep, arrived, filled))
    first = exchange(joined)
    near, far = swap(near), chips(far)
    grad_faces = (near, far) + edges(core, near, grad_hidden, far)
    first, grad_faces = lax.optimization_barrier((first, grad_faces))
    filled = call(
        back_kernel,
        rows,
        (core, grad_hidden) + grad_faces + (conv_weight, meta, divisor),
        scratch=(wide,),
        smem=1,
    )
    shares = call(share_kernel, sds((4, SHARE, C), BF), (first,), mib=4)
    shares = lax.all_to_all(shares, "y", split_axis=0, concat_axis=0, tiled=True)
    joined = call(spread_share_kernel, block, (shares, filled))
    second = exchange(joined)
    output, position, back = call(
        forward_kernel,
        (sds((PTS, C), BF), sds((PTS, C), jnp.int32), sds((PTS, C), F32)),
        (first, slab, features, cotangent, mlp_weight),
    )
    second, back = lax.optimization_barrier((second, back))
    mine = call(take_kernel, sds((HALF, C, C), BF), (second,), mib=4)
    other = swap(mine)
    grad_features = call(backward_kernel, sds((PTS, C), BF), (second, position, back))
    grad_conv, grad_mlp = call(
        weights_kernel, (sds((27, C, C), F32), sds((C, C), F32)), (core, mine, other), smem=1
    )
    return (output, grad_features, grad_conv, grad_mlp)


def solution(mesh):
    fine = Mesh(mesh.devices.reshape(4, 2, 4, 8), ("y", "c", "x", "z"))
    rows = ("y", "c", "x", "z")
    in_specs = (P(rows, None), P(rows, None), P(rows), P(rows), P(None, rows), P(), P(), P(rows, None))
    out_specs = (P(rows, None), P(rows, None), P(), P())
    return jax.shard_map(body, mesh=fine, in_specs=in_specs, out_specs=out_specs, check_vma=False)
```

```python
import math

import jax
import jax.numpy as jnp
from jax import lax
from jax.experimental import pallas as pl
from jax.experimental.pallas import tpu as pltpu
from jax.sharding import Mesh, PartitionSpec as P

C = 128
VX = 4
VY = 8
Z = 16
CELLS = VX * VY * Z
PTS = 512
CAP = 48
GY = 32
SLOTS = GY * CAP
GX = 8
KINDS = 8
HALF = 14
SHARE = HALF * C // GY
ROWS = CAP + SHARE
BF = jnp.bfloat16
F32 = jnp.float32
VMEM = pl.BlockSpec(memory_space=pltpu.VMEM)
SMEM = pl.BlockSpec(memory_space=pltpu.SMEM)
HBM = pl.BlockSpec(memory_space=pltpu.HBM)
LEFT = (((0,), (0,)), ((), ()))
RIGHT = (((1,), (1,)), ((), ()))


def sds(shape, dtype):
    return jax.ShapeDtypeStruct(shape, dtype)


def call(kernel, out_shape, args, scratch=(), smem=0, hbm=0, mib=12, out=VMEM):
    return pl.pallas_call(
        kernel,
        out_shape=out_shape,
        in_specs=[SMEM] * smem + [HBM] * hbm + [VMEM] * (len(args) - smem - hbm),
        out_specs=jax.tree.map(lambda _: out, out_shape),
        scratch_shapes=list(scratch),
        compiler_params=pltpu.CompilerParams(vmem_limit_bytes=mib * 1024 * 1024),
    )(*args)


def iota(shape, dim):
    return lax.broadcasted_iota(jnp.int32, shape, dim)


def dot(a, b, dims=(((1,), (0,)), ((), ()))):
    return lax.dot_general(a, b, dims, preferred_element_type=F32)


def onehot(mask):
    return jnp.where(mask, 1.0, 0.0).astype(BF)


def sigmoid(v):
    return 1.0 / (1.0 + jnp.exp(-v))


def places(slab):
    named = iota((GY, PTS), 0) == slab
    earlier = onehot(iota((PTS, PTS), 0) < iota((PTS, PTS), 1))
    before = dot(onehot(named), earlier)
    rank = jnp.sum(jnp.where(named, before, 0.0), axis=0, keepdims=True)
    return slab * CAP + rank.astype(jnp.int32)


def pack_kernel(feat_hbm, cot_hbm, slab_hbm, base_hbm, near_hbm, off_hbm, sent_hbm,
                both_ref, slab_ref, base_ref, near_ref, off_ref, sent_ref, sems, out_sems):
    moves = [
        pltpu.make_async_copy(slab_hbm, slab_ref, sems.at[0]),
        pltpu.make_async_copy(base_hbm, base_ref, sems.at[1]),
        pltpu.make_async_copy(near_hbm, near_ref, sems.at[2]),
        pltpu.make_async_copy(off_hbm, off_ref, sems.at[3]),
        pltpu.make_async_copy(feat_hbm, both_ref.at[:, 0:C], sems.at[4]),
        pltpu.make_async_copy(cot_hbm, both_ref.at[:, C : 2 * C], sems.at[5]),
    ]
    for move in moves:
        move.start()
    for move in moves[:4]:
        move.wait()
    position = places(slab_ref[...])
    base = base_ref[...]
    near = near_ref[...]
    a = base // (VY * Z)
    b = base // Z % VY
    c = base % Z
    fraction = off_ref[...].astype(F32)
    rows = [a + 2, b, c, near]
    meta = jnp.concatenate(
        [r.astype(F32) for r in rows] + [fraction, jnp.zeros((KINDS - 7, PTS), F32)], axis=0
    ).astype(BF)
    moves[4].wait()
    moves[5].wait()
    both = both_ref[...]
    group = 8
    sends = []
    for g in range(GY // group):
        span = group * CAP
        chosen = onehot(iota((span, PTS), 0) + g * span == position)
        packed = dot(chosen, both).astype(BF).reshape(group, CAP, 2 * C)
        here = pl.ds(g * group, group)
        sent_ref[here, 0:CAP, :] = packed[:, :, :C]
        sent_ref[here, CAP : 2 * CAP, :] = packed[:, :, C:]
        lanes = dot(meta, chosen, RIGHT)
        for i in range(group):
            piece = lanes[:, i * CAP : (i + 1) * CAP]
            wide = jnp.concatenate([piece, jnp.zeros((KINDS, C - CAP), F32)], axis=1)
            sent_ref[g * group + i, 2 * CAP : 2 * CAP + KINDS, :] = wide.astype(BF)
        sends.append(pltpu.make_async_copy(sent_ref.at[here], sent_hbm.at[here], out_sems.at[g]))
        sends[g].start()
    for send in sends:
        send.wait()


def slope(v, s):
    return s * (1.0 + v * (1.0 - s))


def mlp_kernel(feat_ref, cot_ref, mlp_ref, grad_ref):
    feat = feat_ref[...]
    pre = dot(feat, mlp_ref[...])
    grad_pre = (cot_ref[...].astype(F32) * slope(pre, sigmoid(pre))).astype(BF)
    grad_ref[...] = dot(grad_pre, feat, LEFT)


def arrived_meta(got_ref):
    return jnp.concatenate(
        [got_ref[t, 2 * CAP : 2 * CAP + KINDS, :].astype(F32)[:, :CAP] for t in range(GY)], axis=1
    )


def own_matrix(meta):
    near = meta[3:4].astype(jnp.int32)
    base = (meta[0:1] - 2.0) * (VY * Z) + meta[1:2] * Z + meta[2:3]
    own = base.astype(jnp.int32) + near // 4 * (VY * Z) + near // 2 % 2 * Z + near % 2
    return onehot(iota((CELLS, SLOTS), 0) == own)


def voxel_kernel(spot_ref, got_ref, vox_ref, near_ref, far_ref, div_ref, meta_ref):
    meta = arrived_meta(got_ref)
    meta_ref[...] = meta
    own_hot = own_matrix(meta)
    rows = got_ref[:, 0:CAP, :].reshape(SLOTS, C)
    both = jnp.concatenate([rows, jnp.ones((SLOTS, C), BF)], axis=1)
    total = dot(own_hot, both)
    divisor = jnp.maximum(total[:, C:], 1.0)
    div_ref[...] = divisor
    vox_ref[...] = (total[:, :C] / divisor).astype(BF).reshape(VX, VY, Z, C)
    core = spot_ref[0] % 2
    near_ref[...] = vox_ref[pl.ds((VX - 1) * (1 - core), 1)]
    far_ref[...] = vox_ref[pl.ds((VX - 1) * core, 1)]


def spread_kernel(got_ref, meta_ref, matrix_ref, grad_ref):
    meta = meta_ref[...]
    a, b, c = meta[0:1] - 2.0, meta[1:2], meta[2:3]
    fx, fy, fz = meta[4:5], meta[5:6], meta[6:7]

    def side(distance, fraction):
        return jnp.where(distance == 0.0, 1.0 - fraction, jnp.where(distance == 1.0, fraction, 0.0))

    plane = VY * Z
    place = iota((plane, SLOTS), 0)
    wy = side((place // Z).astype(F32) - b, fy)
    wz = side((place % Z).astype(F32) - c, fz)
    for x in range(VX):
        wx = side(x - a, fx)
        matrix_ref[x * plane : (x + 1) * plane, :] = ((wx * wy) * wz).astype(BF)
    cots = got_ref[:, CAP : 2 * CAP, :].reshape(SLOTS, C)
    grad_ref[...] = dot(matrix_ref[...], cots)


def flag(spot_ref, bit):
    return (spot_ref[0] // 2**bit % 2).astype(F32).astype(BF)


def edge_kernel(spot_ref, near_ref, own_ref, far_ref, tail_ref, head_ref):
    core = spot_ref[0] % 2
    inside = flag(spot_ref, 1)
    for ref, y in ((tail_ref, VY - 1), (head_ref, 0)):
        ref[pl.ds((VX + 1) * (1 - core), 1)] = near_ref[:, y : y + 1]
        ref[1 : VX + 1] = own_ref[:, y : y + 1]
        ref[pl.ds((VX + 1) * core, 1)] = far_ref[:, y : y + 1] * inside


def assemble(spot_ref, wide_ref, own_ref, near_ref, far_ref, ylo_ref, yhi_ref):
    core = spot_ref[0] % 2

    def put(x, y, block, inside=None):
        nx, ny = block.shape[0], block.shape[1]
        if inside is not None:
            block = block * flag(spot_ref, inside)
        flat = block.reshape(nx * ny * Z, C).astype(F32)
        z = iota(flat.shape, 0) % Z
        blank = jnp.zeros((8, C), F32)
        down = jnp.concatenate([blank, flat], axis=0)[7 : 7 + flat.shape[0]]
        up = jnp.concatenate([flat, blank], axis=0)[1 : 1 + flat.shape[0]]
        down = jnp.where(z == 0, 0.0, down)
        up = jnp.where(z == Z - 1, 0.0, up)
        shape = (nx, ny, Z, C)
        planes = pl.ds(x, nx)
        wide_ref[planes, y : y + ny, :, 0:C] = down.astype(BF).reshape(shape)
        wide_ref[planes, y : y + ny, :, C : 2 * C] = block
        wide_ref[planes, y : y + ny, :, 2 * C :] = up.astype(BF).reshape(shape)

    put(1, 1, own_ref[...])
    put((VX + 1) * (1 - core), 1, near_ref[...])
    put((VX + 1) * core, 1, far_ref[...], 1)
    put(0, 0, ylo_ref[...], 2)
    put(0, VY + 1, yhi_ref[...], 3)


def window(wide_ref, x, y):
    return wide_ref[x : x + VX, y : y + VY, :, :].reshape(CELLS, 3 * C)


def conv_kernel(spot_ref, vox_ref, near_ref, far_ref, ylo_ref, yhi_ref, weight_ref, gout_ref,
                mlp_ref, keep_ref, send_ref, act_ref, hid_ref, in_ref, out_ref, wide_ref, all_ref):
    core = spot_ref[0] % 2
    assemble(spot_ref, wide_ref, vox_ref, near_ref, far_ref, ylo_ref, yhi_ref)
    hidden = jnp.zeros((CELLS, C), F32)
    for k in range(9):
        taps = weight_ref[3 * k : 3 * k + 3].reshape(3 * C, C)
        hidden = hidden + dot(window(wide_ref, k // 3, k % 3), taps)
    s = sigmoid(hidden)
    act_ref[...] = (hidden * s).astype(BF)
    grad_hidden = (gout_ref[...] * slope(hidden, s)).astype(BF)
    hid_ref[...] = grad_hidden.reshape(VX, VY, Z, C)
    in_ref[...] = hid_ref[pl.ds((VX - 1) * (1 - core), 1)]
    out_ref[...] = hid_ref[pl.ds((VX - 1) * core, 1)]
    turned = grad_hidden.astype(F32).T.astype(BF)
    for k in range(9):
        part = dot(turned, window(wide_ref, k // 3, k % 3))
        for j in range(3):
            all_ref[3 * k + j] = part[:, j * C : (j + 1) * C]
    all_ref[27] = mlp_ref[...]
    keep_ref[...] = all_ref[pl.ds(core * HALF, HALF)]
    send_ref[...] = all_ref[pl.ds((1 - core) * HALF, HALF)].astype(BF)


def sample_kernel(matrix_ref, act_ref, out_ref):
    out_ref[...] = dot(matrix_ref[...], act_ref[...], LEFT).astype(BF).reshape(GY, CAP, C)


def join_kernel(keep_ref, got_ref, filled_ref, out_ref):
    total = keep_ref[...] + got_ref[...].astype(F32)
    out_ref[:, CAP:, :] = total.reshape(GY, SHARE, C).astype(BF)
    out_ref[:, 0:CAP, :] = filled_ref[...]


def share_kernel(got_ref, out_ref):
    total = jnp.sum(got_ref[:, CAP:, :].astype(F32), axis=0)
    out_ref[...] = jnp.broadcast_to(total.astype(BF)[None], out_ref.shape)


def back_kernel(spot_ref, hid_ref, near_ref, far_ref, ylo_ref, yhi_ref, weight_ref, meta_ref, div_ref, out_ref, wide_ref):
    assemble(spot_ref, wide_ref, hid_ref, near_ref, far_ref, ylo_ref, yhi_ref)
    total = jnp.zeros((CELLS, C), F32)
    for k in range(9):
        taps = jnp.concatenate([weight_ref[3 * k + 2 - j] for j in range(3)], axis=1)
        total = total + dot(window(wide_ref, 2 - k // 3, 2 - k % 3), taps, RIGHT)
    mean = (total / div_ref[...]).astype(BF)
    out_ref[...] = dot(own_matrix(meta_ref[...]), mean, LEFT).astype(BF).reshape(GY, CAP, C)


def spread_share_kernel(got_ref, filled_ref, out_ref):
    total = jnp.sum(got_ref[...].astype(F32), axis=0)
    out_ref[:, CAP:, :] = jnp.broadcast_to(total.astype(BF)[None], (GY, SHARE, C))
    out_ref[:, 0:CAP, :] = filled_ref[...]


def unpack(pos, got_ref):
    rows = got_ref[:, 0:CAP, :].reshape(SLOTS, C)
    chosen = jnp.concatenate(
        [onehot(iota((PTS, C), 1) + i * C == pos) for i in range(SLOTS // C)], axis=1
    )
    return dot(chosen, rows)


def forward_kernel(got_ref, slab_ref, feat_ref, cot_ref, mlp_ref, out_ref, pos_ref, back_ref):
    spread = jnp.broadcast_to(places(slab_ref[...]).astype(F32), (C, PTS))
    pos = spread.T.astype(jnp.int32)
    pos_ref[...] = pos
    weight = mlp_ref[...]
    pre = dot(feat_ref[...], weight)
    s = sigmoid(pre)
    grad_pre = (cot_ref[...].astype(F32) * slope(pre, s)).astype(BF)
    back_ref[...] = dot(grad_pre, weight, RIGHT)
    sampled = unpack(pos, got_ref).astype(BF).astype(F32)
    out_ref[...] = (sampled + pre * s).astype(BF)


def take_kernel(got_ref, out_ref):
    out_ref[...] = got_ref[:, CAP:, :].astype(F32).reshape(HALF, C, C).astype(BF)


def backward_kernel(got_ref, pos_ref, back_ref, out_ref):
    out_ref[...] = (unpack(pos_ref[...], got_ref) + back_ref[...]).astype(BF)


def weights_kernel(spot_ref, mine_ref, other_ref, conv_ref, mlp_ref):
    def fill(first_ref, second_ref):
        for o in range(27):
            half = first_ref[o] if o < HALF else second_ref[o - HALF]
            conv_ref[o] = half.astype(F32).T * (1.0 / math.sqrt(GX * GY * CELLS))
        mlp_ref[...] = second_ref[HALF - 1].astype(F32).T * (1.0 / math.sqrt(GX * GY * PTS))

    @pl.when(spot_ref[0] % 2 == 0)
    def _():
        fill(mine_ref, other_ref)

    @pl.when(spot_ref[0] % 2 == 1)
    def _():
        fill(other_ref, mine_ref)


FACE = sds((1, VY, Z, C), BF)
EDGE = sds((VX + 2, 1, Z, C), BF)


def chips(face):
    pairs = [(i, (i + 1) % GX) for i in range(1, GX, 2)]
    return lax.ppermute(face, ("y", "c"), pairs + [(j, i) for i, j in pairs])


def edges(core, near, cells, far):
    tail, head = call(edge_kernel, (EDGE, EDGE), (core, near, cells, far), smem=1, mib=2)
    up = [(i, (i + 1) % GY) for i in range(GY)]
    down = [((i + 1) % GY, i) for i in range(GY)]
    return lax.ppermute(tail, ("x", "z"), up), lax.ppermute(head, ("x", "z"), down)


def exchange(rows):
    return lax.all_to_all(rows, ("x", "z"), split_axis=0, concat_axis=0, tiled=True)


def swap(half):
    return lax.ppermute(half, "c", [(0, 1), (1, 0)])


def body(features, point_slab, base_cell, nearest, offsets, conv_weight, mlp_weight, cotangent):
    strip = lax.axis_index(("y", "c"))
    slab_here = lax.axis_index(("x", "z"))
    core = lax.axis_index("c")
    core = core + 2 * (strip % (GX - 1) != 0) + 4 * (slab_here != 0) + 8 * (slab_here != GY - 1)
    spot = core.reshape(1)
    point_slab, spot = lax.optimization_barrier((point_slab, spot))
    slab = point_slab.reshape(1, PTS)
    line = pltpu.VMEM((1, PTS), jnp.int32)
    sent = call(
        pack_kernel,
        sds((GY, 2 * CAP + KINDS, C), BF),
        (features, cotangent, slab, base_cell.reshape(1, PTS), nearest.reshape(1, PTS), offsets),
        scratch=(
            pltpu.VMEM((PTS, 2 * C), BF),
            line,
            line,
            line,
            pltpu.VMEM((3, PTS), BF),
            pltpu.VMEM((GY, 2 * CAP + KINDS, C), BF),
            pltpu.SemaphoreType.DMA((6,)),
            pltpu.SemaphoreType.DMA((4,)),
        ),
        hbm=6,
        mib=60,
        out=HBM,
    )
    got = exchange(sent)
    mlp_grad = call(mlp_kernel, sds((C, C), F32), (features, cotangent, mlp_weight))
    got, mlp_grad = lax.optimization_barrier((got, mlp_grad))
    cells = sds((VX, VY, Z, C), BF)
    voxels, near, far, divisor, meta = call(
        voxel_kernel,
        (cells, FACE, FACE, sds((CELLS, C), F32), sds((KINDS, SLOTS), F32)),
        (spot, got),
        smem=1,
    )
    near, far = swap(near), chips(far)
    faces = (near, far) + edges(spot, near, voxels, far)
    matrix, grad_out = call(
        spread_kernel, (sds((CELLS, SLOTS), BF), sds((CELLS, C), F32)), (got, meta)
    )
    wide = pltpu.VMEM((VX + 2, VY + 2, Z, 3 * C), BF)
    block = sds((GY, ROWS, C), BF)
    rows = sds((GY, CAP, C), BF)
    keep, send, act, grad_hidden, near, far = call(
        conv_kernel,
        (sds((HALF, C, C), F32), sds((HALF, C, C), BF), sds((CELLS, C), BF), cells, FACE, FACE),
        (spot, voxels) + faces + (conv_weight, grad_out, mlp_grad),
        scratch=(wide, pltpu.VMEM((2 * HALF, C, C), F32)),
        smem=1,
    )
    arrived = swap(send)
    filled = call(sample_kernel, rows, (matrix, act))
    joined = call(join_kernel, block, (keep, arrived, filled))
    first = exchange(joined)
    near, far = swap(near), chips(far)
    grad_faces = (near, far) + edges(spot, near, grad_hidden, far)
    first, grad_faces = lax.optimization_barrier((first, grad_faces))
    filled = call(
        back_kernel,
        rows,
        (spot, grad_hidden) + grad_faces + (conv_weight, meta, divisor),
        scratch=(wide,),
        smem=1,
    )
    shares = call(share_kernel, sds((4, SHARE, C), BF), (first,), mib=4)
    shares = lax.all_to_all(shares, "y", split_axis=0, concat_axis=0, tiled=True)
    joined = call(spread_share_kernel, block, (shares, filled))
    second = exchange(joined)
    output, position, back = call(
        forward_kernel,
        (sds((PTS, C), BF), sds((PTS, C), jnp.int32), sds((PTS, C), F32)),
        (first, slab, features, cotangent, mlp_weight),
    )
    second, back = lax.optimization_barrier((second, back))
    mine = call(take_kernel, sds((HALF, C, C), BF), (second,), mib=4)
    other = swap(mine)
    grad_features = call(backward_kernel, sds((PTS, C), BF), (second, position, back))
    grad_conv, grad_mlp = call(
        weights_kernel, (sds((27, C, C), F32), sds((C, C), F32)), (spot, mine, other), smem=1
    )
    return (output, grad_features, grad_conv, grad_mlp)


def solution(mesh):
    fine = Mesh(mesh.devices.reshape(4, 2, 4, 8), ("y", "c", "x", "z"))
    rows = ("y", "c", "x", "z")
    in_specs = (P(rows, None), P(rows, None), P(rows), P(rows), P(None, rows), P(), P(), P(rows, None))
    out_specs = (P(rows, None), P(rows, None), P(), P())
    return jax.shard_map(body, mesh=fine, in_specs=in_specs, out_specs=out_specs, check_vma=False)
```

```python
import math

import jax
import jax.numpy as jnp
from jax import lax
from jax.experimental import pallas as pl
from jax.experimental.pallas import tpu as pltpu
from jax.sharding import Mesh, PartitionSpec as P

C = 128
VX = 4
VY = 8
Z = 16
CELLS = VX * VY * Z
PTS = 512
CAP = 48
GY = 32
SLOTS = GY * CAP
GX = 8
KINDS = 8
HALF = 14
SHARE = HALF * C // GY
ROWS = CAP + SHARE
BF = jnp.bfloat16
F32 = jnp.float32
VMEM = pl.BlockSpec(memory_space=pltpu.VMEM)
SMEM = pl.BlockSpec(memory_space=pltpu.SMEM)
HBM = pl.BlockSpec(memory_space=pltpu.HBM)
LEFT = (((0,), (0,)), ((), ()))
RIGHT = (((1,), (1,)), ((), ()))


def sds(shape, dtype):
    return jax.ShapeDtypeStruct(shape, dtype)


def call(kernel, out_shape, args, scratch=(), smem=0, hbm=0, mib=12, out=VMEM):
    return pl.pallas_call(
        kernel,
        out_shape=out_shape,
        in_specs=[SMEM] * smem + [HBM] * hbm + [VMEM] * (len(args) - smem - hbm),
        out_specs=jax.tree.map(lambda _: out, out_shape),
        scratch_shapes=list(scratch),
        compiler_params=pltpu.CompilerParams(vmem_limit_bytes=mib * 1024 * 1024),
    )(*args)


def iota(shape, dim):
    return lax.broadcasted_iota(jnp.int32, shape, dim)


def dot(a, b, dims=(((1,), (0,)), ((), ()))):
    return lax.dot_general(a, b, dims, preferred_element_type=F32)


def onehot(mask):
    return jnp.where(mask, 1.0, 0.0).astype(BF)


def sigmoid(v):
    return 1.0 / (1.0 + jnp.exp(-v))


def places(slab):
    named = iota((GY, PTS), 0) == slab
    earlier = onehot(iota((PTS, PTS), 0) < iota((PTS, PTS), 1))
    before = dot(onehot(named), earlier)
    rank = jnp.sum(jnp.where(named, before, 0.0), axis=0, keepdims=True)
    return slab * CAP + rank.astype(jnp.int32)


def pack_kernel(feat_hbm, cot_hbm, slab_hbm, base_hbm, near_hbm, off_hbm, sent_hbm,
                both_ref, slab_ref, base_ref, near_ref, off_ref, sent_ref, sems, out_sems):
    moves = [
        pltpu.make_async_copy(slab_hbm, slab_ref, sems.at[0]),
        pltpu.make_async_copy(base_hbm, base_ref, sems.at[1]),
        pltpu.make_async_copy(near_hbm, near_ref, sems.at[2]),
        pltpu.make_async_copy(off_hbm, off_ref, sems.at[3]),
        pltpu.make_async_copy(feat_hbm, both_ref.at[:, 0:C], sems.at[4]),
        pltpu.make_async_copy(cot_hbm, both_ref.at[:, C : 2 * C], sems.at[5]),
    ]
    for move in moves:
        move.start()
    for move in moves[:4]:
        move.wait()
    position = places(slab_ref[...])
    base = base_ref[...]
    near = near_ref[...]
    a = base // (VY * Z)
    b = base // Z % VY
    c = base % Z
    fraction = off_ref[...].astype(F32)
    rows = [a + 2, b, c, near]
    meta = jnp.concatenate(
        [r.astype(F32) for r in rows] + [fraction, jnp.zeros((KINDS - 7, PTS), F32)], axis=0
    ).astype(BF)
    moves[4].wait()
    moves[5].wait()
    both = both_ref[...]
    group = 8
    sends = []
    for g in range(GY // group):
        span = group * CAP
        chosen = onehot(iota((span, PTS), 0) + g * span == position)
        packed = dot(chosen, both).astype(BF).reshape(group, CAP, 2 * C)
        here = pl.ds(g * group, group)
        sent_ref[here, 0:CAP, :] = packed[:, :, :C]
        sent_ref[here, CAP : 2 * CAP, :] = packed[:, :, C:]
        lanes = dot(meta, chosen, RIGHT)
        for i in range(group):
            piece = lanes[:, i * CAP : (i + 1) * CAP]
            wide = jnp.concatenate([piece, jnp.zeros((KINDS, C - CAP), F32)], axis=1)
            sent_ref[g * group + i, 2 * CAP : 2 * CAP + KINDS, :] = wide.astype(BF)
        sends.append(pltpu.make_async_copy(sent_ref.at[here], sent_hbm.at[here], out_sems.at[g]))
        sends[g].start()
    for send in sends:
        send.wait()


def slope(v, s):
    return s * (1.0 + v * (1.0 - s))


def mlp_kernel(feat_ref, cot_ref, mlp_ref, grad_ref):
    feat = feat_ref[...]
    pre = dot(feat, mlp_ref[...])
    grad_pre = (cot_ref[...].astype(F32) * slope(pre, sigmoid(pre))).astype(BF)
    grad_ref[...] = dot(grad_pre, feat, LEFT)


def arrived_meta(got_ref):
    return jnp.concatenate(
        [got_ref[t, 2 * CAP : 2 * CAP + KINDS, :].astype(F32)[:, :CAP] for t in range(GY)], axis=1
    )


def own_matrix(meta):
    near = meta[3:4].astype(jnp.int32)
    base = (meta[0:1] - 2.0) * (VY * Z) + meta[1:2] * Z + meta[2:3]
    own = base.astype(jnp.int32) + near // 4 * (VY * Z) + near // 2 % 2 * Z + near % 2
    return onehot(iota((CELLS, SLOTS), 0) == own)


def voxel_kernel(spot_ref, got_ref, vox_ref, near_ref, far_ref, div_ref, meta_ref):
    meta = arrived_meta(got_ref)
    meta_ref[...] = meta
    own_hot = own_matrix(meta)
    rows = got_ref[:, 0:CAP, :].reshape(SLOTS, C)
    both = jnp.concatenate([rows, jnp.ones((SLOTS, C), BF)], axis=1)
    total = dot(own_hot, both)
    divisor = jnp.maximum(total[:, C:], 1.0)
    div_ref[...] = divisor
    vox_ref[...] = (total[:, :C] / divisor).astype(BF).reshape(VX, VY, Z, C)
    core = spot_ref[0] % 2
    near_ref[...] = vox_ref[pl.ds((VX - 1) * (1 - core), 1)]
    far_ref[...] = vox_ref[pl.ds((VX - 1) * core, 1)]


def spread_kernel(got_ref, meta_ref, matrix_ref, grad_ref):
    meta = meta_ref[...]
    a, b, c = meta[0:1] - 2.0, meta[1:2], meta[2:3]
    fx, fy, fz = meta[4:5], meta[5:6], meta[6:7]

    def side(distance, fraction):
        return jnp.where(distance == 0.0, 1.0 - fraction, jnp.where(distance == 1.0, fraction, 0.0))

    plane = VY * Z
    place = iota((plane, SLOTS), 0)
    wy = side((place // Z).astype(F32) - b, fy)
    wz = side((place % Z).astype(F32) - c, fz)
    for x in range(VX):
        wx = side(x - a, fx)
        matrix_ref[x * plane : (x + 1) * plane, :] = ((wx * wy) * wz).astype(BF)
    cots = got_ref[:, CAP : 2 * CAP, :].reshape(SLOTS, C)
    grad_ref[...] = dot(matrix_ref[...], cots)


def flag(spot_ref, bit):
    return (spot_ref[0] // 2**bit % 2).astype(F32).astype(BF)


def edge_kernel(spot_ref, near_ref, own_ref, far_ref, even_ref, odd_ref):
    core = spot_ref[0] % 2
    turn = spot_ref[0] // 4 % 2
    inside = flag(spot_ref, 1)
    for ref, y in ((even_ref, (VY - 1) * (1 - turn)), (odd_ref, (VY - 1) * turn)):
        row = pl.ds(y, 1)
        ref[pl.ds((VX + 1) * (1 - core), 1)] = near_ref[:, row]
        ref[1 : VX + 1] = own_ref[:, row]
        ref[pl.ds((VX + 1) * core, 1)] = far_ref[:, row] * inside


def assemble(spot_ref, wide_ref, own_ref, near_ref, far_ref, even_ref, odd_ref):
    core = spot_ref[0] % 2
    turn = spot_ref[0] // 4 % 2

    def put(x, y, block, inside=None):
        nx, ny = block.shape[0], block.shape[1]
        if inside is not None:
            block = block * flag(spot_ref, inside)
        flat = block.reshape(nx * ny * Z, C).astype(F32)
        z = iota(flat.shape, 0) % Z
        blank = jnp.zeros((8, C), F32)
        down = jnp.concatenate([blank, flat], axis=0)[7 : 7 + flat.shape[0]]
        up = jnp.concatenate([flat, blank], axis=0)[1 : 1 + flat.shape[0]]
        down = jnp.where(z == 0, 0.0, down)
        up = jnp.where(z == Z - 1, 0.0, up)
        shape = (nx, ny, Z, C)
        planes, rows = pl.ds(x, nx), pl.ds(y, ny)
        wide_ref[planes, rows, :, 0:C] = down.astype(BF).reshape(shape)
        wide_ref[planes, rows, :, C : 2 * C] = block
        wide_ref[planes, rows, :, 2 * C :] = up.astype(BF).reshape(shape)

    put(1, 1, own_ref[...])
    put((VX + 1) * (1 - core), 1, near_ref[...])
    put((VX + 1) * core, 1, far_ref[...], 1)
    put(0, (VY + 1) * (1 - turn), even_ref[...])
    put(0, (VY + 1) * turn, odd_ref[...], 3)


def window(wide_ref, x, y):
    return wide_ref[x : x + VX, y : y + VY, :, :].reshape(CELLS, 3 * C)


def conv_kernel(spot_ref, vox_ref, near_ref, far_ref, even_ref, odd_ref, weight_ref, gout_ref,
                mlp_ref, keep_ref, send_ref, act_ref, hid_ref, in_ref, out_ref, wide_ref, all_ref):
    core = spot_ref[0] % 2
    assemble(spot_ref, wide_ref, vox_ref, near_ref, far_ref, even_ref, odd_ref)
    hidden = jnp.zeros((CELLS, C), F32)
    for k in range(9):
        taps = weight_ref[3 * k : 3 * k + 3].reshape(3 * C, C)
        hidden = hidden + dot(window(wide_ref, k // 3, k % 3), taps)
    s = sigmoid(hidden)
    act_ref[...] = (hidden * s).astype(BF)
    grad_hidden = (gout_ref[...] * slope(hidden, s)).astype(BF)
    hid_ref[...] = grad_hidden.reshape(VX, VY, Z, C)
    in_ref[...] = hid_ref[pl.ds((VX - 1) * (1 - core), 1)]
    out_ref[...] = hid_ref[pl.ds((VX - 1) * core, 1)]
    turned = grad_hidden.astype(F32).T.astype(BF)
    for k in range(9):
        part = dot(turned, window(wide_ref, k // 3, k % 3))
        for j in range(3):
            all_ref[3 * k + j] = part[:, j * C : (j + 1) * C]
    all_ref[27] = mlp_ref[...]
    keep_ref[...] = all_ref[pl.ds(core * HALF, HALF)]
    send_ref[...] = all_ref[pl.ds((1 - core) * HALF, HALF)].astype(BF)


def sample_kernel(matrix_ref, act_ref, out_ref):
    out_ref[...] = dot(matrix_ref[...], act_ref[...], LEFT).astype(BF).reshape(GY, CAP, C)


def join_kernel(keep_ref, got_ref, filled_ref, out_ref):
    total = keep_ref[...] + got_ref[...].astype(F32)
    out_ref[:, CAP:, :] = total.reshape(GY, SHARE, C).astype(BF)
    out_ref[:, 0:CAP, :] = filled_ref[...]


def share_kernel(got_ref, out_ref):
    total = jnp.sum(got_ref[:, CAP:, :].astype(F32), axis=0)
    out_ref[...] = jnp.broadcast_to(total.astype(BF)[None], out_ref.shape)


def back_kernel(spot_ref, hid_ref, near_ref, far_ref, even_ref, odd_ref, weight_ref, meta_ref, div_ref, out_ref, wide_ref):
    assemble(spot_ref, wide_ref, hid_ref, near_ref, far_ref, even_ref, odd_ref)
    total = jnp.zeros((CELLS, C), F32)
    for k in range(9):
        taps = jnp.concatenate([weight_ref[3 * k + 2 - j] for j in range(3)], axis=1)
        total = total + dot(window(wide_ref, 2 - k // 3, 2 - k % 3), taps, RIGHT)
    mean = (total / div_ref[...]).astype(BF)
    out_ref[...] = dot(own_matrix(meta_ref[...]), mean, LEFT).astype(BF).reshape(GY, CAP, C)


def spread_share_kernel(got_ref, filled_ref, out_ref):
    total = jnp.sum(got_ref[...].astype(F32), axis=0)
    out_ref[:, CAP:, :] = jnp.broadcast_to(total.astype(BF)[None], (GY, SHARE, C))
    out_ref[:, 0:CAP, :] = filled_ref[...]


def unpack(pos, got_ref):
    rows = got_ref[:, 0:CAP, :].reshape(SLOTS, C)
    chosen = jnp.concatenate(
        [onehot(iota((PTS, C), 1) + i * C == pos) for i in range(SLOTS // C)], axis=1
    )
    return dot(chosen, rows)


def forward_kernel(got_ref, slab_ref, feat_ref, cot_ref, mlp_ref, out_ref, pos_ref, back_ref):
    spread = jnp.broadcast_to(places(slab_ref[...]).astype(F32), (C, PTS))
    pos = spread.T.astype(jnp.int32)
    pos_ref[...] = pos
    weight = mlp_ref[...]
    pre = dot(feat_ref[...], weight)
    s = sigmoid(pre)
    grad_pre = (cot_ref[...].astype(F32) * slope(pre, s)).astype(BF)
    back_ref[...] = dot(grad_pre, weight, RIGHT)
    sampled = unpack(pos, got_ref).astype(BF).astype(F32)
    out_ref[...] = (sampled + pre * s).astype(BF)


def take_kernel(got_ref, out_ref):
    out_ref[...] = got_ref[:, CAP:, :].astype(F32).reshape(HALF, C, C).astype(BF)


def backward_kernel(got_ref, pos_ref, back_ref, out_ref):
    out_ref[...] = (unpack(pos_ref[...], got_ref) + back_ref[...]).astype(BF)


def weights_kernel(spot_ref, mine_ref, other_ref, conv_ref, mlp_ref):
    def fill(first_ref, second_ref):
        for o in range(27):
            half = first_ref[o] if o < HALF else second_ref[o - HALF]
            conv_ref[o] = half.astype(F32).T * (1.0 / math.sqrt(GX * GY * CELLS))
        mlp_ref[...] = second_ref[HALF - 1].astype(F32).T * (1.0 / math.sqrt(GX * GY * PTS))

    @pl.when(spot_ref[0] % 2 == 0)
    def _():
        fill(mine_ref, other_ref)

    @pl.when(spot_ref[0] % 2 == 1)
    def _():
        fill(other_ref, mine_ref)


FACE = sds((1, VY, Z, C), BF)
EDGE = sds((VX + 2, 1, Z, C), BF)


def pairs(count, start):
    swaps = [(i, (i + 1) % count) for i in range(start, count, 2)]
    return swaps + [(j, i) for i, j in swaps]


def chips(face):
    return lax.ppermute(face, ("y", "c"), pairs(GX, 1))


def edges(spot, near, cells, far):
    even, odd = call(edge_kernel, (EDGE, EDGE), (spot, near, cells, far), smem=1, mib=2)
    odds = [(s * GY + i, s * GY + j) for s in range(GX) for i, j in pairs(GY, 1) if abs(i - j) == 1]
    ends = [(s * GY + i, (s ^ 1) * GY + i) for s in range(GX) for i in (0, GY - 1)]
    return (
        lax.ppermute(even, ("x", "z"), pairs(GY, 0)),
        lax.ppermute(odd, ("y", "c", "x", "z"), odds + ends),
    )


def exchange(rows):
    return lax.all_to_all(rows, ("x", "z"), split_axis=0, concat_axis=0, tiled=True)


def swap(half):
    return lax.ppermute(half, "c", [(0, 1), (1, 0)])


def body(features, point_slab, base_cell, nearest, offsets, conv_weight, mlp_weight, cotangent):
    strip = lax.axis_index(("y", "c"))
    slab_here = lax.axis_index(("x", "z"))
    core = lax.axis_index("c")
    core = core + 2 * (strip % (GX - 1) != 0) + 4 * (slab_here % 2) + 8 * (slab_here % (GY - 1) != 0)
    spot = core.reshape(1)
    point_slab, spot = lax.optimization_barrier((point_slab, spot))
    slab = point_slab.reshape(1, PTS)
    line = pltpu.VMEM((1, PTS), jnp.int32)
    sent = call(
        pack_kernel,
        sds((GY, 2 * CAP + KINDS, C), BF),
        (features, cotangent, slab, base_cell.reshape(1, PTS), nearest.reshape(1, PTS), offsets),
        scratch=(
            pltpu.VMEM((PTS, 2 * C), BF),
            line,
            line,
            line,
            pltpu.VMEM((3, PTS), BF),
            pltpu.VMEM((GY, 2 * CAP + KINDS, C), BF),
            pltpu.SemaphoreType.DMA((6,)),
            pltpu.SemaphoreType.DMA((4,)),
        ),
        hbm=6,
        mib=60,
        out=HBM,
    )
    got = exchange(sent)
    mlp_grad = call(mlp_kernel, sds((C, C), F32), (features, cotangent, mlp_weight))
    got, mlp_grad = lax.optimization_barrier((got, mlp_grad))
    cells = sds((VX, VY, Z, C), BF)
    voxels, near, far, divisor, meta = call(
        voxel_kernel,
        (cells, FACE, FACE, sds((CELLS, C), F32), sds((KINDS, SLOTS), F32)),
        (spot, got),
        smem=1,
    )
    near, far = swap(near), chips(far)
    faces = (near, far) + edges(spot, near, voxels, far)
    matrix, grad_out = call(
        spread_kernel, (sds((CELLS, SLOTS), BF), sds((CELLS, C), F32)), (got, meta)
    )
    wide = pltpu.VMEM((VX + 2, VY + 2, Z, 3 * C), BF)
    block = sds((GY, ROWS, C), BF)
    rows = sds((GY, CAP, C), BF)
    keep, send, act, grad_hidden, near, far = call(
        conv_kernel,
        (sds((HALF, C, C), F32), sds((HALF, C, C), BF), sds((CELLS, C), BF), cells, FACE, FACE),
        (spot, voxels) + faces + (conv_weight, grad_out, mlp_grad),
        scratch=(wide, pltpu.VMEM((2 * HALF, C, C), F32)),
        smem=1,
    )
    arrived = swap(send)
    filled = call(sample_kernel, rows, (matrix, act))
    joined = call(join_kernel, block, (keep, arrived, filled))
    first = exchange(joined)
    near, far = swap(near), chips(far)
    grad_faces = (near, far) + edges(spot, near, grad_hidden, far)
    first, grad_faces = lax.optimization_barrier((first, grad_faces))
    filled = call(
        back_kernel,
        rows,
        (spot, grad_hidden) + grad_faces + (conv_weight, meta, divisor),
        scratch=(wide,),
        smem=1,
    )
    shares = call(share_kernel, sds((4, SHARE, C), BF), (first,), mib=4)
    shares = lax.all_to_all(shares, "y", split_axis=0, concat_axis=0, tiled=True)
    joined = call(spread_share_kernel, block, (shares, filled))
    second = exchange(joined)
    output, position, back = call(
        forward_kernel,
        (sds((PTS, C), BF), sds((PTS, C), jnp.int32), sds((PTS, C), F32)),
        (first, slab, features, cotangent, mlp_weight),
    )
    second, back = lax.optimization_barrier((second, back))
    mine = call(take_kernel, sds((HALF, C, C), BF), (second,), mib=4)
    other = swap(mine)
    grad_features = call(backward_kernel, sds((PTS, C), BF), (second, position, back))
    grad_conv, grad_mlp = call(
        weights_kernel, (sds((27, C, C), F32), sds((C, C), F32)), (spot, mine, other), smem=1
    )
    return (output, grad_features, grad_conv, grad_mlp)


def solution(mesh):
    fine = Mesh(mesh.devices.reshape(4, 2, 4, 8), ("y", "c", "x", "z"))
    rows = ("y", "c", "x", "z")
    in_specs = (P(rows, None), P(rows, None), P(rows), P(rows), P(None, rows), P(), P(), P(rows, None))
    out_specs = (P(rows, None), P(rows, None), P(), P())
    return jax.shard_map(body, mesh=fine, in_specs=in_specs, out_specs=out_specs, check_vma=False)
```

```python
import math

import jax
import jax.numpy as jnp
from jax import lax
from jax.experimental import pallas as pl
from jax.experimental.pallas import tpu as pltpu
from jax.sharding import Mesh, PartitionSpec as P

C = 128
VX = 4
VY = 8
Z = 16
CELLS = VX * VY * Z
PTS = 512
CAP = 48
GY = 32
SLOTS = GY * CAP
GX = 8
KINDS = 8
HALF = 14
SHARE = HALF * C // GY
ROWS = CAP + SHARE
BF = jnp.bfloat16
F32 = jnp.float32
VMEM = pl.BlockSpec(memory_space=pltpu.VMEM)
SMEM = pl.BlockSpec(memory_space=pltpu.SMEM)
HBM = pl.BlockSpec(memory_space=pltpu.HBM)
LEFT = (((0,), (0,)), ((), ()))
RIGHT = (((1,), (1,)), ((), ()))


def sds(shape, dtype):
    return jax.ShapeDtypeStruct(shape, dtype)


def call(kernel, out_shape, args, scratch=(), smem=0, hbm=0, mib=12, out=VMEM):
    return pl.pallas_call(
        kernel,
        out_shape=out_shape,
        in_specs=[SMEM] * smem + [HBM] * hbm + [VMEM] * (len(args) - smem - hbm),
        out_specs=jax.tree.map(lambda _: out, out_shape),
        scratch_shapes=list(scratch),
        compiler_params=pltpu.CompilerParams(vmem_limit_bytes=mib * 1024 * 1024),
    )(*args)


def iota(shape, dim):
    return lax.broadcasted_iota(jnp.int32, shape, dim)


def dot(a, b, dims=(((1,), (0,)), ((), ()))):
    return lax.dot_general(a, b, dims, preferred_element_type=F32)


def onehot(mask):
    return jnp.where(mask, 1.0, 0.0).astype(BF)


def sigmoid(v):
    return 1.0 / (1.0 + jnp.exp(-v))


def places(slab):
    named = iota((GY, PTS), 0) == slab
    earlier = onehot(iota((PTS, PTS), 0) < iota((PTS, PTS), 1))
    before = dot(onehot(named), earlier)
    rank = jnp.sum(jnp.where(named, before, 0.0), axis=0, keepdims=True)
    return slab * CAP + rank.astype(jnp.int32)


def pack_kernel(feat_hbm, cot_hbm, slab_hbm, base_hbm, near_hbm, off_hbm, sent_hbm,
                both_ref, slab_ref, base_ref, near_ref, off_ref, sent_ref, sems, out_sems):
    moves = [
        pltpu.make_async_copy(slab_hbm, slab_ref, sems.at[0]),
        pltpu.make_async_copy(base_hbm, base_ref, sems.at[1]),
        pltpu.make_async_copy(near_hbm, near_ref, sems.at[2]),
        pltpu.make_async_copy(off_hbm, off_ref, sems.at[3]),
        pltpu.make_async_copy(feat_hbm, both_ref.at[:, 0:C], sems.at[4]),
        pltpu.make_async_copy(cot_hbm, both_ref.at[:, C : 2 * C], sems.at[5]),
    ]
    for move in moves:
        move.start()
    for move in moves[:4]:
        move.wait()
    position = places(slab_ref[...])
    base = base_ref[...]
    near = near_ref[...]
    a = base // (VY * Z)
    b = base // Z % VY
    c = base % Z
    fraction = off_ref[...].astype(F32)
    rows = [a + 2, b, c, near]
    meta = jnp.concatenate(
        [r.astype(F32) for r in rows] + [fraction, jnp.zeros((KINDS - 7, PTS), F32)], axis=0
    ).astype(BF)
    moves[4].wait()
    moves[5].wait()
    both = both_ref[...]
    group = 8
    sends = []
    for g in range(GY // group):
        span = group * CAP
        chosen = onehot(iota((span, PTS), 0) + g * span == position)
        packed = dot(chosen, both).astype(BF).reshape(group, CAP, 2 * C)
        here = pl.ds(g * group, group)
        sent_ref[here, 0:CAP, :] = packed[:, :, :C]
        sent_ref[here, CAP : 2 * CAP, :] = packed[:, :, C:]
        lanes = dot(meta, chosen, RIGHT)
        for i in range(group):
            piece = lanes[:, i * CAP : (i + 1) * CAP]
            wide = jnp.concatenate([piece, jnp.zeros((KINDS, C - CAP), F32)], axis=1)
            sent_ref[g * group + i, 2 * CAP : 2 * CAP + KINDS, :] = wide.astype(BF)
        sends.append(pltpu.make_async_copy(sent_ref.at[here], sent_hbm.at[here], out_sems.at[g]))
        sends[g].start()
    for send in sends:
        send.wait()


def slope(v, s):
    return s * (1.0 + v * (1.0 - s))


def mlp_kernel(feat_ref, cot_ref, mlp_ref, grad_ref):
    feat = feat_ref[...]
    pre = dot(feat, mlp_ref[...])
    grad_pre = (cot_ref[...].astype(F32) * slope(pre, sigmoid(pre))).astype(BF)
    grad_ref[...] = dot(grad_pre, feat, LEFT)


def arrived_meta(got_ref):
    return jnp.concatenate(
        [got_ref[t, 2 * CAP : 2 * CAP + KINDS, :].astype(F32)[:, :CAP] for t in range(GY)], axis=1
    )


def own_matrix(meta):
    near = meta[3:4].astype(jnp.int32)
    base = (meta[0:1] - 2.0) * (VY * Z) + meta[1:2] * Z + meta[2:3]
    own = base.astype(jnp.int32) + near // 4 * (VY * Z) + near // 2 % 2 * Z + near % 2
    return onehot(iota((CELLS, SLOTS), 0) == own)


def voxel_kernel(spot_ref, got_ref, vox_ref, near_ref, far_ref, div_ref, meta_ref):
    meta = arrived_meta(got_ref)
    meta_ref[...] = meta
    own_hot = own_matrix(meta)
    rows = got_ref[:, 0:CAP, :].reshape(SLOTS, C)
    both = jnp.concatenate([rows, jnp.ones((SLOTS, C), BF)], axis=1)
    total = dot(own_hot, both)
    divisor = jnp.maximum(total[:, C:], 1.0)
    div_ref[...] = divisor
    vox_ref[...] = (total[:, :C] / divisor).astype(BF).reshape(VX, VY, Z, C)
    core = spot_ref[0] % 2
    near_ref[...] = vox_ref[pl.ds((VX - 1) * (1 - core), 1)]
    far_ref[...] = vox_ref[pl.ds((VX - 1) * core, 1)]


def spread_kernel(got_ref, meta_ref, matrix_ref, grad_ref):
    meta = meta_ref[...]
    a, b, c = meta[0:1] - 2.0, meta[1:2], meta[2:3]
    fx, fy, fz = meta[4:5], meta[5:6], meta[6:7]

    def side(distance, fraction):
        return jnp.where(distance == 0.0, 1.0 - fraction, jnp.where(distance == 1.0, fraction, 0.0))

    plane = VY * Z
    place = iota((plane, SLOTS), 0)
    wy = side((place // Z).astype(F32) - b, fy)
    wz = side((place % Z).astype(F32) - c, fz)
    for x in range(VX):
        wx = side(x - a, fx)
        matrix_ref[x * plane : (x + 1) * plane, :] = ((wx * wy) * wz).astype(BF)
    cots = got_ref[:, CAP : 2 * CAP, :].reshape(SLOTS, C)
    grad_ref[...] = dot(matrix_ref[...], cots)


def flag(spot_ref, bit):
    return (spot_ref[0] // 2**bit % 2).astype(F32).astype(BF)


def edge_kernel(spot_ref, near_ref, own_ref, far_ref, even_ref, odd_ref):
    core = spot_ref[0] % 2
    turn = spot_ref[0] // 4 % 2
    inside = flag(spot_ref, 1)
    for ref, y in ((even_ref, (VY - 1) * (1 - turn)), (odd_ref, (VY - 1) * turn)):
        row = pl.ds(y, 1)
        ref[pl.ds((VX + 1) * (1 - core), 1)] = near_ref[:, row]
        ref[1 : VX + 1] = own_ref[:, row]
        ref[pl.ds((VX + 1) * core, 1)] = far_ref[:, row] * inside


def assemble(spot_ref, wide_ref, own_ref, near_ref, far_ref, even_ref, odd_ref):
    core = spot_ref[0] % 2
    turn = spot_ref[0] // 4 % 2

    def put(x, y, block, inside=None):
        nx, ny = block.shape[0], block.shape[1]
        if inside is not None:
            block = block * flag(spot_ref, inside)
        flat = block.reshape(nx * ny * Z, C).astype(F32)
        z = iota(flat.shape, 0) % Z
        blank = jnp.zeros((8, C), F32)
        down = jnp.concatenate([blank, flat], axis=0)[7 : 7 + flat.shape[0]]
        up = jnp.concatenate([flat, blank], axis=0)[1 : 1 + flat.shape[0]]
        down = jnp.where(z == 0, 0.0, down)
        up = jnp.where(z == Z - 1, 0.0, up)
        shape = (nx, ny, Z, C)
        planes, rows = pl.ds(x, nx), pl.ds(y, ny)
        wide_ref[planes, rows, :, 0:C] = down.astype(BF).reshape(shape)
        wide_ref[planes, rows, :, C : 2 * C] = block
        wide_ref[planes, rows, :, 2 * C :] = up.astype(BF).reshape(shape)

    put(1, 1, own_ref[...])
    put((VX + 1) * (1 - core), 1, near_ref[...])
    put((VX + 1) * core, 1, far_ref[...], 1)
    put(0, (VY + 1) * (1 - turn), even_ref[...])
    put(0, (VY + 1) * turn, odd_ref[...], 3)


def window(wide_ref, x, y):
    return wide_ref[x : x + VX, y : y + VY, :, :].reshape(CELLS, 3 * C)


def conv_kernel(spot_ref, vox_ref, near_ref, far_ref, even_ref, odd_ref, weight_ref, gout_ref,
                mlp_ref, keep_ref, send_ref, act_ref, hid_ref, in_ref, out_ref, wide_ref, all_ref):
    core = spot_ref[0] % 2
    assemble(spot_ref, wide_ref, vox_ref, near_ref, far_ref, even_ref, odd_ref)
    hidden = jnp.zeros((CELLS, C), F32)
    for k in range(9):
        taps = weight_ref[3 * k : 3 * k + 3].reshape(3 * C, C)
        hidden = hidden + dot(window(wide_ref, k // 3, k % 3), taps)
    s = sigmoid(hidden)
    act_ref[...] = (hidden * s).astype(BF)
    grad_hidden = (gout_ref[...] * slope(hidden, s)).astype(BF)
    hid_ref[...] = grad_hidden.reshape(VX, VY, Z, C)
    in_ref[...] = hid_ref[pl.ds((VX - 1) * (1 - core), 1)]
    out_ref[...] = hid_ref[pl.ds((VX - 1) * core, 1)]
    turned = grad_hidden.astype(F32).T.astype(BF)
    for k in range(9):
        part = dot(turned, window(wide_ref, k // 3, k % 3))
        for j in range(3):
            all_ref[3 * k + j] = part[:, j * C : (j + 1) * C]
    all_ref[27] = mlp_ref[...]
    keep_ref[...] = all_ref[pl.ds(core * HALF, HALF)]
    send_ref[...] = all_ref[pl.ds((1 - core) * HALF, HALF)].astype(BF)


def sample_kernel(matrix_ref, act_ref, out_ref):
    out_ref[...] = dot(matrix_ref[...], act_ref[...], LEFT).astype(BF).reshape(GY, CAP, C)


def join_kernel(keep_ref, got_ref, filled_ref, out_ref):
    total = keep_ref[...] + got_ref[...].astype(F32)
    out_ref[:, CAP:, :] = total.reshape(GY, SHARE, C).astype(BF)
    out_ref[:, 0:CAP, :] = filled_ref[...]


def share_kernel(got_ref, out_ref):
    out_ref[...] = jnp.sum(got_ref[:, CAP:, :].astype(F32), axis=0).astype(BF)


def pair_kernel(own_ref, got_ref, out_ref):
    out_ref[...] = own_ref[...].astype(F32) + got_ref[...].astype(F32)


def back_kernel(spot_ref, hid_ref, near_ref, far_ref, even_ref, odd_ref, weight_ref, meta_ref, div_ref, out_ref, wide_ref):
    assemble(spot_ref, wide_ref, hid_ref, near_ref, far_ref, even_ref, odd_ref)
    total = jnp.zeros((CELLS, C), F32)
    for k in range(9):
        taps = jnp.concatenate([weight_ref[3 * k + 2 - j] for j in range(3)], axis=1)
        total = total + dot(window(wide_ref, 2 - k // 3, 2 - k % 3), taps, RIGHT)
    mean = (total / div_ref[...]).astype(BF)
    out_ref[...] = dot(own_matrix(meta_ref[...]), mean, LEFT).astype(BF).reshape(GY, CAP, C)


def deal_kernel(own_ref, got_ref, filled_ref, out_ref):
    total = (own_ref[...] + got_ref[...]).astype(BF)
    out_ref[:, CAP:, :] = jnp.broadcast_to(total[None], (GY, SHARE, C))
    out_ref[:, 0:CAP, :] = filled_ref[...]


def unpack(pos, got_ref):
    rows = got_ref[:, 0:CAP, :].reshape(SLOTS, C)
    chosen = jnp.concatenate(
        [onehot(iota((PTS, C), 1) + i * C == pos) for i in range(SLOTS // C)], axis=1
    )
    return dot(chosen, rows)


def forward_kernel(got_ref, slab_ref, feat_ref, cot_ref, mlp_ref, out_ref, pos_ref, back_ref):
    spread = jnp.broadcast_to(places(slab_ref[...]).astype(F32), (C, PTS))
    pos = spread.T.astype(jnp.int32)
    pos_ref[...] = pos
    weight = mlp_ref[...]
    pre = dot(feat_ref[...], weight)
    s = sigmoid(pre)
    grad_pre = (cot_ref[...].astype(F32) * slope(pre, s)).astype(BF)
    back_ref[...] = dot(grad_pre, weight, RIGHT)
    sampled = unpack(pos, got_ref).astype(BF).astype(F32)
    out_ref[...] = (sampled + pre * s).astype(BF)


def take_kernel(got_ref, out_ref):
    out_ref[...] = got_ref[:, CAP:, :].astype(F32).reshape(HALF, C, C).astype(BF)


def backward_kernel(got_ref, pos_ref, back_ref, out_ref):
    out_ref[...] = (unpack(pos_ref[...], got_ref) + back_ref[...]).astype(BF)


def weights_kernel(spot_ref, mine_ref, other_ref, conv_ref, mlp_ref):
    def fill(first_ref, second_ref):
        for o in range(27):
            half = first_ref[o] if o < HALF else second_ref[o - HALF]
            conv_ref[o] = half.astype(F32).T * (1.0 / math.sqrt(GX * GY * CELLS))
        mlp_ref[...] = second_ref[HALF - 1].astype(F32).T * (1.0 / math.sqrt(GX * GY * PTS))

    @pl.when(spot_ref[0] % 2 == 0)
    def _():
        fill(mine_ref, other_ref)

    @pl.when(spot_ref[0] % 2 == 1)
    def _():
        fill(other_ref, mine_ref)


FACE = sds((1, VY, Z, C), BF)
EDGE = sds((VX + 2, 1, Z, C), BF)


def pairs(count, start):
    swaps = [(i, (i + 1) % count) for i in range(start, count, 2)]
    return swaps + [(j, i) for i, j in swaps]


def chips(face):
    return lax.ppermute(face, ("y", "c"), pairs(GX, 1))


def edges(spot, near, cells, far):
    even, odd = call(edge_kernel, (EDGE, EDGE), (spot, near, cells, far), smem=1, mib=2)
    odds = [(s * GY + i, s * GY + j) for s in range(GX) for i, j in pairs(GY, 1) if abs(i - j) == 1]
    ends = [(s * GY + i, (s ^ 1) * GY + i) for s in range(GX) for i in (0, GY - 1)]
    return (
        lax.ppermute(even, ("x", "z"), pairs(GY, 0)),
        lax.ppermute(odd, ("y", "c", "x", "z"), odds + ends),
    )


def exchange(rows):
    return lax.all_to_all(rows, ("x", "z"), split_axis=0, concat_axis=0, tiled=True)


def across(share, partner):
    return lax.ppermute(share, "y", list(enumerate(partner)))


def swap(half):
    return lax.ppermute(half, "c", [(0, 1), (1, 0)])


def body(features, point_slab, base_cell, nearest, offsets, conv_weight, mlp_weight, cotangent):
    strip = lax.axis_index(("y", "c"))
    slab_here = lax.axis_index(("x", "z"))
    core = lax.axis_index("c")
    core = core + 2 * (strip % (GX - 1) != 0) + 4 * (slab_here % 2) + 8 * (slab_here % (GY - 1) != 0)
    spot = core.reshape(1)
    point_slab, spot = lax.optimization_barrier((point_slab, spot))
    slab = point_slab.reshape(1, PTS)
    line = pltpu.VMEM((1, PTS), jnp.int32)
    sent = call(
        pack_kernel,
        sds((GY, 2 * CAP + KINDS, C), BF),
        (features, cotangent, slab, base_cell.reshape(1, PTS), nearest.reshape(1, PTS), offsets),
        scratch=(
            pltpu.VMEM((PTS, 2 * C), BF),
            line,
            line,
            line,
            pltpu.VMEM((3, PTS), BF),
            pltpu.VMEM((GY, 2 * CAP + KINDS, C), BF),
            pltpu.SemaphoreType.DMA((6,)),
            pltpu.SemaphoreType.DMA((4,)),
        ),
        hbm=6,
        mib=60,
        out=HBM,
    )
    got = exchange(sent)
    mlp_grad = call(mlp_kernel, sds((C, C), F32), (features, cotangent, mlp_weight))
    got, mlp_grad = lax.optimization_barrier((got, mlp_grad))
    cells = sds((VX, VY, Z, C), BF)
    voxels, near, far, divisor, meta = call(
        voxel_kernel,
        (cells, FACE, FACE, sds((CELLS, C), F32), sds((KINDS, SLOTS), F32)),
        (spot, got),
        smem=1,
    )
    near, far = swap(near), chips(far)
    faces = (near, far) + edges(spot, near, voxels, far)
    matrix, grad_out = call(
        spread_kernel, (sds((CELLS, SLOTS), BF), sds((CELLS, C), F32)), (got, meta)
    )
    wide = pltpu.VMEM((VX + 2, VY + 2, Z, 3 * C), BF)
    block = sds((GY, ROWS, C), BF)
    rows = sds((GY, CAP, C), BF)
    keep, send, act, grad_hidden, near, far = call(
        conv_kernel,
        (sds((HALF, C, C), F32), sds((HALF, C, C), BF), sds((CELLS, C), BF), cells, FACE, FACE),
        (spot, voxels) + faces + (conv_weight, grad_out, mlp_grad),
        scratch=(wide, pltpu.VMEM((2 * HALF, C, C), F32)),
        smem=1,
    )
    arrived = swap(send)
    filled = call(sample_kernel, rows, (matrix, act))
    joined = call(join_kernel, block, (keep, arrived, filled))
    first = exchange(joined)
    near, far = swap(near), chips(far)
    grad_faces = (near, far) + edges(spot, near, grad_hidden, far)
    first, grad_faces = lax.optimization_barrier((first, grad_faces))
    filled = call(
        back_kernel,
        rows,
        (spot, grad_hidden) + grad_faces + (conv_weight, meta, divisor),
        scratch=(wide,),
        smem=1,
    )
    share = call(share_kernel, sds((SHARE, C), BF), (first,), mib=4)
    pair = call(pair_kernel, sds((SHARE, C), F32), (share, across(share, (1, 0, 3, 2))), mib=1)
    joined = call(deal_kernel, block, (pair, across(pair, (3, 2, 1, 0)), filled))
    second = exchange(joined)
    output, position, back = call(
        forward_kernel,
        (sds((PTS, C), BF), sds((PTS, C), jnp.int32), sds((PTS, C), F32)),
        (first, slab, features, cotangent, mlp_weight),
    )
    second, back = lax.optimization_barrier((second, back))
    mine = call(take_kernel, sds((HALF, C, C), BF), (second,), mib=4)
    other = swap(mine)
    grad_features = call(backward_kernel, sds((PTS, C), BF), (second, position, back))
    grad_conv, grad_mlp = call(
        weights_kernel, (sds((27, C, C), F32), sds((C, C), F32)), (spot, mine, other), smem=1
    )
    return (output, grad_features, grad_conv, grad_mlp)


def solution(mesh):
    fine = Mesh(mesh.devices.reshape(4, 2, 4, 8), ("y", "c", "x", "z"))
    rows = ("y", "c", "x", "z")
    in_specs = (P(rows, None), P(rows, None), P(rows), P(rows), P(None, rows), P(), P(), P(rows, None))
    out_specs = (P(rows, None), P(rows, None), P(), P())
    return jax.shard_map(body, mesh=fine, in_specs=in_specs, out_specs=out_specs, check_vma=False)
```

```python
import math

import jax
import jax.numpy as jnp
from jax import lax
from jax.experimental import pallas as pl
from jax.experimental.pallas import tpu as pltpu
from jax.sharding import Mesh, PartitionSpec as P

C = 128
VX = 4
VY = 8
Z = 16
CELLS = VX * VY * Z
PTS = 512
CAP = 48
GY = 32
SLOTS = GY * CAP
GX = 8
KINDS = 8
HALF = 14
SHARE = HALF * C // GY
ROWS = CAP + SHARE
BF = jnp.bfloat16
F32 = jnp.float32
VMEM = pl.BlockSpec(memory_space=pltpu.VMEM)
SMEM = pl.BlockSpec(memory_space=pltpu.SMEM)
HBM = pl.BlockSpec(memory_space=pltpu.HBM)
LEFT = (((0,), (0,)), ((), ()))
RIGHT = (((1,), (1,)), ((), ()))


def sds(shape, dtype):
    return jax.ShapeDtypeStruct(shape, dtype)


def call(kernel, out_shape, args, scratch=(), smem=0, hbm=0, mib=12, out=VMEM):
    return pl.pallas_call(
        kernel,
        out_shape=out_shape,
        in_specs=[SMEM] * smem + [HBM] * hbm + [VMEM] * (len(args) - smem - hbm),
        out_specs=jax.tree.map(lambda _: out, out_shape),
        scratch_shapes=list(scratch),
        compiler_params=pltpu.CompilerParams(vmem_limit_bytes=mib * 1024 * 1024),
    )(*args)


def iota(shape, dim):
    return lax.broadcasted_iota(jnp.int32, shape, dim)


def dot(a, b, dims=(((1,), (0,)), ((), ()))):
    return lax.dot_general(a, b, dims, preferred_element_type=F32)


def onehot(mask):
    return jnp.where(mask, 1.0, 0.0).astype(BF)


def sigmoid(v):
    return 1.0 / (1.0 + jnp.exp(-v))


def places(slab):
    named = iota((GY, PTS), 0) == slab
    earlier = onehot(iota((PTS, PTS), 0) < iota((PTS, PTS), 1))
    before = dot(onehot(named), earlier)
    rank = jnp.sum(jnp.where(named, before, 0.0), axis=0, keepdims=True)
    return slab * CAP + rank.astype(jnp.int32)


def pack_kernel(feat_hbm, cot_hbm, slab_hbm, base_hbm, near_hbm, off_hbm, sent_hbm,
                both_ref, slab_ref, base_ref, near_ref, off_ref, sent_ref, sems, out_sems):
    moves = [
        pltpu.make_async_copy(slab_hbm, slab_ref, sems.at[0]),
        pltpu.make_async_copy(base_hbm, base_ref, sems.at[1]),
        pltpu.make_async_copy(near_hbm, near_ref, sems.at[2]),
        pltpu.make_async_copy(off_hbm, off_ref, sems.at[3]),
        pltpu.make_async_copy(feat_hbm, both_ref.at[:, 0:C], sems.at[4]),
        pltpu.make_async_copy(cot_hbm, both_ref.at[:, C : 2 * C], sems.at[5]),
    ]
    for move in moves:
        move.start()
    for move in moves[:4]:
        move.wait()
    position = places(slab_ref[...])
    base = base_ref[...]
    near = near_ref[...]
    a = base // (VY * Z)
    b = base // Z % VY
    c = base % Z
    fraction = off_ref[...].astype(F32)
    rows = [a + 2, b, c, near]
    meta = jnp.concatenate(
        [r.astype(F32) for r in rows] + [fraction, jnp.zeros((KINDS - 7, PTS), F32)], axis=0
    ).astype(BF)
    moves[4].wait()
    moves[5].wait()
    both = both_ref[...]
    group = 8
    sends = []
    for g in range(GY // group):
        span = group * CAP
        chosen = onehot(iota((span, PTS), 0) + g * span == position)
        packed = dot(chosen, both).astype(BF).reshape(group, CAP, 2 * C)
        here = pl.ds(g * group, group)
        sent_ref[here, 0:CAP, :] = packed[:, :, :C]
        sent_ref[here, CAP : 2 * CAP, :] = packed[:, :, C:]
        lanes = dot(meta, chosen, RIGHT)
        for i in range(group):
            piece = lanes[:, i * CAP : (i + 1) * CAP]
            wide = jnp.concatenate([piece, jnp.zeros((KINDS, C - CAP), F32)], axis=1)
            sent_ref[g * group + i, 2 * CAP : 2 * CAP + KINDS, :] = wide.astype(BF)
        sends.append(pltpu.make_async_copy(sent_ref.at[here], sent_hbm.at[here], out_sems.at[g]))
        sends[g].start()
    for send in sends:
        send.wait()


def slope(v, s):
    return s * (1.0 + v * (1.0 - s))


def mlp_kernel(feat_ref, cot_ref, mlp_ref, grad_ref):
    feat = feat_ref[...]
    pre = dot(feat, mlp_ref[...])
    grad_pre = (cot_ref[...].astype(F32) * slope(pre, sigmoid(pre))).astype(BF)
    grad_ref[...] = dot(grad_pre, feat, LEFT)


def arrived_meta(got_ref):
    return jnp.concatenate(
        [got_ref[t, 2 * CAP : 2 * CAP + KINDS, :].astype(F32)[:, :CAP] for t in range(GY)], axis=1
    )


def own_matrix(meta):
    near = meta[3:4].astype(jnp.int32)
    base = (meta[0:1] - 2.0) * (VY * Z) + meta[1:2] * Z + meta[2:3]
    own = base.astype(jnp.int32) + near // 4 * (VY * Z) + near // 2 % 2 * Z + near % 2
    return onehot(iota((CELLS, SLOTS), 0) == own)


def voxel_kernel(spot_ref, got_ref, vox_ref, near_ref, far_ref, div_ref, meta_ref):
    meta = arrived_meta(got_ref)
    meta_ref[...] = meta
    own_hot = own_matrix(meta)
    rows = got_ref[:, 0:CAP, :].reshape(SLOTS, C)
    both = jnp.concatenate([rows, jnp.ones((SLOTS, C), BF)], axis=1)
    total = dot(own_hot, both)
    divisor = jnp.maximum(total[:, C:], 1.0)
    div_ref[...] = divisor
    vox_ref[...] = (total[:, :C] / divisor).astype(BF).reshape(VX, VY, Z, C)
    core = spot_ref[0] % 2
    near_ref[...] = vox_ref[pl.ds((VX - 1) * (1 - core), 1)]
    far_ref[...] = vox_ref[pl.ds((VX - 1) * core, 1)]


def spread_kernel(got_ref, meta_ref, matrix_ref, grad_ref):
    meta = meta_ref[...]
    a, b, c = meta[0:1] - 2.0, meta[1:2], meta[2:3]
    fx, fy, fz = meta[4:5], meta[5:6], meta[6:7]

    def side(distance, fraction):
        return jnp.where(distance == 0.0, 1.0 - fraction, jnp.where(distance == 1.0, fraction, 0.0))

    plane = VY * Z
    place = iota((plane, SLOTS), 0)
    wy = side((place // Z).astype(F32) - b, fy)
    wz = side((place % Z).astype(F32) - c, fz)
    for x in range(VX):
        wx = side(x - a, fx)
        matrix_ref[x * plane : (x + 1) * plane, :] = ((wx * wy) * wz).astype(BF)
    cots = got_ref[:, CAP : 2 * CAP, :].reshape(SLOTS, C)
    grad_ref[...] = dot(matrix_ref[...], cots)


def flag(spot_ref, bit):
    return (spot_ref[0] // 2**bit % 2).astype(F32).astype(BF)


def edge_kernel(spot_ref, near_ref, own_ref, far_ref, even_ref, odd_ref):
    core = spot_ref[0] % 2
    turn = spot_ref[0] // 4 % 2
    inside = flag(spot_ref, 1)
    for ref, y in ((even_ref, (VY - 1) * (1 - turn)), (odd_ref, (VY - 1) * turn)):
        row = pl.ds(y, 1)
        ref[pl.ds((VX + 1) * (1 - core), 1)] = near_ref[:, row]
        ref[1 : VX + 1] = own_ref[:, row]
        ref[pl.ds((VX + 1) * core, 1)] = far_ref[:, row] * inside


def placer(spot_ref, wide_ref):
    def put(x, y, block, inside=None):
        nx, ny = block.shape[0], block.shape[1]
        if inside is not None:
            block = block * flag(spot_ref, inside)
        flat = block.reshape(nx * ny * Z, C).astype(F32)
        z = iota(flat.shape, 0) % Z
        blank = jnp.zeros((8, C), F32)
        down = jnp.concatenate([blank, flat], axis=0)[7 : 7 + flat.shape[0]]
        up = jnp.concatenate([flat, blank], axis=0)[1 : 1 + flat.shape[0]]
        down = jnp.where(z == 0, 0.0, down)
        up = jnp.where(z == Z - 1, 0.0, up)
        shape = (nx, ny, Z, C)
        planes, rows = pl.ds(x, nx), pl.ds(y, ny)
        wide_ref[planes, rows, :, 0:C] = down.astype(BF).reshape(shape)
        wide_ref[planes, rows, :, C : 2 * C] = block
        wide_ref[planes, rows, :, 2 * C :] = up.astype(BF).reshape(shape)

    return put


def assemble(spot_ref, wide_ref, own_ref, near_ref, far_ref):
    core = spot_ref[0] % 2
    put = placer(spot_ref, wide_ref)
    put(1, 1, own_ref[...])
    put((VX + 1) * (1 - core), 1, near_ref[...])
    put((VX + 1) * core, 1, far_ref[...], 1)


def add_rows(spot_ref, wide_ref, even_ref, odd_ref):
    turn = spot_ref[0] // 4 % 2
    put = placer(spot_ref, wide_ref)
    put(0, (VY + 1) * (1 - turn), even_ref[...])
    put(0, (VY + 1) * turn, odd_ref[...], 3)


def window(wide_ref, x, y):
    return wide_ref[x : x + VX, y : y + VY, :, :].reshape(CELLS, 3 * C)


def taps(weight_ref, k):
    return weight_ref[3 * k : 3 * k + 3].reshape(3 * C, C)


def inner_kernel(spot_ref, vox_ref, near_ref, far_ref, weight_ref, wide_ref, hidden_ref):
    assemble(spot_ref, wide_ref, vox_ref, near_ref, far_ref)
    blank = jnp.zeros((VX + 2, 1, Z, 3 * C), BF)
    wide_ref[:, 0:1] = blank
    wide_ref[:, VY + 1 :] = blank
    hidden = jnp.zeros((CELLS, C), F32)
    for k in range(9):
        hidden = hidden + dot(window(wide_ref, k // 3, k % 3), taps(weight_ref, k))
    hidden_ref[...] = hidden.reshape(VX, VY, Z, C)


def half_blocks(half, wide_ref, turned, mlp_ref, out_ref):
    def part(k):
        return dot(turned, wide_ref[pl.ds(k // 3, VX), pl.ds(k % 3, VY)].reshape(CELLS, 3 * C)).astype(out_ref.dtype)

    for i in range(4):
        blocks = part(5 * half + i)
        for j in range(3):
            out_ref[3 * i + half + j] = blocks[:, j * C : (j + 1) * C]
    blocks = part(4)

    @pl.when(half == 0)
    def _():
        out_ref[12] = blocks[:, 0:C]
        out_ref[13] = blocks[:, C : 2 * C]

    @pl.when(half == 1)
    def _():
        out_ref[0] = blocks[:, 2 * C :]
        out_ref[13] = mlp_ref[...].astype(out_ref.dtype)


def conv_kernel(spot_ref, inner_ref, hidden_ref, even_ref, odd_ref, weight_ref, gout_ref, mlp_ref,
                send_ref, wide_ref, turned_ref, act_ref, hid_ref, in_ref, out_ref, sum_ref):
    wide_ref[...] = inner_ref[...]
    add_rows(spot_ref, wide_ref, even_ref, odd_ref)
    sum_ref[...] = hidden_ref[...]
    for y, at, dy in ((0, 0, 0), (VY - 1, VY + 1, 2)):
        more = jnp.zeros((VX * Z, C), F32)
        for dx in range(3):
            row = wide_ref[dx : dx + VX, at].reshape(VX * Z, 3 * C)
            more = more + dot(row, taps(weight_ref, 3 * dx + dy))
        sum_ref[:, y] += more.reshape(VX, Z, C)
    hidden = sum_ref[...].reshape(CELLS, C)
    s = sigmoid(hidden)
    act_ref[...] = (hidden * s).astype(BF)
    grad_hidden = (gout_ref[...] * slope(hidden, s)).astype(BF)
    core = spot_ref[0] % 2
    hid_ref[...] = grad_hidden.reshape(VX, VY, Z, C)
    in_ref[...] = hid_ref[pl.ds((VX - 1) * (1 - core), 1)]
    out_ref[...] = hid_ref[pl.ds((VX - 1) * core, 1)]
    turned = grad_hidden.astype(F32).T.astype(BF)
    turned_ref[...] = turned
    half_blocks(1 - core, wide_ref, turned, mlp_ref, send_ref)


def keep_kernel(spot_ref, wide_ref, turned_ref, mlp_ref, keep_ref):
    half_blocks(spot_ref[0] % 2, wide_ref, turned_ref[...], mlp_ref, keep_ref)


def sample_kernel(matrix_ref, act_ref, out_ref):
    out_ref[...] = dot(matrix_ref[...], act_ref[...], LEFT).astype(BF).reshape(GY, CAP, C)


def join_kernel(keep_ref, got_ref, filled_ref, out_ref):
    total = keep_ref[...] + got_ref[...].astype(F32)
    out_ref[:, CAP:, :] = total.reshape(GY, SHARE, C).astype(BF)
    out_ref[:, 0:CAP, :] = filled_ref[...]


def share_kernel(got_ref, out_ref):
    out_ref[...] = jnp.sum(got_ref[:, CAP:, :].astype(F32), axis=0).astype(BF)


def back_kernel(spot_ref, hid_ref, near_ref, far_ref, even_ref, odd_ref, weight_ref, meta_ref, div_ref, out_ref, wide_ref):
    assemble(spot_ref, wide_ref, hid_ref, near_ref, far_ref)
    add_rows(spot_ref, wide_ref, even_ref, odd_ref)
    total = jnp.zeros((CELLS, C), F32)
    for k in range(9):
        taps = jnp.concatenate([weight_ref[3 * k + 2 - j] for j in range(3)], axis=1)
        total = total + dot(window(wide_ref, 2 - k // 3, 2 - k % 3), taps, RIGHT)
    mean = (total / div_ref[...]).astype(BF)
    out_ref[...] = dot(own_matrix(meta_ref[...]), mean, LEFT).astype(BF).reshape(GY, CAP, C)


def deal_kernel(spot_ref, own_ref, one_ref, two_ref, three_ref, filled_ref, out_ref, part_ref):
    y = spot_ref[0] // 16
    for k, ref in enumerate((own_ref, one_ref, two_ref, three_ref)):
        part_ref[y ^ k] = ref[...].astype(F32)
    total = jnp.sum(part_ref[...], axis=0).astype(BF)
    out_ref[:, CAP:, :] = jnp.broadcast_to(total[None], (GY, SHARE, C))
    out_ref[:, 0:CAP, :] = filled_ref[...]


def unpack(pos, got_ref):
    rows = got_ref[:, 0:CAP, :].reshape(SLOTS, C)
    chosen = jnp.concatenate(
        [onehot(iota((PTS, C), 1) + i * C == pos) for i in range(SLOTS // C)], axis=1
    )
    return dot(chosen, rows)


def forward_kernel(got_ref, slab_ref, feat_ref, cot_ref, mlp_ref, out_ref, pos_ref, back_ref):
    spread = jnp.broadcast_to(places(slab_ref[...]).astype(F32), (C, PTS))
    pos = spread.T.astype(jnp.int32)
    pos_ref[...] = pos
    weight = mlp_ref[...]
    pre = dot(feat_ref[...], weight)
    s = sigmoid(pre)
    grad_pre = (cot_ref[...].astype(F32) * slope(pre, s)).astype(BF)
    back_ref[...] = dot(grad_pre, weight, RIGHT)
    sampled = unpack(pos, got_ref).astype(BF).astype(F32)
    out_ref[...] = (sampled + pre * s).astype(BF)


def take_kernel(got_ref, out_ref):
    out_ref[...] = got_ref[:, CAP:, :].astype(F32).reshape(HALF, C, C).astype(BF)


def backward_kernel(got_ref, pos_ref, back_ref, out_ref):
    out_ref[...] = (unpack(pos_ref[...], got_ref) + back_ref[...]).astype(BF)


def weights_kernel(spot_ref, mine_ref, other_ref, conv_ref, mlp_ref):
    def fill(first_ref, second_ref):
        for o in range(27):
            half = first_ref[o] if o < HALF else second_ref[o - HALF]
            conv_ref[o] = half.astype(F32).T * (1.0 / math.sqrt(GX * GY * CELLS))
        mlp_ref[...] = second_ref[HALF - 1].astype(F32).T * (1.0 / math.sqrt(GX * GY * PTS))

    @pl.when(spot_ref[0] % 2 == 0)
    def _():
        fill(mine_ref, other_ref)

    @pl.when(spot_ref[0] % 2 == 1)
    def _():
        fill(other_ref, mine_ref)


FACE = sds((1, VY, Z, C), BF)
EDGE = sds((VX + 2, 1, Z, C), BF)


def pairs(count, start):
    swaps = [(i, (i + 1) % count) for i in range(start, count, 2)]
    return swaps + [(j, i) for i, j in swaps]


def chips(face):
    return lax.ppermute(face, ("y", "c"), pairs(GX, 1))


def edges(spot, near, cells, far):
    even, odd = call(edge_kernel, (EDGE, EDGE), (spot, near, cells, far), smem=1, mib=2)
    odds = [(s * GY + i, s * GY + j) for s in range(GX) for i, j in pairs(GY, 1) if abs(i - j) == 1]
    ends = [(s * GY + i, (s ^ 1) * GY + i) for s in range(GX) for i in (0, GY - 1)]
    return (
        lax.ppermute(even, ("x", "z"), pairs(GY, 0)),
        lax.ppermute(odd, ("y", "c", "x", "z"), odds + ends),
    )


def exchange(rows):
    return lax.all_to_all(rows, ("x", "z"), split_axis=0, concat_axis=0, tiled=True)


def across(share, partner):
    return lax.ppermute(share, "y", list(enumerate(partner)))


def swap(half):
    return lax.ppermute(half, "c", [(0, 1), (1, 0)])


def body(features, point_slab, base_cell, nearest, offsets, conv_weight, mlp_weight, cotangent):
    strip = lax.axis_index(("y", "c"))
    slab_here = lax.axis_index(("x", "z"))
    core = lax.axis_index("c")
    core = core + 16 * (strip // 2) + 2 * (strip % (GX - 1) != 0) + 4 * (slab_here % 2) + 8 * (slab_here % (GY - 1) != 0)
    spot = core.reshape(1)
    point_slab, spot = lax.optimization_barrier((point_slab, spot))
    slab = point_slab.reshape(1, PTS)
    line = pltpu.VMEM((1, PTS), jnp.int32)
    sent = call(
        pack_kernel,
        sds((GY, 2 * CAP + KINDS, C), BF),
        (features, cotangent, slab, base_cell.reshape(1, PTS), nearest.reshape(1, PTS), offsets),
        scratch=(
            pltpu.VMEM((PTS, 2 * C), BF),
            line,
            line,
            line,
            pltpu.VMEM((3, PTS), BF),
            pltpu.VMEM((GY, 2 * CAP + KINDS, C), BF),
            pltpu.SemaphoreType.DMA((6,)),
            pltpu.SemaphoreType.DMA((4,)),
        ),
        hbm=6,
        mib=60,
        out=HBM,
    )
    got = exchange(sent)
    mlp_grad = call(mlp_kernel, sds((C, C), F32), (features, cotangent, mlp_weight))
    got, mlp_grad = lax.optimization_barrier((got, mlp_grad))
    cells = sds((VX, VY, Z, C), BF)
    voxels, near, far, divisor, meta = call(
        voxel_kernel,
        (cells, FACE, FACE, sds((CELLS, C), F32), sds((KINDS, SLOTS), F32)),
        (spot, got),
        smem=1,
    )
    near, far = swap(near), chips(far)
    even, odd = edges(spot, near, voxels, far)
    spread = sds((VX + 2, VY + 2, Z, 3 * C), BF)
    inner, hidden = call(
        inner_kernel,
        (spread, sds((VX, VY, Z, C), F32)),
        (spot, voxels, near, far, conv_weight),
        smem=1,
    )
    matrix, grad_out = call(
        spread_kernel, (sds((CELLS, SLOTS), BF), sds((CELLS, C), F32)), (got, meta)
    )
    wide = pltpu.VMEM((VX + 2, VY + 2, Z, 3 * C), BF)
    block = sds((GY, ROWS, C), BF)
    rows = sds((GY, CAP, C), BF)
    half = sds((HALF, C, C), BF)
    send, full, turned, act, grad_hidden, near, far = call(
        conv_kernel,
        (half, spread, sds((C, CELLS), BF), sds((CELLS, C), BF), cells, FACE, FACE),
        (spot, inner, hidden, even, odd, conv_weight, grad_out, mlp_grad),
        scratch=(pltpu.VMEM((VX, VY, Z, C), F32),),
        smem=1,
    )
    arrived = swap(send)
    keep = call(keep_kernel, sds((HALF, C, C), F32), (spot, full, turned, mlp_grad), smem=1)
    filled = call(sample_kernel, rows, (matrix, act))
    joined = call(join_kernel, block, (keep, arrived, filled))
    first = exchange(joined)
    near, far = swap(near), chips(far)
    grad_faces = (near, far) + edges(spot, near, grad_hidden, far)
    first, grad_faces = lax.optimization_barrier((first, grad_faces))
    filled = call(
        back_kernel,
        rows,
        (spot, grad_hidden) + grad_faces + (conv_weight, meta, divisor),
        scratch=(wide,),
        smem=1,
    )
    share = call(share_kernel, sds((SHARE, C), BF), (first,), mib=4)
    others = tuple(across(share, [y ^ k for y in range(4)]) for k in (1, 2, 3))
    joined = call(
        deal_kernel,
        block,
        (spot, share) + others + (filled,),
        scratch=(pltpu.VMEM((4, SHARE, C), F32),),
        smem=1,
    )
    second = exchange(joined)
    output, position, back = call(
        forward_kernel,
        (sds((PTS, C), BF), sds((PTS, C), jnp.int32), sds((PTS, C), F32)),
        (first, slab, features, cotangent, mlp_weight),
    )
    second, back = lax.optimization_barrier((second, back))
    mine = call(take_kernel, sds((HALF, C, C), BF), (second,), mib=4)
    other = swap(mine)
    grad_features = call(backward_kernel, sds((PTS, C), BF), (second, position, back))
    grad_conv, grad_mlp = call(
        weights_kernel, (sds((27, C, C), F32), sds((C, C), F32)), (spot, mine, other), smem=1
    )
    return (output, grad_features, grad_conv, grad_mlp)


def solution(mesh):
    fine = Mesh(mesh.devices.reshape(4, 2, 4, 8), ("y", "c", "x", "z"))
    rows = ("y", "c", "x", "z")
    in_specs = (P(rows, None), P(rows, None), P(rows), P(rows), P(None, rows), P(), P(), P(rows, None))
    out_specs = (P(rows, None), P(rows, None), P(), P())
    return jax.shard_map(body, mesh=fine, in_specs=in_specs, out_specs=out_specs, check_vma=False)
```

```python
import math

import jax
import jax.numpy as jnp
from jax import lax
from jax.experimental import pallas as pl
from jax.experimental.pallas import tpu as pltpu
from jax.sharding import Mesh, PartitionSpec as P

C = 128
VX = 4
VY = 8
Z = 16
CELLS = VX * VY * Z
PTS = 512
CAP = 48
GY = 32
SLOTS = GY * CAP
GX = 8
KINDS = 8
HALF = 14
SHARE = HALF * C // GY
ROWS = CAP + SHARE
BF = jnp.bfloat16
F32 = jnp.float32
VMEM = pl.BlockSpec(memory_space=pltpu.VMEM)
SMEM = pl.BlockSpec(memory_space=pltpu.SMEM)
HBM = pl.BlockSpec(memory_space=pltpu.HBM)
LEFT = (((0,), (0,)), ((), ()))
RIGHT = (((1,), (1,)), ((), ()))


def sds(shape, dtype):
    return jax.ShapeDtypeStruct(shape, dtype)


def call(kernel, out_shape, args, scratch=(), smem=0, hbm=0, mib=12, out=VMEM):
    return pl.pallas_call(
        kernel,
        out_shape=out_shape,
        in_specs=[SMEM] * smem + [HBM] * hbm + [VMEM] * (len(args) - smem - hbm),
        out_specs=jax.tree.map(lambda _: out, out_shape),
        scratch_shapes=list(scratch),
        compiler_params=pltpu.CompilerParams(vmem_limit_bytes=mib * 1024 * 1024),
    )(*args)


def iota(shape, dim):
    return lax.broadcasted_iota(jnp.int32, shape, dim)


def dot(a, b, dims=(((1,), (0,)), ((), ()))):
    return lax.dot_general(a, b, dims, preferred_element_type=F32)


def onehot(mask):
    return jnp.where(mask, 1.0, 0.0).astype(BF)


def sigmoid(v):
    return 1.0 / (1.0 + jnp.exp(-v))


def places(slab):
    named = iota((GY, PTS), 0) == slab
    earlier = onehot(iota((PTS, PTS), 0) < iota((PTS, PTS), 1))
    before = dot(onehot(named), earlier)
    rank = jnp.sum(jnp.where(named, before, 0.0), axis=0, keepdims=True)
    return slab * CAP + rank.astype(jnp.int32)


def pack_kernel(feat_hbm, cot_hbm, slab_hbm, base_hbm, near_hbm, off_hbm, sent_hbm,
                feat_ref, cot_ref, slab_ref, base_ref, near_ref, off_ref, sent_ref, sems, out_sems):
    moves = [
        pltpu.make_async_copy(slab_hbm, slab_ref, sems.at[0]),
        pltpu.make_async_copy(base_hbm, base_ref, sems.at[1]),
        pltpu.make_async_copy(near_hbm, near_ref, sems.at[2]),
        pltpu.make_async_copy(off_hbm, off_ref, sems.at[3]),
        pltpu.make_async_copy(feat_hbm, feat_ref, sems.at[4]),
        pltpu.make_async_copy(cot_hbm, cot_ref, sems.at[5]),
    ]
    for move in moves:
        move.start()
    for move in moves[:4]:
        move.wait()
    position = places(slab_ref[...])
    base = base_ref[...]
    near = near_ref[...]
    a = base // (VY * Z)
    b = base // Z % VY
    c = base % Z
    fraction = off_ref[...].astype(F32)
    rows = [a + 2, b, c, near]
    meta = jnp.concatenate(
        [r.astype(F32) for r in rows] + [fraction, jnp.zeros((KINDS - 7, PTS), F32)], axis=0
    ).astype(BF)
    moves[4].wait()
    moves[5].wait()
    both = jnp.concatenate([feat_ref[...], cot_ref[...]], axis=1)
    group = 4
    sends = []
    for g in range(GY // group):
        span = group * CAP
        chosen = onehot(iota((span, PTS), 0) + g * span == position)
        packed = dot(chosen, both).astype(BF).reshape(group, CAP, 2 * C)
        here = pl.ds(g * group, group)
        sent_ref[here, 0:CAP, :] = packed[:, :, :C]
        sent_ref[here, CAP : 2 * CAP, :] = packed[:, :, C:]
        lanes = dot(meta, chosen, RIGHT)
        for i in range(group):
            piece = lanes[:, i * CAP : (i + 1) * CAP]
            wide = jnp.concatenate([piece, jnp.zeros((KINDS, C - CAP), F32)], axis=1)
            sent_ref[g * group + i, 2 * CAP : 2 * CAP + KINDS, :] = wide.astype(BF)
        sends.append(pltpu.make_async_copy(sent_ref.at[here], sent_hbm.at[here], out_sems.at[g]))
        sends[g].start()
    for send in sends:
        send.wait()


def slope(v, s):
    return s * (1.0 + v * (1.0 - s))


def mlp_kernel(feat_ref, cot_ref, mlp_ref, grad_ref):
    feat = feat_ref[...]
    pre = dot(feat, mlp_ref[...])
    grad_pre = (cot_ref[...].astype(F32) * slope(pre, sigmoid(pre))).astype(BF)
    grad_ref[...] = dot(grad_pre, feat, LEFT)


def arrived_meta(got_ref):
    return jnp.concatenate(
        [got_ref[t, 2 * CAP : 2 * CAP + KINDS, :].astype(F32)[:, :CAP] for t in range(GY)], axis=1
    )


def own_matrix(meta):
    near = meta[3:4].astype(jnp.int32)
    base = (meta[0:1] - 2.0) * (VY * Z) + meta[1:2] * Z + meta[2:3]
    own = base.astype(jnp.int32) + near // 4 * (VY * Z) + near // 2 % 2 * Z + near % 2
    return onehot(iota((CELLS, SLOTS), 0) == own)


def voxel_kernel(spot_ref, got_ref, vox_ref, near_ref, far_ref, div_ref, meta_ref):
    meta = arrived_meta(got_ref)
    meta_ref[...] = meta
    own_hot = own_matrix(meta)
    rows = got_ref[:, 0:CAP, :].reshape(SLOTS, C)
    both = jnp.concatenate([rows, jnp.ones((SLOTS, C), BF)], axis=1)
    total = dot(own_hot, both)
    divisor = jnp.maximum(total[:, C:], 1.0)
    div_ref[...] = divisor
    vox_ref[...] = (total[:, :C] / divisor).astype(BF).reshape(VX, VY, Z, C)
    core = spot_ref[0] % 2
    near_ref[...] = vox_ref[pl.ds((VX - 1) * (1 - core), 1)]
    far_ref[...] = vox_ref[pl.ds((VX - 1) * core, 1)]


def spread_kernel(got_ref, meta_ref, matrix_ref, grad_ref):
    meta = meta_ref[...]
    a, b, c = meta[0:1] - 2.0, meta[1:2], meta[2:3]
    fx, fy, fz = meta[4:5], meta[5:6], meta[6:7]

    def side(distance, fraction):
        return jnp.where(distance == 0.0, 1.0 - fraction, jnp.where(distance == 1.0, fraction, 0.0))

    plane = VY * Z
    place = iota((plane, SLOTS), 0)
    wy = side((place // Z).astype(F32) - b, fy)
    wz = side((place % Z).astype(F32) - c, fz)
    for x in range(VX):
        wx = side(x - a, fx)
        matrix_ref[x * plane : (x + 1) * plane, :] = ((wx * wy) * wz).astype(BF)
    cots = got_ref[:, CAP : 2 * CAP, :].reshape(SLOTS, C)
    grad_ref[...] = dot(matrix_ref[...], cots)


def flag(spot_ref, bit):
    return (spot_ref[0] // 2**bit % 2).astype(F32).astype(BF)


def edge_kernel(spot_ref, near_ref, own_ref, far_ref, even_ref, odd_ref):
    core = spot_ref[0] % 2
    turn = spot_ref[0] // 4 % 2
    inside = flag(spot_ref, 1)
    for ref, y in ((even_ref, (VY - 1) * (1 - turn)), (odd_ref, (VY - 1) * turn)):
        row = pl.ds(y, 1)
        ref[pl.ds((VX + 1) * (1 - core), 1)] = near_ref[:, row]
        ref[1 : VX + 1] = own_ref[:, row]
        ref[pl.ds((VX + 1) * core, 1)] = far_ref[:, row] * inside


def placer(spot_ref, wide_ref):
    def put(x, y, block, inside=None):
        nx, ny = block.shape[0], block.shape[1]
        if inside is not None:
            block = block * flag(spot_ref, inside)
        flat = block.reshape(nx * ny * Z, C).astype(F32)
        z = iota(flat.shape, 0) % Z
        blank = jnp.zeros((8, C), F32)
        down = jnp.concatenate([blank, flat], axis=0)[7 : 7 + flat.shape[0]]
        up = jnp.concatenate([flat, blank], axis=0)[1 : 1 + flat.shape[0]]
        down = jnp.where(z == 0, 0.0, down)
        up = jnp.where(z == Z - 1, 0.0, up)
        shape = (nx, ny, Z, C)
        planes, rows = pl.ds(x, nx), pl.ds(y, ny)
        wide_ref[planes, rows, :, 0:C] = down.astype(BF).reshape(shape)
        wide_ref[planes, rows, :, C : 2 * C] = block
        wide_ref[planes, rows, :, 2 * C :] = up.astype(BF).reshape(shape)

    return put


def assemble(spot_ref, wide_ref, own_ref, near_ref, far_ref):
    core = spot_ref[0] % 2
    put = placer(spot_ref, wide_ref)
    put(1, 1, own_ref[...])
    put((VX + 1) * (1 - core), 1, near_ref[...])
    put((VX + 1) * core, 1, far_ref[...], 1)


def add_rows(spot_ref, wide_ref, even_ref, odd_ref):
    turn = spot_ref[0] // 4 % 2
    put = placer(spot_ref, wide_ref)
    put(0, (VY + 1) * (1 - turn), even_ref[...])
    put(0, (VY + 1) * turn, odd_ref[...], 3)


def window(wide_ref, x, y):
    return wide_ref[x : x + VX, y : y + VY, :, :].reshape(CELLS, 3 * C)


def taps(weight_ref, k):
    return weight_ref[3 * k : 3 * k + 3].reshape(3 * C, C)


def inner_kernel(spot_ref, vox_ref, near_ref, far_ref, weight_ref, wide_ref, hidden_ref):
    assemble(spot_ref, wide_ref, vox_ref, near_ref, far_ref)
    blank = jnp.zeros((VX + 2, 1, Z, 3 * C), BF)
    wide_ref[:, 0:1] = blank
    wide_ref[:, VY + 1 :] = blank
    hidden = jnp.zeros((CELLS, C), F32)
    for k in range(9):
        hidden = hidden + dot(window(wide_ref, k // 3, k % 3), taps(weight_ref, k))
    hidden_ref[...] = hidden.reshape(VX, VY, Z, C)


def half_blocks(half, wide_ref, turned, mlp_ref, out_ref):
    def part(k):
        return dot(turned, wide_ref[pl.ds(k // 3, VX), pl.ds(k % 3, VY)].reshape(CELLS, 3 * C)).astype(out_ref.dtype)

    for i in range(4):
        blocks = part(5 * half + i)
        for j in range(3):
            out_ref[3 * i + half + j] = blocks[:, j * C : (j + 1) * C]
    blocks = part(4)

    @pl.when(half == 0)
    def _():
        out_ref[12] = blocks[:, 0:C]
        out_ref[13] = blocks[:, C : 2 * C]

    @pl.when(half == 1)
    def _():
        out_ref[0] = blocks[:, 2 * C :]
        out_ref[13] = mlp_ref[...].astype(out_ref.dtype)


def conv_kernel(spot_ref, inner_ref, hidden_ref, even_ref, odd_ref, weight_ref, gout_ref, mlp_ref,
                send_ref, wide_ref, turned_ref, act_ref, hid_ref, in_ref, out_ref, sum_ref):
    wide_ref[...] = inner_ref[...]
    add_rows(spot_ref, wide_ref, even_ref, odd_ref)
    sum_ref[...] = hidden_ref[...]
    for y, at, dy in ((0, 0, 0), (VY - 1, VY + 1, 2)):
        more = jnp.zeros((VX * Z, C), F32)
        for dx in range(3):
            row = wide_ref[dx : dx + VX, at].reshape(VX * Z, 3 * C)
            more = more + dot(row, taps(weight_ref, 3 * dx + dy))
        sum_ref[:, y] += more.reshape(VX, Z, C)
    hidden = sum_ref[...].reshape(CELLS, C)
    s = sigmoid(hidden)
    act_ref[...] = (hidden * s).astype(BF)
    grad_hidden = (gout_ref[...] * slope(hidden, s)).astype(BF)
    core = spot_ref[0] % 2
    hid_ref[...] = grad_hidden.reshape(VX, VY, Z, C)
    in_ref[...] = hid_ref[pl.ds((VX - 1) * (1 - core), 1)]
    out_ref[...] = hid_ref[pl.ds((VX - 1) * core, 1)]
    turned = grad_hidden.astype(F32).T.astype(BF)
    turned_ref[...] = turned
    half_blocks(1 - core, wide_ref, turned, mlp_ref, send_ref)


def keep_kernel(spot_ref, wide_ref, turned_ref, mlp_ref, keep_ref):
    half_blocks(spot_ref[0] % 2, wide_ref, turned_ref[...], mlp_ref, keep_ref)


def sample_kernel(matrix_ref, act_ref, out_ref):
    out_ref[...] = dot(matrix_ref[...], act_ref[...], LEFT).astype(BF).reshape(GY, CAP, C)


def join_kernel(keep_ref, got_ref, filled_ref, out_ref):
    total = keep_ref[...] + got_ref[...].astype(F32)
    out_ref[:, CAP:, :] = total.reshape(GY, SHARE, C).astype(BF)
    out_ref[:, 0:CAP, :] = filled_ref[...]


def share_kernel(got_ref, out_ref):
    out_ref[...] = jnp.sum(got_ref[:, CAP:, :].astype(F32), axis=0).astype(BF)


def back_kernel(spot_ref, hid_ref, near_ref, far_ref, even_ref, odd_ref, weight_ref, meta_ref, div_ref, out_ref, wide_ref):
    assemble(spot_ref, wide_ref, hid_ref, near_ref, far_ref)
    add_rows(spot_ref, wide_ref, even_ref, odd_ref)
    total = jnp.zeros((CELLS, C), F32)
    for k in range(9):
        taps = jnp.concatenate([weight_ref[3 * k + 2 - j] for j in range(3)], axis=1)
        total = total + dot(window(wide_ref, 2 - k // 3, 2 - k % 3), taps, RIGHT)
    mean = (total / div_ref[...]).astype(BF)
    out_ref[...] = dot(own_matrix(meta_ref[...]), mean, LEFT).astype(BF).reshape(GY, CAP, C)


def deal_kernel(spot_ref, own_ref, one_ref, two_ref, three_ref, filled_ref, out_ref, part_ref):
    y = spot_ref[0] // 16
    for k, ref in enumerate((own_ref, one_ref, two_ref, three_ref)):
        part_ref[y ^ k] = ref[...].astype(F32)
    total = jnp.sum(part_ref[...], axis=0).astype(BF)
    out_ref[:, CAP:, :] = jnp.broadcast_to(total[None], (GY, SHARE, C))
    out_ref[:, 0:CAP, :] = filled_ref[...]


def unpack(pos, got_ref):
    rows = got_ref[:, 0:CAP, :].reshape(SLOTS, C)
    chosen = jnp.concatenate(
        [onehot(iota((PTS, C), 1) + i * C == pos) for i in range(SLOTS // C)], axis=1
    )
    return dot(chosen, rows)


def forward_kernel(got_ref, slab_ref, feat_ref, cot_ref, mlp_ref, out_ref, pos_ref, back_ref):
    spread = jnp.broadcast_to(places(slab_ref[...]).astype(F32), (C, PTS))
    pos = spread.T.astype(jnp.int32)
    pos_ref[...] = pos
    weight = mlp_ref[...]
    pre = dot(feat_ref[...], weight)
    s = sigmoid(pre)
    grad_pre = (cot_ref[...].astype(F32) * slope(pre, s)).astype(BF)
    back_ref[...] = dot(grad_pre, weight, RIGHT)
    sampled = unpack(pos, got_ref).astype(BF).astype(F32)
    out_ref[...] = (sampled + pre * s).astype(BF)


def take_kernel(got_ref, out_ref):
    out_ref[...] = got_ref[:, CAP:, :].astype(F32).reshape(HALF, C, C).astype(BF)


def backward_kernel(got_ref, pos_ref, back_ref, out_ref):
    out_ref[...] = (unpack(pos_ref[...], got_ref) + back_ref[...]).astype(BF)


def weights_kernel(spot_ref, mine_ref, other_ref, conv_ref, mlp_ref):
    def fill(first_ref, second_ref):
        for o in range(27):
            half = first_ref[o] if o < HALF else second_ref[o - HALF]
            conv_ref[o] = half.astype(F32).T * (1.0 / math.sqrt(GX * GY * CELLS))
        mlp_ref[...] = second_ref[HALF - 1].astype(F32).T * (1.0 / math.sqrt(GX * GY * PTS))

    @pl.when(spot_ref[0] % 2 == 0)
    def _():
        fill(mine_ref, other_ref)

    @pl.when(spot_ref[0] % 2 == 1)
    def _():
        fill(other_ref, mine_ref)


FACE = sds((1, VY, Z, C), BF)
EDGE = sds((VX + 2, 1, Z, C), BF)


def pairs(count, start):
    swaps = [(i, (i + 1) % count) for i in range(start, count, 2)]
    return swaps + [(j, i) for i, j in swaps]


def chips(face):
    return lax.ppermute(face, ("y", "c"), pairs(GX, 1))


def edges(spot, near, cells, far):
    even, odd = call(edge_kernel, (EDGE, EDGE), (spot, near, cells, far), smem=1, mib=2)
    odds = [(s * GY + i, s * GY + j) for s in range(GX) for i, j in pairs(GY, 1) if abs(i - j) == 1]
    ends = [(s * GY + i, (s ^ 1) * GY + i) for s in range(GX) for i in (0, GY - 1)]
    return (
        lax.ppermute(even, ("x", "z"), pairs(GY, 0)),
        lax.ppermute(odd, ("y", "c", "x", "z"), odds + ends),
    )


def exchange(rows):
    return lax.all_to_all(rows, ("x", "z"), split_axis=0, concat_axis=0, tiled=True)


def across(share, partner):
    return lax.ppermute(share, "y", list(enumerate(partner)))


def swap(half):
    return lax.ppermute(half, "c", [(0, 1), (1, 0)])


def body(features, point_slab, base_cell, nearest, offsets, conv_weight, mlp_weight, cotangent):
    strip = lax.axis_index(("y", "c"))
    slab_here = lax.axis_index(("x", "z"))
    core = lax.axis_index("c")
    core = core + 16 * (strip // 2) + 2 * (strip % (GX - 1) != 0) + 4 * (slab_here % 2) + 8 * (slab_here % (GY - 1) != 0)
    spot = core.reshape(1)
    point_slab, spot = lax.optimization_barrier((point_slab, spot))
    slab = point_slab.reshape(1, PTS)
    line = pltpu.VMEM((1, PTS), jnp.int32)
    sent = call(
        pack_kernel,
        sds((GY, 2 * CAP + KINDS, C), BF),
        (features, cotangent, slab, base_cell.reshape(1, PTS), nearest.reshape(1, PTS), offsets),
        scratch=(
            pltpu.VMEM((PTS, C), BF),
            pltpu.VMEM((PTS, C), BF),
            line,
            line,
            line,
            pltpu.VMEM((3, PTS), BF),
            pltpu.VMEM((GY, 2 * CAP + KINDS, C), BF),
            pltpu.SemaphoreType.DMA((6,)),
            pltpu.SemaphoreType.DMA((8,)),
        ),
        hbm=6,
        mib=60,
        out=HBM,
    )
    got = exchange(sent)
    mlp_grad = call(mlp_kernel, sds((C, C), F32), (features, cotangent, mlp_weight))
    got, mlp_grad = lax.optimization_barrier((got, mlp_grad))
    cells = sds((VX, VY, Z, C), BF)
    voxels, near, far, divisor, meta = call(
        voxel_kernel,
        (cells, FACE, FACE, sds((CELLS, C), F32), sds((KINDS, SLOTS), F32)),
        (spot, got),
        smem=1,
    )
    near, far = swap(near), chips(far)
    even, odd = edges(spot, near, voxels, far)
    spread = sds((VX + 2, VY + 2, Z, 3 * C), BF)
    inner, hidden = call(
        inner_kernel,
        (spread, sds((VX, VY, Z, C), F32)),
        (spot, voxels, near, far, conv_weight),
        smem=1,
    )
    matrix, grad_out = call(
        spread_kernel, (sds((CELLS, SLOTS), BF), sds((CELLS, C), F32)), (got, meta)
    )
    wide = pltpu.VMEM((VX + 2, VY + 2, Z, 3 * C), BF)
    block = sds((GY, ROWS, C), BF)
    rows = sds((GY, CAP, C), BF)
    half = sds((HALF, C, C), BF)
    send, full, turned, act, grad_hidden, near, far = call(
        conv_kernel,
        (half, spread, sds((C, CELLS), BF), sds((CELLS, C), BF), cells, FACE, FACE),
        (spot, inner, hidden, even, odd, conv_weight, grad_out, mlp_grad),
        scratch=(pltpu.VMEM((VX, VY, Z, C), F32),),
        smem=1,
    )
    arrived = swap(send)
    keep = call(keep_kernel, sds((HALF, C, C), F32), (spot, full, turned, mlp_grad), smem=1)
    filled = call(sample_kernel, rows, (matrix, act))
    joined = call(join_kernel, block, (keep, arrived, filled))
    first = exchange(joined)
    near, far = swap(near), chips(far)
    grad_faces = (near, far) + edges(spot, near, grad_hidden, far)
    first, grad_faces = lax.optimization_barrier((first, grad_faces))
    filled = call(
        back_kernel,
        rows,
        (spot, grad_hidden) + grad_faces + (conv_weight, meta, divisor),
        scratch=(wide,),
        smem=1,
    )
    share = call(share_kernel, sds((SHARE, C), BF), (first,), mib=4)
    others = tuple(across(share, [y ^ k for y in range(4)]) for k in (1, 2, 3))
    joined = call(
        deal_kernel,
        block,
        (spot, share) + others + (filled,),
        scratch=(pltpu.VMEM((4, SHARE, C), F32),),
        smem=1,
    )
    second = exchange(joined)
    output, position, back = call(
        forward_kernel,
        (sds((PTS, C), BF), sds((PTS, C), jnp.int32), sds((PTS, C), F32)),
        (first, slab, features, cotangent, mlp_weight),
    )
    second, back = lax.optimization_barrier((second, back))
    mine = call(take_kernel, sds((HALF, C, C), BF), (second,), mib=4)
    other = swap(mine)
    grad_features = call(backward_kernel, sds((PTS, C), BF), (second, position, back))
    grad_conv, grad_mlp = call(
        weights_kernel, (sds((27, C, C), F32), sds((C, C), F32)), (spot, mine, other), smem=1
    )
    return (output, grad_features, grad_conv, grad_mlp)


def solution(mesh):
    fine = Mesh(mesh.devices.reshape(4, 2, 4, 8), ("y", "c", "x", "z"))
    rows = ("y", "c", "x", "z")
    in_specs = (P(rows, None), P(rows, None), P(rows), P(rows), P(None, rows), P(), P(), P(rows, None))
    out_specs = (P(rows, None), P(rows, None), P(), P())
    return jax.shard_map(body, mesh=fine, in_specs=in_specs, out_specs=out_specs, check_vma=False)
```

```python
import math

import jax
import jax.numpy as jnp
from jax import lax
from jax.experimental import pallas as pl
from jax.experimental.pallas import tpu as pltpu
from jax.sharding import Mesh, PartitionSpec as P

C = 128
VX = 4
VY = 8
Z = 16
CELLS = VX * VY * Z
PTS = 512
CAP = 48
GY = 32
SLOTS = GY * CAP
GX = 8
KINDS = 8
HALF = 14
SHARE = HALF * C // GY
ROWS = CAP + SHARE
BF = jnp.bfloat16
F32 = jnp.float32
VMEM = pl.BlockSpec(memory_space=pltpu.VMEM)
SMEM = pl.BlockSpec(memory_space=pltpu.SMEM)
HBM = pl.BlockSpec(memory_space=pltpu.HBM)
LEFT = (((0,), (0,)), ((), ()))
RIGHT = (((1,), (1,)), ((), ()))


def sds(shape, dtype):
    return jax.ShapeDtypeStruct(shape, dtype)


def call(kernel, out_shape, args, scratch=(), smem=0, hbm=0, mib=12, out=VMEM):
    return pl.pallas_call(
        kernel,
        out_shape=out_shape,
        in_specs=[SMEM] * smem + [HBM] * hbm + [VMEM] * (len(args) - smem - hbm),
        out_specs=jax.tree.map(lambda _: out, out_shape),
        scratch_shapes=list(scratch),
        compiler_params=pltpu.CompilerParams(vmem_limit_bytes=mib * 1024 * 1024),
    )(*args)


def iota(shape, dim):
    return lax.broadcasted_iota(jnp.int32, shape, dim)


def dot(a, b, dims=(((1,), (0,)), ((), ()))):
    return lax.dot_general(a, b, dims, preferred_element_type=F32)


def onehot(mask):
    return jnp.where(mask, 1.0, 0.0).astype(BF)


def sigmoid(v):
    return 1.0 / (1.0 + jnp.exp(-v))


def places(slab):
    named = iota((GY, PTS), 0) == slab
    earlier = onehot(iota((PTS, PTS), 0) < iota((PTS, PTS), 1))
    before = dot(onehot(named), earlier)
    rank = jnp.sum(jnp.where(named, before, 0.0), axis=0, keepdims=True)
    return slab * CAP + rank.astype(jnp.int32)


def pack_kernel(feat_hbm, cot_hbm, slab_hbm, base_hbm, near_hbm, off_hbm, sent_hbm,
                feat_ref, cot_ref, slab_ref, base_ref, near_ref, off_ref, sent_ref, sems, out_sems):
    moves = [
        pltpu.make_async_copy(slab_hbm, slab_ref, sems.at[0]),
        pltpu.make_async_copy(base_hbm, base_ref, sems.at[1]),
        pltpu.make_async_copy(near_hbm, near_ref, sems.at[2]),
        pltpu.make_async_copy(off_hbm, off_ref, sems.at[3]),
        pltpu.make_async_copy(feat_hbm, feat_ref, sems.at[4]),
        pltpu.make_async_copy(cot_hbm, cot_ref, sems.at[5]),
    ]
    for move in moves:
        move.start()
    for move in moves[:4]:
        move.wait()
    position = places(slab_ref[...])
    base = base_ref[...]
    near = near_ref[...]
    a = base // (VY * Z)
    b = base // Z % VY
    c = base % Z
    fraction = off_ref[...].astype(F32)
    rows = [a + 2, b, c, near]
    meta = jnp.concatenate(
        [r.astype(F32) for r in rows] + [fraction, jnp.zeros((KINDS - 7, PTS), F32)], axis=0
    ).astype(BF)
    moves[4].wait()
    moves[5].wait()
    both = jnp.concatenate([feat_ref[...], cot_ref[...]], axis=1)
    group = 4
    sends = []
    for g in range(GY // group):
        span = group * CAP
        chosen = onehot(iota((span, PTS), 0) + g * span == position)
        packed = dot(chosen, both).astype(BF).reshape(group, CAP, 2 * C)
        here = pl.ds(g * group, group)
        sent_ref[here, 0:CAP, :] = packed[:, :, :C]
        sent_ref[here, CAP : 2 * CAP, :] = packed[:, :, C:]
        lanes = dot(meta, chosen, RIGHT)
        for i in range(group):
            piece = lanes[:, i * CAP : (i + 1) * CAP]
            wide = jnp.concatenate([piece, jnp.zeros((KINDS, C - CAP), F32)], axis=1)
            sent_ref[g * group + i, 2 * CAP : 2 * CAP + KINDS, :] = wide.astype(BF)
        sends.append(pltpu.make_async_copy(sent_ref.at[here], sent_hbm.at[here], out_sems.at[g]))
        sends[g].start()
    for send in sends:
        send.wait()


def slope(v, s):
    return s * (1.0 + v * (1.0 - s))


def mlp_kernel(feat_ref, cot_ref, mlp_ref, grad_ref):
    feat = feat_ref[...]
    pre = dot(feat, mlp_ref[...])
    grad_pre = (cot_ref[...].astype(F32) * slope(pre, sigmoid(pre))).astype(BF)
    grad_ref[...] = dot(grad_pre, feat, LEFT)


def arrived_meta(got_ref):
    return jnp.concatenate(
        [got_ref[t, 2 * CAP : 2 * CAP + KINDS, :].astype(F32)[:, :CAP] for t in range(GY)], axis=1
    )


def own_matrix(meta):
    near = meta[3:4].astype(jnp.int32)
    base = (meta[0:1] - 2.0) * (VY * Z) + meta[1:2] * Z + meta[2:3]
    own = base.astype(jnp.int32) + near // 4 * (VY * Z) + near // 2 % 2 * Z + near % 2
    return onehot(iota((CELLS, SLOTS), 0) == own)


def voxel_kernel(spot_ref, got_ref, vox_ref, near_ref, far_ref, div_ref, meta_ref):
    meta = arrived_meta(got_ref)
    meta_ref[...] = meta
    own_hot = own_matrix(meta)
    rows = got_ref[:, 0:CAP, :].reshape(SLOTS, C)
    both = jnp.concatenate([rows, jnp.ones((SLOTS, C), BF)], axis=1)
    total = dot(own_hot, both)
    divisor = jnp.maximum(total[:, C:], 1.0)
    div_ref[...] = divisor
    vox_ref[...] = (total[:, :C] / divisor).astype(BF).reshape(VX, VY, Z, C)
    core = spot_ref[0] % 2
    near_ref[...] = vox_ref[pl.ds((VX - 1) * (1 - core), 1)]
    far_ref[...] = vox_ref[pl.ds((VX - 1) * core, 1)]


def spread_kernel(got_ref, meta_ref, matrix_ref, grad_ref):
    meta = meta_ref[...]
    a, b, c = meta[0:1] - 2.0, meta[1:2], meta[2:3]
    fx, fy, fz = meta[4:5], meta[5:6], meta[6:7]

    def side(distance, fraction):
        return jnp.where(distance == 0.0, 1.0 - fraction, jnp.where(distance == 1.0, fraction, 0.0))

    plane = VY * Z
    place = iota((plane, SLOTS), 0)
    wy = side((place // Z).astype(F32) - b, fy)
    wz = side((place % Z).astype(F32) - c, fz)
    for x in range(VX):
        wx = side(x - a, fx)
        matrix_ref[x * plane : (x + 1) * plane, :] = ((wx * wy) * wz).astype(BF)
    cots = got_ref[:, CAP : 2 * CAP, :].reshape(SLOTS, C)
    grad_ref[...] = dot(matrix_ref[...], cots)


def flag(spot_ref, bit):
    return (spot_ref[0] // 2**bit % 2).astype(F32).astype(BF)


def edge_kernel(spot_ref, near_ref, own_ref, far_ref, even_ref, odd_ref):
    core = spot_ref[0] % 2
    turn = spot_ref[0] // 4 % 2
    inside = flag(spot_ref, 1)
    for ref, y in ((even_ref, (VY - 1) * (1 - turn)), (odd_ref, (VY - 1) * turn)):
        row = pl.ds(y, 1)
        ref[pl.ds((VX + 1) * (1 - core), 1)] = near_ref[:, row]
        ref[1 : VX + 1] = own_ref[:, row]
        ref[pl.ds((VX + 1) * core, 1)] = far_ref[:, row] * inside


def placer(spot_ref, wide_ref):
    def put(x, y, block, inside=None):
        nx, ny = block.shape[0], block.shape[1]
        if inside is not None:
            block = block * flag(spot_ref, inside)
        flat = block.reshape(nx * ny * Z, C).astype(F32)
        z = iota(flat.shape, 0) % Z
        blank = jnp.zeros((8, C), F32)
        down = jnp.concatenate([blank, flat], axis=0)[7 : 7 + flat.shape[0]]
        up = jnp.concatenate([flat, blank], axis=0)[1 : 1 + flat.shape[0]]
        down = jnp.where(z == 0, 0.0, down)
        up = jnp.where(z == Z - 1, 0.0, up)
        shape = (nx, ny, Z, C)
        planes, rows = pl.ds(x, nx), pl.ds(y, ny)
        wide_ref[planes, rows, :, 0:C] = down.astype(BF).reshape(shape)
        wide_ref[planes, rows, :, C : 2 * C] = block
        wide_ref[planes, rows, :, 2 * C :] = up.astype(BF).reshape(shape)

    return put


def assemble(spot_ref, wide_ref, own_ref, near_ref, far_ref):
    core = spot_ref[0] % 2
    put = placer(spot_ref, wide_ref)
    put(1, 1, own_ref[...])
    put((VX + 1) * (1 - core), 1, near_ref[...])
    put((VX + 1) * core, 1, far_ref[...], 1)


def add_rows(spot_ref, wide_ref, even_ref, odd_ref):
    turn = spot_ref[0] // 4 % 2
    put = placer(spot_ref, wide_ref)
    put(0, (VY + 1) * (1 - turn), even_ref[...])
    put(0, (VY + 1) * turn, odd_ref[...], 3)


def window(wide_ref, x, y):
    return wide_ref[x : x + VX, y : y + VY, :, :].reshape(CELLS, 3 * C)


def taps(weight_ref, k):
    return weight_ref[3 * k : 3 * k + 3].reshape(3 * C, C)


def inner_kernel(spot_ref, vox_ref, near_ref, far_ref, weight_ref, wide_ref, hidden_ref):
    assemble(spot_ref, wide_ref, vox_ref, near_ref, far_ref)
    blank = jnp.zeros((VX + 2, 1, Z, 3 * C), BF)
    wide_ref[:, 0:1] = blank
    wide_ref[:, VY + 1 :] = blank
    hidden = jnp.zeros((CELLS, C), F32)
    for k in range(9):
        hidden = hidden + dot(window(wide_ref, k // 3, k % 3), taps(weight_ref, k))
    hidden_ref[...] = hidden.reshape(VX, VY, Z, C)


def half_blocks(half, wide_ref, turned, mlp_ref, out_ref):
    def part(k):
        return dot(turned, wide_ref[pl.ds(k // 3, VX), pl.ds(k % 3, VY)].reshape(CELLS, 3 * C)).astype(out_ref.dtype)

    for i in range(4):
        blocks = part(5 * half + i)
        for j in range(3):
            out_ref[3 * i + half + j] = blocks[:, j * C : (j + 1) * C]
    blocks = part(4)

    @pl.when(half == 0)
    def _():
        out_ref[12] = blocks[:, 0:C]
        out_ref[13] = blocks[:, C : 2 * C]

    @pl.when(half == 1)
    def _():
        out_ref[0] = blocks[:, 2 * C :]
        out_ref[13] = mlp_ref[...].astype(out_ref.dtype)


def conv_kernel(spot_ref, inner_ref, hidden_ref, even_ref, odd_ref, weight_ref, gout_ref, mlp_ref,
                send_ref, wide_ref, turned_ref, act_ref, hid_ref, in_ref, out_ref, sum_ref):
    wide_ref[...] = inner_ref[...]
    add_rows(spot_ref, wide_ref, even_ref, odd_ref)
    sum_ref[...] = hidden_ref[...]
    for y, at, dy in ((0, 0, 0), (VY - 1, VY + 1, 2)):
        more = jnp.zeros((VX * Z, C), F32)
        for dx in range(3):
            row = wide_ref[dx : dx + VX, at].reshape(VX * Z, 3 * C)
            more = more + dot(row, taps(weight_ref, 3 * dx + dy))
        sum_ref[:, y] += more.reshape(VX, Z, C)
    hidden = sum_ref[...].reshape(CELLS, C)
    s = sigmoid(hidden)
    act_ref[...] = (hidden * s).astype(BF)
    grad_hidden = (gout_ref[...] * slope(hidden, s)).astype(BF)
    core = spot_ref[0] % 2
    hid_ref[...] = grad_hidden.reshape(VX, VY, Z, C)
    in_ref[...] = hid_ref[pl.ds((VX - 1) * (1 - core), 1)]
    out_ref[...] = hid_ref[pl.ds((VX - 1) * core, 1)]
    turned = grad_hidden.astype(F32).T.astype(BF)
    turned_ref[...] = turned
    half_blocks(1 - core, wide_ref, turned, mlp_ref, send_ref)


def keep_kernel(spot_ref, wide_ref, turned_ref, mlp_ref, keep_ref):
    half_blocks(spot_ref[0] % 2, wide_ref, turned_ref[...], mlp_ref, keep_ref)


def sample_kernel(matrix_ref, act_ref, out_ref):
    out_ref[...] = dot(matrix_ref[...], act_ref[...], LEFT).astype(BF).reshape(GY, CAP, C)


def join_kernel(keep_ref, got_ref, filled_ref, out_ref):
    total = keep_ref[...] + got_ref[...].astype(F32)
    out_ref[:, CAP:, :] = total.reshape(GY, SHARE, C).astype(BF)
    out_ref[:, 0:CAP, :] = filled_ref[...]


def share_kernel(got_ref, out_ref):
    out_ref[...] = jnp.sum(got_ref[:, CAP:, :].astype(F32), axis=0).astype(BF)


def back_kernel(spot_ref, hid_ref, near_ref, far_ref, even_ref, odd_ref, weight_ref, meta_ref, div_ref, out_ref, wide_ref):
    assemble(spot_ref, wide_ref, hid_ref, near_ref, far_ref)
    add_rows(spot_ref, wide_ref, even_ref, odd_ref)
    total = jnp.zeros((CELLS, C), F32)
    for k in range(9):
        taps = jnp.concatenate([weight_ref[3 * k + 2 - j] for j in range(3)], axis=1)
        total = total + dot(window(wide_ref, 2 - k // 3, 2 - k % 3), taps, RIGHT)
    mean = (total / div_ref[...]).astype(BF)
    out_ref[...] = dot(own_matrix(meta_ref[...]), mean, LEFT).astype(BF).reshape(GY, CAP, C)


def deal_kernel(spot_ref, own_ref, one_ref, two_ref, three_ref, filled_ref, out_ref, part_ref):
    y = spot_ref[0] // 16
    for k, ref in enumerate((own_ref, one_ref, two_ref, three_ref)):
        part_ref[y ^ k] = ref[...].astype(F32)
    total = jnp.sum(part_ref[...], axis=0).astype(BF)
    out_ref[:, CAP:, :] = jnp.broadcast_to(total[None], (GY, SHARE, C))
    out_ref[:, 0:CAP, :] = filled_ref[...]


def unpack(pos, got_ref):
    rows = got_ref[:, 0:CAP, :].reshape(SLOTS, C)
    chosen = jnp.concatenate(
        [onehot(iota((PTS, C), 1) + i * C == pos) for i in range(SLOTS // C)], axis=1
    )
    return dot(chosen, rows)


def forward_kernel(got_ref, slab_ref, feat_ref, cot_ref, mlp_ref, out_ref, pos_ref, back_ref):
    spread = jnp.broadcast_to(places(slab_ref[...]).astype(F32), (C, PTS))
    pos = spread.T.astype(jnp.int32)
    pos_ref[...] = pos
    weight = mlp_ref[...]
    pre = dot(feat_ref[...], weight)
    s = sigmoid(pre)
    grad_pre = (cot_ref[...].astype(F32) * slope(pre, s)).astype(BF)
    back_ref[...] = dot(grad_pre, weight, RIGHT)
    sampled = unpack(pos, got_ref).astype(BF).astype(F32)
    out_ref[...] = (sampled + pre * s).astype(BF)


def take_kernel(got_ref, out_ref):
    out_ref[...] = got_ref[:, CAP:, :].astype(F32).reshape(HALF, C, C).astype(BF)


def backward_kernel(got_ref, pos_ref, back_ref, out_ref):
    out_ref[...] = (unpack(pos_ref[...], got_ref) + back_ref[...]).astype(BF)


def weights_kernel(spot_ref, mine_ref, other_ref, conv_ref, mlp_ref):
    def fill(first_ref, second_ref):
        for o in range(27):
            half = first_ref[o] if o < HALF else second_ref[o - HALF]
            conv_ref[o] = half.astype(F32).T * (1.0 / math.sqrt(GX * GY * CELLS))
        mlp_ref[...] = second_ref[HALF - 1].astype(F32).T * (1.0 / math.sqrt(GX * GY * PTS))

    @pl.when(spot_ref[0] % 2 == 0)
    def _():
        fill(mine_ref, other_ref)

    @pl.when(spot_ref[0] % 2 == 1)
    def _():
        fill(other_ref, mine_ref)


FACE = sds((1, VY, Z, C), BF)
EDGE = sds((VX + 2, 1, Z, C), BF)


def pairs(count, start):
    swaps = [(i, (i + 1) % count) for i in range(start, count, 2)]
    return swaps + [(j, i) for i, j in swaps]


def chips(face):
    return lax.ppermute(face, ("y", "c"), pairs(GX, 1))


def edges(spot, near, cells, far):
    even, odd = call(edge_kernel, (EDGE, EDGE), (spot, near, cells, far), smem=1, mib=2)
    odds = [(s * GY + i, s * GY + j) for s in range(GX) for i, j in pairs(GY, 1) if abs(i - j) == 1]
    ends = [(s * GY + i, (s ^ 1) * GY + i) for s in range(GX) for i in (0, GY - 1)]
    return (
        lax.ppermute(even, ("x", "z"), pairs(GY, 0)),
        lax.ppermute(odd, ("y", "c", "x", "z"), odds + ends),
    )


def exchange(rows):
    return lax.all_to_all(rows, ("x", "z"), split_axis=0, concat_axis=0, tiled=True)


def across(share, partner):
    return lax.ppermute(share, "y", list(enumerate(partner)))


def swap(half):
    return lax.ppermute(half, "c", [(0, 1), (1, 0)])


def body(features, point_slab, base_cell, nearest, offsets, conv_weight, mlp_weight, cotangent):
    strip = lax.axis_index(("y", "c"))
    slab_here = lax.axis_index(("x", "z"))
    core = lax.axis_index("c")
    core = core + 16 * (strip // 2) + 2 * (strip % (GX - 1) != 0) + 4 * (slab_here % 2) + 8 * (slab_here % (GY - 1) != 0)
    spot = core.reshape(1)
    point_slab, spot = lax.optimization_barrier((point_slab, spot))
    slab = point_slab.reshape(1, PTS)
    line = pltpu.VMEM((1, PTS), jnp.int32)
    sent = call(
        pack_kernel,
        sds((GY, 2 * CAP + KINDS, C), BF),
        (features, cotangent, slab, base_cell.reshape(1, PTS), nearest.reshape(1, PTS), offsets),
        scratch=(
            pltpu.VMEM((PTS, C), BF),
            pltpu.VMEM((PTS, C), BF),
            line,
            line,
            line,
            pltpu.VMEM((3, PTS), BF),
            pltpu.VMEM((GY, 2 * CAP + KINDS, C), BF),
            pltpu.SemaphoreType.DMA((6,)),
            pltpu.SemaphoreType.DMA((8,)),
        ),
        hbm=6,
        mib=60,
        out=HBM,
    )
    got = exchange(sent)
    mlp_grad = call(mlp_kernel, sds((C, C), F32), (features, cotangent, mlp_weight))
    got, mlp_grad = lax.optimization_barrier((got, mlp_grad))
    cells = sds((VX, VY, Z, C), BF)
    voxels, near, far, divisor, meta = call(
        voxel_kernel,
        (cells, FACE, FACE, sds((CELLS, C), F32), sds((KINDS, SLOTS), F32)),
        (spot, got),
        smem=1,
    )
    near, far = swap(near), chips(far)
    matrix, grad_out = call(
        spread_kernel, (sds((CELLS, SLOTS), BF), sds((CELLS, C), F32)), (got, meta)
    )
    near, far, matrix, grad_out = lax.optimization_barrier((near, far, matrix, grad_out))
    even, odd = edges(spot, near, voxels, far)
    spread = sds((VX + 2, VY + 2, Z, 3 * C), BF)
    inner, hidden = call(
        inner_kernel,
        (spread, sds((VX, VY, Z, C), F32)),
        (spot, voxels, near, far, conv_weight),
        smem=1,
    )
    wide = pltpu.VMEM((VX + 2, VY + 2, Z, 3 * C), BF)
    block = sds((GY, ROWS, C), BF)
    rows = sds((GY, CAP, C), BF)
    half = sds((HALF, C, C), BF)
    send, full, turned, act, grad_hidden, near, far = call(
        conv_kernel,
        (half, spread, sds((C, CELLS), BF), sds((CELLS, C), BF), cells, FACE, FACE),
        (spot, inner, hidden, even, odd, conv_weight, grad_out, mlp_grad),
        scratch=(pltpu.VMEM((VX, VY, Z, C), F32),),
        smem=1,
    )
    arrived = swap(send)
    keep = call(keep_kernel, sds((HALF, C, C), F32), (spot, full, turned, mlp_grad), smem=1)
    filled = call(sample_kernel, rows, (matrix, act))
    joined = call(join_kernel, block, (keep, arrived, filled))
    first = exchange(joined)
    near, far = swap(near), chips(far)
    grad_faces = (near, far) + edges(spot, near, grad_hidden, far)
    first, grad_faces = lax.optimization_barrier((first, grad_faces))
    filled = call(
        back_kernel,
        rows,
        (spot, grad_hidden) + grad_faces + (conv_weight, meta, divisor),
        scratch=(wide,),
        smem=1,
    )
    share = call(share_kernel, sds((SHARE, C), BF), (first,), mib=4)
    others = tuple(across(share, [y ^ k for y in range(4)]) for k in (1, 2, 3))
    joined = call(
        deal_kernel,
        block,
        (spot, share) + others + (filled,),
        scratch=(pltpu.VMEM((4, SHARE, C), F32),),
        smem=1,
    )
    second = exchange(joined)
    output, position, back = call(
        forward_kernel,
        (sds((PTS, C), BF), sds((PTS, C), jnp.int32), sds((PTS, C), F32)),
        (first, slab, features, cotangent, mlp_weight),
    )
    second, back = lax.optimization_barrier((second, back))
    mine = call(take_kernel, sds((HALF, C, C), BF), (second,), mib=4)
    other = swap(mine)
    grad_features = call(backward_kernel, sds((PTS, C), BF), (second, position, back))
    grad_conv, grad_mlp = call(
        weights_kernel, (sds((27, C, C), F32), sds((C, C), F32)), (spot, mine, other), smem=1
    )
    return (output, grad_features, grad_conv, grad_mlp)


def solution(mesh):
    fine = Mesh(mesh.devices.reshape(4, 2, 4, 8), ("y", "c", "x", "z"))
    rows = ("y", "c", "x", "z")
    in_specs = (P(rows, None), P(rows, None), P(rows), P(rows), P(None, rows), P(), P(), P(rows, None))
    out_specs = (P(rows, None), P(rows, None), P(), P())
    return jax.shard_map(body, mesh=fine, in_specs=in_specs, out_specs=out_specs, check_vma=False)
```

```python
import math

import jax
import jax.numpy as jnp
from jax import lax
from jax.experimental import pallas as pl
from jax.experimental.pallas import tpu as pltpu
from jax.sharding import Mesh, PartitionSpec as P

C = 128
VX = 4
VY = 8
Z = 16
CELLS = VX * VY * Z
PTS = 512
CAP = 48
GY = 32
SLOTS = GY * CAP
GX = 8
KINDS = 8
HALF = 14
SHARE = HALF * C // GY
ROWS = CAP + SHARE
BF = jnp.bfloat16
F32 = jnp.float32
VMEM = pl.BlockSpec(memory_space=pltpu.VMEM)
SMEM = pl.BlockSpec(memory_space=pltpu.SMEM)
HBM = pl.BlockSpec(memory_space=pltpu.HBM)
LEFT = (((0,), (0,)), ((), ()))
RIGHT = (((1,), (1,)), ((), ()))


def sds(shape, dtype):
    return jax.ShapeDtypeStruct(shape, dtype)


def call(kernel, out_shape, args, scratch=(), smem=0, hbm=0, mib=12, out=VMEM):
    return pl.pallas_call(
        kernel,
        out_shape=out_shape,
        in_specs=[SMEM] * smem + [HBM] * hbm + [VMEM] * (len(args) - smem - hbm),
        out_specs=jax.tree.map(lambda _: out, out_shape),
        scratch_shapes=list(scratch),
        compiler_params=pltpu.CompilerParams(vmem_limit_bytes=mib * 1024 * 1024),
    )(*args)


def iota(shape, dim):
    return lax.broadcasted_iota(jnp.int32, shape, dim)


def dot(a, b, dims=(((1,), (0,)), ((), ()))):
    return lax.dot_general(a, b, dims, preferred_element_type=F32)


def onehot(mask):
    return jnp.where(mask, 1.0, 0.0).astype(BF)


def sigmoid(v):
    return 1.0 / (1.0 + jnp.exp(-v))


def places(slab):
    named = iota((GY, PTS), 0) == slab
    earlier = onehot(iota((PTS, PTS), 0) < iota((PTS, PTS), 1))
    before = dot(onehot(named), earlier)
    rank = jnp.sum(jnp.where(named, before, 0.0), axis=0, keepdims=True)
    return slab * CAP + rank.astype(jnp.int32)


def pack_kernel(feat_hbm, cot_hbm, slab_hbm, base_hbm, near_hbm, off_hbm, sent_hbm,
                feat_ref, cot_ref, slab_ref, base_ref, near_ref, off_ref, sent_ref, sems, out_sems):
    moves = [
        pltpu.make_async_copy(slab_hbm, slab_ref, sems.at[0]),
        pltpu.make_async_copy(base_hbm, base_ref, sems.at[1]),
        pltpu.make_async_copy(near_hbm, near_ref, sems.at[2]),
        pltpu.make_async_copy(off_hbm, off_ref, sems.at[3]),
        pltpu.make_async_copy(feat_hbm, feat_ref, sems.at[4]),
        pltpu.make_async_copy(cot_hbm, cot_ref, sems.at[5]),
    ]
    for move in moves:
        move.start()
    for move in moves[:4]:
        move.wait()
    position = places(slab_ref[...])
    base = base_ref[...]
    near = near_ref[...]
    a = base // (VY * Z)
    b = base // Z % VY
    c = base % Z
    fraction = off_ref[...].astype(F32)
    rows = [a + 2, b, c, near]
    meta = jnp.concatenate(
        [r.astype(F32) for r in rows] + [fraction, jnp.zeros((KINDS - 7, PTS), F32)], axis=0
    ).astype(BF)
    moves[4].wait()
    moves[5].wait()
    both = jnp.concatenate([feat_ref[...], cot_ref[...]], axis=1)
    group = 4
    sends = []
    for g in range(GY // group):
        span = group * CAP
        chosen = onehot(iota((span, PTS), 0) + g * span == position)
        packed = dot(chosen, both).astype(BF).reshape(group, CAP, 2 * C)
        here = pl.ds(g * group, group)
        sent_ref[here, 0:CAP, :] = packed[:, :, :C]
        sent_ref[here, CAP : 2 * CAP, :] = packed[:, :, C:]
        lanes = dot(meta, chosen, RIGHT)
        for i in range(group):
            piece = lanes[:, i * CAP : (i + 1) * CAP]
            wide = jnp.concatenate([piece, jnp.zeros((KINDS, C - CAP), F32)], axis=1)
            sent_ref[g * group + i, 2 * CAP : 2 * CAP + KINDS, :] = wide.astype(BF)
        sends.append(pltpu.make_async_copy(sent_ref.at[here], sent_hbm.at[here], out_sems.at[g]))
        sends[g].start()
    for send in sends:
        send.wait()


def slope(v, s):
    return s * (1.0 + v * (1.0 - s))


def mlp_kernel(feat_ref, cot_ref, mlp_ref, grad_ref):
    feat = feat_ref[...]
    pre = dot(feat, mlp_ref[...])
    grad_pre = (cot_ref[...].astype(F32) * slope(pre, sigmoid(pre))).astype(BF)
    grad_ref[...] = dot(grad_pre, feat, LEFT)


def arrived_meta(got_ref):
    return jnp.concatenate(
        [got_ref[t, 2 * CAP : 2 * CAP + KINDS, :].astype(F32)[:, :CAP] for t in range(GY)], axis=1
    )


def own_matrix(meta):
    near = meta[3:4].astype(jnp.int32)
    base = (meta[0:1] - 2.0) * (VY * Z) + meta[1:2] * Z + meta[2:3]
    own = base.astype(jnp.int32) + near // 4 * (VY * Z) + near // 2 % 2 * Z + near % 2
    return onehot(iota((CELLS, SLOTS), 0) == own)


def voxel_kernel(spot_ref, got_ref, vox_ref, near_ref, far_ref, div_ref, meta_ref):
    meta = arrived_meta(got_ref)
    meta_ref[...] = meta
    own_hot = own_matrix(meta)
    rows = got_ref[:, 0:CAP, :].reshape(SLOTS, C)
    both = jnp.concatenate([rows, jnp.ones((SLOTS, C), BF)], axis=1)
    total = dot(own_hot, both)
    divisor = jnp.maximum(total[:, C:], 1.0)
    div_ref[...] = divisor
    vox_ref[...] = (total[:, :C] / divisor).astype(BF).reshape(VX, VY, Z, C)
    core = spot_ref[0] % 2
    near_ref[...] = vox_ref[pl.ds((VX - 1) * (1 - core), 1)]
    far_ref[...] = vox_ref[pl.ds((VX - 1) * core, 1)]


def spread_kernel(got_ref, meta_ref, matrix_ref, grad_ref):
    meta = meta_ref[...]
    a, b, c = meta[0:1] - 2.0, meta[1:2], meta[2:3]
    fx, fy, fz = meta[4:5], meta[5:6], meta[6:7]

    def side(distance, fraction):
        return jnp.where(distance == 0.0, 1.0 - fraction, jnp.where(distance == 1.0, fraction, 0.0))

    plane = VY * Z
    place = iota((plane, SLOTS), 0)
    wy = side((place // Z).astype(F32) - b, fy)
    wz = side((place % Z).astype(F32) - c, fz)
    for x in range(VX):
        wx = side(x - a, fx)
        matrix_ref[x * plane : (x + 1) * plane, :] = ((wx * wy) * wz).astype(BF)
    cots = got_ref[:, CAP : 2 * CAP, :].reshape(SLOTS, C)
    grad_ref[...] = dot(matrix_ref[...], cots)


def flag(spot_ref, bit):
    return (spot_ref[0] // 2**bit % 2).astype(F32).astype(BF)


def edge_kernel(spot_ref, near_ref, own_ref, far_ref, even_ref, odd_ref):
    core = spot_ref[0] % 2
    turn = spot_ref[0] // 4 % 2
    inside = flag(spot_ref, 1)
    for ref, y in ((even_ref, (VY - 1) * (1 - turn)), (odd_ref, (VY - 1) * turn)):
        row = pl.ds(y, 1)
        ref[pl.ds((VX + 1) * (1 - core), 1)] = near_ref[:, row]
        ref[1 : VX + 1] = own_ref[:, row]
        ref[pl.ds((VX + 1) * core, 1)] = far_ref[:, row] * inside


def placer(spot_ref, wide_ref):
    def put(x, y, block, inside=None):
        nx, ny = block.shape[0], block.shape[1]
        if inside is not None:
            block = block * flag(spot_ref, inside)
        flat = block.reshape(nx * ny * Z, C).astype(F32)
        z = iota(flat.shape, 0) % Z
        blank = jnp.zeros((8, C), F32)
        down = jnp.concatenate([blank, flat], axis=0)[7 : 7 + flat.shape[0]]
        up = jnp.concatenate([flat, blank], axis=0)[1 : 1 + flat.shape[0]]
        down = jnp.where(z == 0, 0.0, down)
        up = jnp.where(z == Z - 1, 0.0, up)
        shape = (nx, ny, Z, C)
        planes, rows = pl.ds(x, nx), pl.ds(y, ny)
        wide_ref[planes, rows, :, 0:C] = down.astype(BF).reshape(shape)
        wide_ref[planes, rows, :, C : 2 * C] = block
        wide_ref[planes, rows, :, 2 * C :] = up.astype(BF).reshape(shape)

    return put


def assemble(spot_ref, wide_ref, own_ref, near_ref, far_ref):
    core = spot_ref[0] % 2
    put = placer(spot_ref, wide_ref)
    put(1, 1, own_ref[...])
    put((VX + 1) * (1 - core), 1, near_ref[...])
    put((VX + 1) * core, 1, far_ref[...], 1)


def add_rows(spot_ref, wide_ref, even_ref, odd_ref):
    turn = spot_ref[0] // 4 % 2
    put = placer(spot_ref, wide_ref)
    put(0, (VY + 1) * (1 - turn), even_ref[...])
    put(0, (VY + 1) * turn, odd_ref[...], 3)


def window(wide_ref, x, y):
    return wide_ref[x : x + VX, y : y + VY, :, :].reshape(CELLS, 3 * C)


def taps(weight_ref, k):
    return weight_ref[3 * k : 3 * k + 3].reshape(3 * C, C)


def inner_kernel(spot_ref, vox_ref, near_ref, far_ref, weight_ref, wide_ref, hidden_ref):
    assemble(spot_ref, wide_ref, vox_ref, near_ref, far_ref)
    blank = jnp.zeros((VX + 2, 1, Z, 3 * C), BF)
    wide_ref[:, 0:1] = blank
    wide_ref[:, VY + 1 :] = blank
    hidden = jnp.zeros((CELLS, C), F32)
    for k in range(9):
        hidden = hidden + dot(window(wide_ref, k // 3, k % 3), taps(weight_ref, k))
    hidden_ref[...] = hidden.reshape(VX, VY, Z, C)


def half_blocks(half, wide_ref, turned, mlp_ref, out_ref):
    def part(k):
        return dot(turned, wide_ref[pl.ds(k // 3, VX), pl.ds(k % 3, VY)].reshape(CELLS, 3 * C)).astype(out_ref.dtype)

    for i in range(4):
        blocks = part(5 * half + i)
        for j in range(3):
            out_ref[3 * i + half + j] = blocks[:, j * C : (j + 1) * C]
    blocks = part(4)

    @pl.when(half == 0)
    def _():
        out_ref[12] = blocks[:, 0:C]
        out_ref[13] = blocks[:, C : 2 * C]

    @pl.when(half == 1)
    def _():
        out_ref[0] = blocks[:, 2 * C :]
        out_ref[13] = mlp_ref[...].astype(out_ref.dtype)


def conv_kernel(spot_ref, inner_ref, hidden_ref, even_ref, odd_ref, weight_ref, gout_ref, mlp_ref,
                send_ref, wide_ref, turned_ref, act_ref, hid_ref, in_ref, out_ref, sum_ref):
    wide_ref[...] = inner_ref[...]
    add_rows(spot_ref, wide_ref, even_ref, odd_ref)
    sum_ref[...] = hidden_ref[...]
    for y, at, dy in ((0, 0, 0), (VY - 1, VY + 1, 2)):
        more = jnp.zeros((VX * Z, C), F32)
        for dx in range(3):
            row = wide_ref[dx : dx + VX, at].reshape(VX * Z, 3 * C)
            more = more + dot(row, taps(weight_ref, 3 * dx + dy))
        sum_ref[:, y] += more.reshape(VX, Z, C)
    hidden = sum_ref[...].reshape(CELLS, C)
    s = sigmoid(hidden)
    act_ref[...] = (hidden * s).astype(BF)
    grad_hidden = (gout_ref[...] * slope(hidden, s)).astype(BF)
    core = spot_ref[0] % 2
    hid_ref[...] = grad_hidden.reshape(VX, VY, Z, C)
    in_ref[...] = hid_ref[pl.ds((VX - 1) * (1 - core), 1)]
    out_ref[...] = hid_ref[pl.ds((VX - 1) * core, 1)]
    turned = grad_hidden.astype(F32).T.astype(BF)
    turned_ref[...] = turned
    half_blocks(1 - core, wide_ref, turned, mlp_ref, send_ref)


def keep_kernel(spot_ref, wide_ref, turned_ref, mlp_ref, keep_ref):
    half_blocks(spot_ref[0] % 2, wide_ref, turned_ref[...], mlp_ref, keep_ref)


def sample_kernel(matrix_ref, act_ref, out_ref):
    out_ref[...] = dot(matrix_ref[...], act_ref[...], LEFT).astype(BF).reshape(GY, CAP, C)


def join_kernel(keep_ref, got_ref, filled_ref, out_ref):
    total = keep_ref[...] + got_ref[...].astype(F32)
    out_ref[:, CAP:, :] = total.reshape(GY, SHARE, C).astype(BF)
    out_ref[:, 0:CAP, :] = filled_ref[...]


def share_kernel(got_ref, out_ref):
    out_ref[...] = jnp.sum(got_ref[:, CAP:, :].astype(F32), axis=0).astype(BF)


def back_kernel(spot_ref, hid_ref, near_ref, far_ref, even_ref, odd_ref, weight_ref, meta_ref, div_ref, out_ref, wide_ref):
    assemble(spot_ref, wide_ref, hid_ref, near_ref, far_ref)
    add_rows(spot_ref, wide_ref, even_ref, odd_ref)
    total = jnp.zeros((CELLS, C), F32)
    for k in range(9):
        taps = jnp.concatenate([weight_ref[3 * k + 2 - j] for j in range(3)], axis=1)
        total = total + dot(window(wide_ref, 2 - k // 3, 2 - k % 3), taps, RIGHT)
    mean = (total / div_ref[...]).astype(BF)
    out_ref[...] = dot(own_matrix(meta_ref[...]), mean, LEFT).astype(BF).reshape(GY, CAP, C)


def deal_kernel(spot_ref, own_ref, one_ref, two_ref, three_ref, filled_ref, out_ref, part_ref):
    y = spot_ref[0] // 16
    for k, ref in enumerate((own_ref, one_ref, two_ref, three_ref)):
        part_ref[y ^ k] = ref[...].astype(F32)
    total = jnp.sum(part_ref[...], axis=0).astype(BF)
    out_ref[:, CAP:, :] = jnp.broadcast_to(total[None], (GY, SHARE, C))
    out_ref[:, 0:CAP, :] = filled_ref[...]


def unpack(pos, got_ref):
    rows = got_ref[:, 0:CAP, :].reshape(SLOTS, C)
    chosen = jnp.concatenate(
        [onehot(iota((PTS, C), 1) + i * C == pos) for i in range(SLOTS // C)], axis=1
    )
    return dot(chosen, rows)


def forward_kernel(got_ref, slab_ref, feat_ref, cot_ref, mlp_ref, out_ref, pos_ref, back_ref):
    spread = jnp.broadcast_to(places(slab_ref[...]).astype(F32), (C, PTS))
    pos = spread.T.astype(jnp.int32)
    pos_ref[...] = pos
    weight = mlp_ref[...]
    pre = dot(feat_ref[...], weight)
    s = sigmoid(pre)
    grad_pre = (cot_ref[...].astype(F32) * slope(pre, s)).astype(BF)
    back_ref[...] = dot(grad_pre, weight, RIGHT)
    sampled = unpack(pos, got_ref).astype(BF).astype(F32)
    out_ref[...] = (sampled + pre * s).astype(BF)


def take_kernel(got_ref, out_ref):
    out_ref[...] = got_ref[:, CAP:, :].astype(F32).reshape(HALF, C, C).astype(BF)


def backward_kernel(got_ref, pos_ref, back_ref, out_ref):
    out_ref[...] = (unpack(pos_ref[...], got_ref) + back_ref[...]).astype(BF)


def weights_kernel(spot_ref, mine_ref, other_ref, conv_hbm, mlp_hbm, conv_ref, mlp_ref, sems):
    moves = [
        pltpu.make_async_copy(conv_ref.at[pl.ds(9 * k, 9)], conv_hbm.at[pl.ds(9 * k, 9)], sems.at[k])
        for k in range(3)
    ]
    moves.append(pltpu.make_async_copy(mlp_ref, mlp_hbm, sems.at[3]))

    def fill(first_ref, second_ref, k):
        for o in range(9 * k, 9 * k + 9):
            half = first_ref[o] if o < HALF else second_ref[o - HALF]
            conv_ref[o] = half.astype(F32).T * (1.0 / math.sqrt(GX * GY * CELLS))
        if k == 2:
            mlp_ref[...] = second_ref[HALF - 1].astype(F32).T * (1.0 / math.sqrt(GX * GY * PTS))

    for k in range(3):

        @pl.when(spot_ref[0] % 2 == 0)
        def _():
            fill(mine_ref, other_ref, k)

        @pl.when(spot_ref[0] % 2 == 1)
        def _():
            fill(other_ref, mine_ref, k)

        moves[k].start()
    moves[3].start()
    for move in moves:
        move.wait()


FACE = sds((1, VY, Z, C), BF)
EDGE = sds((VX + 2, 1, Z, C), BF)


def pairs(count, start):
    swaps = [(i, (i + 1) % count) for i in range(start, count, 2)]
    return swaps + [(j, i) for i, j in swaps]


def chips(face):
    return lax.ppermute(face, ("y", "c"), pairs(GX, 1))


def edges(spot, near, cells, far):
    even, odd = call(edge_kernel, (EDGE, EDGE), (spot, near, cells, far), smem=1, mib=2)
    odds = [(s * GY + i, s * GY + j) for s in range(GX) for i, j in pairs(GY, 1) if abs(i - j) == 1]
    ends = [(s * GY + i, (s ^ 1) * GY + i) for s in range(GX) for i in (0, GY - 1)]
    return (
        lax.ppermute(even, ("x", "z"), pairs(GY, 0)),
        lax.ppermute(odd, ("y", "c", "x", "z"), odds + ends),
    )


def exchange(rows):
    return lax.all_to_all(rows, ("x", "z"), split_axis=0, concat_axis=0, tiled=True)


def across(share, partner):
    return lax.ppermute(share, "y", list(enumerate(partner)))


def swap(half):
    return lax.ppermute(half, "c", [(0, 1), (1, 0)])


def body(features, point_slab, base_cell, nearest, offsets, conv_weight, mlp_weight, cotangent):
    strip = lax.axis_index(("y", "c"))
    slab_here = lax.axis_index(("x", "z"))
    core = lax.axis_index("c")
    core = core + 16 * (strip // 2) + 2 * (strip % (GX - 1) != 0) + 4 * (slab_here % 2) + 8 * (slab_here % (GY - 1) != 0)
    spot = core.reshape(1)
    point_slab, spot = lax.optimization_barrier((point_slab, spot))
    slab = point_slab.reshape(1, PTS)
    line = pltpu.VMEM((1, PTS), jnp.int32)
    sent = call(
        pack_kernel,
        sds((GY, 2 * CAP + KINDS, C), BF),
        (features, cotangent, slab, base_cell.reshape(1, PTS), nearest.reshape(1, PTS), offsets),
        scratch=(
            pltpu.VMEM((PTS, C), BF),
            pltpu.VMEM((PTS, C), BF),
            line,
            line,
            line,
            pltpu.VMEM((3, PTS), BF),
            pltpu.VMEM((GY, 2 * CAP + KINDS, C), BF),
            pltpu.SemaphoreType.DMA((6,)),
            pltpu.SemaphoreType.DMA((8,)),
        ),
        hbm=6,
        mib=60,
        out=HBM,
    )
    got = exchange(sent)
    mlp_grad = call(mlp_kernel, sds((C, C), F32), (features, cotangent, mlp_weight))
    got, mlp_grad = lax.optimization_barrier((got, mlp_grad))
    cells = sds((VX, VY, Z, C), BF)
    voxels, near, far, divisor, meta = call(
        voxel_kernel,
        (cells, FACE, FACE, sds((CELLS, C), F32), sds((KINDS, SLOTS), F32)),
        (spot, got),
        smem=1,
    )
    far = chips(far)
    near = swap(near)
    matrix, grad_out = call(
        spread_kernel, (sds((CELLS, SLOTS), BF), sds((CELLS, C), F32)), (got, meta)
    )
    near, far, matrix, grad_out = lax.optimization_barrier((near, far, matrix, grad_out))
    even, odd = edges(spot, near, voxels, far)
    spread = sds((VX + 2, VY + 2, Z, 3 * C), BF)
    inner, hidden = call(
        inner_kernel,
        (spread, sds((VX, VY, Z, C), F32)),
        (spot, voxels, near, far, conv_weight),
        smem=1,
    )
    wide = pltpu.VMEM((VX + 2, VY + 2, Z, 3 * C), BF)
    block = sds((GY, ROWS, C), BF)
    rows = sds((GY, CAP, C), BF)
    half = sds((HALF, C, C), BF)
    send, full, turned, act, grad_hidden, near, far = call(
        conv_kernel,
        (half, spread, sds((C, CELLS), BF), sds((CELLS, C), BF), cells, FACE, FACE),
        (spot, inner, hidden, even, odd, conv_weight, grad_out, mlp_grad),
        scratch=(pltpu.VMEM((VX, VY, Z, C), F32),),
        smem=1,
    )
    arrived = swap(send)
    keep = call(keep_kernel, sds((HALF, C, C), F32), (spot, full, turned, mlp_grad), smem=1)
    filled = call(sample_kernel, rows, (matrix, act))
    joined = call(join_kernel, block, (keep, arrived, filled))
    first = exchange(joined)
    far = chips(far)
    near = swap(near)
    grad_faces = (near, far) + edges(spot, near, grad_hidden, far)
    first, grad_faces = lax.optimization_barrier((first, grad_faces))
    filled = call(
        back_kernel,
        rows,
        (spot, grad_hidden) + grad_faces + (conv_weight, meta, divisor),
        scratch=(wide,),
        smem=1,
    )
    share = call(share_kernel, sds((SHARE, C), BF), (first,), mib=4)
    others = tuple(across(share, [y ^ k for y in range(4)]) for k in (1, 2, 3))
    joined = call(
        deal_kernel,
        block,
        (spot, share) + others + (filled,),
        scratch=(pltpu.VMEM((4, SHARE, C), F32),),
        smem=1,
    )
    second = exchange(joined)
    output, position, back = call(
        forward_kernel,
        (sds((PTS, C), BF), sds((PTS, C), jnp.int32), sds((PTS, C), F32)),
        (first, slab, features, cotangent, mlp_weight),
    )
    second, back = lax.optimization_barrier((second, back))
    mine = call(take_kernel, sds((HALF, C, C), BF), (second,), mib=4)
    other = swap(mine)
    grad_features = call(backward_kernel, sds((PTS, C), BF), (second, position, back))
    grad_conv, grad_mlp = call(
        weights_kernel,
        (sds((27, C, C), F32), sds((C, C), F32)),
        (spot, mine, other),
        scratch=(
            pltpu.VMEM((27, C, C), F32),
            pltpu.VMEM((C, C), F32),
            pltpu.SemaphoreType.DMA((4,)),
        ),
        smem=1,
        out=HBM,
    )
    return (output, grad_features, grad_conv, grad_mlp)


def solution(mesh):
    fine = Mesh(mesh.devices.reshape(4, 2, 4, 8), ("y", "c", "x", "z"))
    rows = ("y", "c", "x", "z")
    in_specs = (P(rows, None), P(rows, None), P(rows), P(rows), P(None, rows), P(), P(), P(rows, None))
    out_specs = (P(rows, None), P(rows, None), P(), P())
    return jax.shard_map(body, mesh=fine, in_specs=in_specs, out_specs=out_specs, check_vma=False)
```

```python
import math

import jax
import jax.numpy as jnp
from jax import lax
from jax.experimental import pallas as pl
from jax.experimental.pallas import tpu as pltpu
from jax.sharding import Mesh, PartitionSpec as P

C = 128
VX = 4
VY = 8
Z = 16
CELLS = VX * VY * Z
PTS = 512
CAP = 48
GY = 32
SLOTS = GY * CAP
GX = 8
KINDS = 8
HALF = 14
SHARE = HALF * C // GY
ROWS = CAP + SHARE
BF = jnp.bfloat16
F32 = jnp.float32
VMEM = pl.BlockSpec(memory_space=pltpu.VMEM)
SMEM = pl.BlockSpec(memory_space=pltpu.SMEM)
HBM = pl.BlockSpec(memory_space=pltpu.HBM)
LEFT = (((0,), (0,)), ((), ()))
RIGHT = (((1,), (1,)), ((), ()))


def sds(shape, dtype):
    return jax.ShapeDtypeStruct(shape, dtype)


def call(kernel, out_shape, args, scratch=(), smem=0, hbm=0, mib=12, out=VMEM):
    return pl.pallas_call(
        kernel,
        out_shape=out_shape,
        in_specs=[SMEM] * smem + [HBM] * hbm + [VMEM] * (len(args) - smem - hbm),
        out_specs=jax.tree.map(lambda _: out, out_shape),
        scratch_shapes=list(scratch),
        compiler_params=pltpu.CompilerParams(vmem_limit_bytes=mib * 1024 * 1024),
    )(*args)


def iota(shape, dim):
    return lax.broadcasted_iota(jnp.int32, shape, dim)


def dot(a, b, dims=(((1,), (0,)), ((), ()))):
    return lax.dot_general(a, b, dims, preferred_element_type=F32)


def onehot(mask):
    return jnp.where(mask, 1.0, 0.0).astype(BF)


def sigmoid(v):
    return 1.0 / (1.0 + jnp.exp(-v))


def places(slab):
    named = iota((GY, PTS), 0) == slab
    earlier = onehot(iota((PTS, PTS), 0) < iota((PTS, PTS), 1))
    before = dot(onehot(named), earlier)
    rank = jnp.sum(jnp.where(named, before, 0.0), axis=0, keepdims=True)
    return slab * CAP + rank.astype(jnp.int32)


def pack_kernel(feat_hbm, cot_hbm, slab_hbm, base_hbm, near_hbm, off_hbm, sent_hbm,
                feat_ref, cot_ref, slab_ref, base_ref, near_ref, off_ref, sent_ref, sems, out_sems):
    moves = [
        pltpu.make_async_copy(slab_hbm, slab_ref, sems.at[0]),
        pltpu.make_async_copy(base_hbm, base_ref, sems.at[1]),
        pltpu.make_async_copy(near_hbm, near_ref, sems.at[2]),
        pltpu.make_async_copy(off_hbm, off_ref, sems.at[3]),
        pltpu.make_async_copy(feat_hbm, feat_ref, sems.at[4]),
        pltpu.make_async_copy(cot_hbm, cot_ref, sems.at[5]),
    ]
    for move in moves:
        move.start()
    for move in moves[:4]:
        move.wait()
    position = places(slab_ref[...])
    base = base_ref[...]
    near = near_ref[...]
    a = base // (VY * Z)
    b = base // Z % VY
    c = base % Z
    fraction = off_ref[...].astype(F32)
    rows = [a + 2, b, c, near]
    meta = jnp.concatenate(
        [r.astype(F32) for r in rows] + [fraction, jnp.zeros((KINDS - 7, PTS), F32)], axis=0
    ).astype(BF)
    moves[4].wait()
    moves[5].wait()
    both = jnp.concatenate([feat_ref[...], cot_ref[...]], axis=1)
    group = 4
    sends = []
    for g in range(GY // group):
        span = group * CAP
        chosen = onehot(iota((span, PTS), 0) + g * span == position)
        packed = dot(chosen, both).astype(BF).reshape(group, CAP, 2 * C)
        here = pl.ds(g * group, group)
        sent_ref[here, 0:CAP, :] = packed[:, :, :C]
        sent_ref[here, CAP : 2 * CAP, :] = packed[:, :, C:]
        lanes = dot(meta, chosen, RIGHT)
        for i in range(group):
            piece = lanes[:, i * CAP : (i + 1) * CAP]
            wide = jnp.concatenate([piece, jnp.zeros((KINDS, C - CAP), F32)], axis=1)
            sent_ref[g * group + i, 2 * CAP : 2 * CAP + KINDS, :] = wide.astype(BF)
        sends.append(pltpu.make_async_copy(sent_ref.at[here], sent_hbm.at[here], out_sems.at[g]))
        sends[g].start()
    for send in sends:
        send.wait()


def slope(v, s):
    return s * (1.0 + v * (1.0 - s))


def mlp_kernel(feat_ref, cot_ref, mlp_ref, grad_ref):
    feat = feat_ref[...]
    pre = dot(feat, mlp_ref[...])
    grad_pre = (cot_ref[...].astype(F32) * slope(pre, sigmoid(pre))).astype(BF)
    grad_ref[...] = dot(grad_pre, feat, LEFT)


def arrived_meta(got_ref):
    return jnp.concatenate(
        [got_ref[t, 2 * CAP : 2 * CAP + KINDS, :].astype(F32)[:, :CAP] for t in range(GY)], axis=1
    )


def own_matrix(meta):
    near = meta[3:4].astype(jnp.int32)
    base = (meta[0:1] - 2.0) * (VY * Z) + meta[1:2] * Z + meta[2:3]
    own = base.astype(jnp.int32) + near // 4 * (VY * Z) + near // 2 % 2 * Z + near % 2
    return onehot(iota((CELLS, SLOTS), 0) == own)


def voxel_kernel(spot_ref, got_ref, vox_ref, near_ref, far_ref, div_ref, meta_ref):
    meta = arrived_meta(got_ref)
    meta_ref[...] = meta
    own_hot = own_matrix(meta)
    rows = got_ref[:, 0:CAP, :].reshape(SLOTS, C)
    both = jnp.concatenate([rows, jnp.ones((SLOTS, C), BF)], axis=1)
    total = dot(own_hot, both)
    divisor = jnp.maximum(total[:, C:], 1.0)
    div_ref[...] = divisor
    vox_ref[...] = (total[:, :C] / divisor).astype(BF).reshape(VX, VY, Z, C)
    core = spot_ref[0] % 2
    near_ref[...] = vox_ref[pl.ds((VX - 1) * (1 - core), 1)]
    far_ref[...] = vox_ref[pl.ds((VX - 1) * core, 1)]


def spread_kernel(got_ref, meta_ref, matrix_ref, grad_ref):
    meta = meta_ref[...]
    a, b, c = meta[0:1] - 2.0, meta[1:2], meta[2:3]
    fx, fy, fz = meta[4:5], meta[5:6], meta[6:7]

    def side(distance, fraction):
        return jnp.where(distance == 0.0, 1.0 - fraction, jnp.where(distance == 1.0, fraction, 0.0))

    plane = VY * Z
    place = iota((plane, SLOTS), 0)
    wy = side((place // Z).astype(F32) - b, fy)
    wz = side((place % Z).astype(F32) - c, fz)
    for x in range(VX):
        wx = side(x - a, fx)
        matrix_ref[x * plane : (x + 1) * plane, :] = ((wx * wy) * wz).astype(BF)
    cots = got_ref[:, CAP : 2 * CAP, :].reshape(SLOTS, C)
    grad_ref[...] = dot(matrix_ref[...], cots)


def flag(spot_ref, bit):
    return (spot_ref[0] // 2**bit % 2).astype(F32).astype(BF)


def edge_kernel(spot_ref, near_ref, own_ref, far_ref, even_ref, odd_ref):
    core = spot_ref[0] % 2
    turn = spot_ref[0] // 4 % 2
    inside = flag(spot_ref, 1)
    for ref, y in ((even_ref, (VY - 1) * (1 - turn)), (odd_ref, (VY - 1) * turn)):
        row = pl.ds(y, 1)
        ref[pl.ds((VX + 1) * (1 - core), 1)] = near_ref[:, row]
        ref[1 : VX + 1] = own_ref[:, row]
        ref[pl.ds((VX + 1) * core, 1)] = far_ref[:, row] * inside


def placer(spot_ref, wide_ref):
    def put(x, y, block, inside=None):
        nx, ny = block.shape[0], block.shape[1]
        if inside is not None:
            block = block * flag(spot_ref, inside)
        flat = block.reshape(nx * ny * Z, C).astype(F32)
        z = iota(flat.shape, 0) % Z
        blank = jnp.zeros((8, C), F32)
        down = jnp.concatenate([blank, flat], axis=0)[7 : 7 + flat.shape[0]]
        up = jnp.concatenate([flat, blank], axis=0)[1 : 1 + flat.shape[0]]
        down = jnp.where(z == 0, 0.0, down)
        up = jnp.where(z == Z - 1, 0.0, up)
        shape = (nx, ny, Z, C)
        planes, rows = pl.ds(x, nx), pl.ds(y, ny)
        wide_ref[planes, rows, :, 0:C] = down.astype(BF).reshape(shape)
        wide_ref[planes, rows, :, C : 2 * C] = block
        wide_ref[planes, rows, :, 2 * C :] = up.astype(BF).reshape(shape)

    return put


def assemble(spot_ref, wide_ref, own_ref, near_ref, far_ref):
    core = spot_ref[0] % 2
    put = placer(spot_ref, wide_ref)
    put(1, 1, own_ref[...])
    put((VX + 1) * (1 - core), 1, near_ref[...])
    put((VX + 1) * core, 1, far_ref[...], 1)


def add_rows(spot_ref, wide_ref, even_ref, odd_ref):
    turn = spot_ref[0] // 4 % 2
    put = placer(spot_ref, wide_ref)
    put(0, (VY + 1) * (1 - turn), even_ref[...])
    put(0, (VY + 1) * turn, odd_ref[...], 3)


def window(wide_ref, x, y):
    return wide_ref[x : x + VX, y : y + VY, :, :].reshape(CELLS, 3 * C)


def taps(weight_ref, k):
    return weight_ref[3 * k : 3 * k + 3].reshape(3 * C, C)


def inner_kernel(spot_ref, vox_ref, near_ref, far_ref, weight_ref, wide_ref, hidden_ref):
    assemble(spot_ref, wide_ref, vox_ref, near_ref, far_ref)
    blank = jnp.zeros((VX + 2, 1, Z, 3 * C), BF)
    wide_ref[:, 0:1] = blank
    wide_ref[:, VY + 1 :] = blank
    hidden = jnp.zeros((CELLS, C), F32)
    for k in range(9):
        hidden = hidden + dot(window(wide_ref, k // 3, k % 3), taps(weight_ref, k))
    hidden_ref[...] = hidden.reshape(VX, VY, Z, C)


def half_blocks(half, wide_ref, turned, mlp_ref, out_ref):
    def part(k):
        return dot(turned, wide_ref[pl.ds(k // 3, VX), pl.ds(k % 3, VY)].reshape(CELLS, 3 * C)).astype(out_ref.dtype)

    for i in range(4):
        blocks = part(5 * half + i)
        for j in range(3):
            out_ref[3 * i + half + j] = blocks[:, j * C : (j + 1) * C]
    blocks = part(4)

    @pl.when(half == 0)
    def _():
        out_ref[12] = blocks[:, 0:C]
        out_ref[13] = blocks[:, C : 2 * C]

    @pl.when(half == 1)
    def _():
        out_ref[0] = blocks[:, 2 * C :]
        out_ref[13] = mlp_ref[...].astype(out_ref.dtype)


def conv_kernel(spot_ref, inner_ref, hidden_ref, even_ref, odd_ref, weight_ref, gout_ref, mlp_ref,
                send_ref, wide_ref, turned_ref, act_ref, hid_ref, in_ref, out_ref, sum_ref):
    wide_ref[...] = inner_ref[...]
    add_rows(spot_ref, wide_ref, even_ref, odd_ref)
    sum_ref[...] = hidden_ref[...]
    for y, at, dy in ((0, 0, 0), (VY - 1, VY + 1, 2)):
        more = jnp.zeros((VX * Z, C), F32)
        for dx in range(3):
            row = wide_ref[dx : dx + VX, at].reshape(VX * Z, 3 * C)
            more = more + dot(row, taps(weight_ref, 3 * dx + dy))
        sum_ref[:, y] += more.reshape(VX, Z, C)
    hidden = sum_ref[...].reshape(CELLS, C)
    s = sigmoid(hidden)
    act_ref[...] = (hidden * s).astype(BF)
    grad_hidden = (gout_ref[...] * slope(hidden, s)).astype(BF)
    core = spot_ref[0] % 2
    hid_ref[...] = grad_hidden.reshape(VX, VY, Z, C)
    in_ref[...] = hid_ref[pl.ds((VX - 1) * (1 - core), 1)]
    out_ref[...] = hid_ref[pl.ds((VX - 1) * core, 1)]
    turned = grad_hidden.astype(F32).T.astype(BF)
    turned_ref[...] = turned
    half_blocks(1 - core, wide_ref, turned, mlp_ref, send_ref)


def keep_kernel(spot_ref, wide_ref, turned_ref, mlp_ref, keep_ref):
    half_blocks(spot_ref[0] % 2, wide_ref, turned_ref[...], mlp_ref, keep_ref)


def sample_kernel(matrix_ref, act_ref, out_ref):
    out_ref[...] = dot(matrix_ref[...], act_ref[...], LEFT).astype(BF).reshape(GY, CAP, C)


def deliver(filled_ref, share, out_hbm, out_ref, sems):
    moves = []
    for g in range(4):
        here = pl.ds(8 * g, 8)
        out_ref[here, 0:CAP, :] = filled_ref[here]
        out_ref[here, CAP:, :] = share(8 * g)
        moves.append(pltpu.make_async_copy(out_ref.at[here], out_hbm.at[here], sems.at[g]))
        moves[g].start()
    for move in moves:
        move.wait()


def join_kernel(keep_ref, got_ref, filled_ref, out_hbm, out_ref, sems):
    total = (keep_ref[...] + got_ref[...].astype(F32)).reshape(GY, SHARE, C)
    deliver(filled_ref, lambda t: total[t : t + 8].astype(BF), out_hbm, out_ref, sems)


def share_kernel(got_ref, out_ref):
    out_ref[...] = jnp.sum(got_ref[:, CAP:, :].astype(F32), axis=0).astype(BF)


def back_kernel(spot_ref, hid_ref, near_ref, far_ref, even_ref, odd_ref, weight_ref, meta_ref, div_ref, out_ref, wide_ref):
    assemble(spot_ref, wide_ref, hid_ref, near_ref, far_ref)
    add_rows(spot_ref, wide_ref, even_ref, odd_ref)
    total = jnp.zeros((CELLS, C), F32)
    for k in range(9):
        taps = jnp.concatenate([weight_ref[3 * k + 2 - j] for j in range(3)], axis=1)
        total = total + dot(window(wide_ref, 2 - k // 3, 2 - k % 3), taps, RIGHT)
    mean = (total / div_ref[...]).astype(BF)
    out_ref[...] = dot(own_matrix(meta_ref[...]), mean, LEFT).astype(BF).reshape(GY, CAP, C)


def deal_kernel(spot_ref, own_ref, one_ref, two_ref, three_ref, filled_ref, out_hbm, part_ref, out_ref, sems):
    y = spot_ref[0] // 16
    for k, ref in enumerate((own_ref, one_ref, two_ref, three_ref)):
        part_ref[y ^ k] = ref[...].astype(F32)
    total = jnp.sum(part_ref[...], axis=0).astype(BF)
    spread = jnp.broadcast_to(total[None], (8, SHARE, C))
    deliver(filled_ref, lambda t: spread, out_hbm, out_ref, sems)


def unpack(pos, got_ref):
    rows = got_ref[:, 0:CAP, :].reshape(SLOTS, C)
    chosen = jnp.concatenate(
        [onehot(iota((PTS, C), 1) + i * C == pos) for i in range(SLOTS // C)], axis=1
    )
    return dot(chosen, rows)


def forward_kernel(got_ref, slab_ref, feat_ref, cot_ref, mlp_ref, out_ref, pos_ref, back_ref):
    spread = jnp.broadcast_to(places(slab_ref[...]).astype(F32), (C, PTS))
    pos = spread.T.astype(jnp.int32)
    pos_ref[...] = pos
    weight = mlp_ref[...]
    pre = dot(feat_ref[...], weight)
    s = sigmoid(pre)
    grad_pre = (cot_ref[...].astype(F32) * slope(pre, s)).astype(BF)
    back_ref[...] = dot(grad_pre, weight, RIGHT)
    sampled = unpack(pos, got_ref).astype(BF).astype(F32)
    out_ref[...] = (sampled + pre * s).astype(BF)


def take_kernel(got_ref, out_ref):
    out_ref[...] = got_ref[:, CAP:, :].astype(F32).reshape(HALF, C, C).astype(BF)


def backward_kernel(got_ref, pos_ref, back_ref, out_ref):
    out_ref[...] = (unpack(pos_ref[...], got_ref) + back_ref[...]).astype(BF)


def weights_kernel(spot_ref, mine_ref, other_ref, conv_hbm, mlp_hbm, conv_ref, mlp_ref, sems):
    moves = [
        pltpu.make_async_copy(conv_ref.at[pl.ds(9 * k, 9)], conv_hbm.at[pl.ds(9 * k, 9)], sems.at[k])
        for k in range(3)
    ]
    moves.append(pltpu.make_async_copy(mlp_ref, mlp_hbm, sems.at[3]))

    def fill(first_ref, second_ref, k):
        for o in range(9 * k, 9 * k + 9):
            half = first_ref[o] if o < HALF else second_ref[o - HALF]
            conv_ref[o] = half.astype(F32).T * (1.0 / math.sqrt(GX * GY * CELLS))
        if k == 2:
            mlp_ref[...] = second_ref[HALF - 1].astype(F32).T * (1.0 / math.sqrt(GX * GY * PTS))

    for k in range(3):

        @pl.when(spot_ref[0] % 2 == 0)
        def _():
            fill(mine_ref, other_ref, k)

        @pl.when(spot_ref[0] % 2 == 1)
        def _():
            fill(other_ref, mine_ref, k)

        moves[k].start()
    moves[3].start()
    for move in moves:
        move.wait()


FACE = sds((1, VY, Z, C), BF)
EDGE = sds((VX + 2, 1, Z, C), BF)


def pairs(count, start):
    swaps = [(i, (i + 1) % count) for i in range(start, count, 2)]
    return swaps + [(j, i) for i, j in swaps]


def chips(face):
    return lax.ppermute(face, ("y", "c"), pairs(GX, 1))


def edges(spot, near, cells, far):
    even, odd = call(edge_kernel, (EDGE, EDGE), (spot, near, cells, far), smem=1, mib=2)
    odds = [(s * GY + i, s * GY + j) for s in range(GX) for i, j in pairs(GY, 1) if abs(i - j) == 1]
    ends = [(s * GY + i, (s ^ 1) * GY + i) for s in range(GX) for i in (0, GY - 1)]
    return (
        lax.ppermute(even, ("x", "z"), pairs(GY, 0)),
        lax.ppermute(odd, ("y", "c", "x", "z"), odds + ends),
    )


def exchange(rows):
    return lax.all_to_all(rows, ("x", "z"), split_axis=0, concat_axis=0, tiled=True)


def across(share, partner):
    return lax.ppermute(share, "y", list(enumerate(partner)))


def swap(half):
    return lax.ppermute(half, "c", [(0, 1), (1, 0)])


def body(features, point_slab, base_cell, nearest, offsets, conv_weight, mlp_weight, cotangent):
    strip = lax.axis_index(("y", "c"))
    slab_here = lax.axis_index(("x", "z"))
    core = lax.axis_index("c")
    core = core + 16 * (strip // 2) + 2 * (strip % (GX - 1) != 0) + 4 * (slab_here % 2) + 8 * (slab_here % (GY - 1) != 0)
    spot = core.reshape(1)
    point_slab, spot = lax.optimization_barrier((point_slab, spot))
    slab = point_slab.reshape(1, PTS)
    line = pltpu.VMEM((1, PTS), jnp.int32)
    sent = call(
        pack_kernel,
        sds((GY, 2 * CAP + KINDS, C), BF),
        (features, cotangent, slab, base_cell.reshape(1, PTS), nearest.reshape(1, PTS), offsets),
        scratch=(
            pltpu.VMEM((PTS, C), BF),
            pltpu.VMEM((PTS, C), BF),
            line,
            line,
            line,
            pltpu.VMEM((3, PTS), BF),
            pltpu.VMEM((GY, 2 * CAP + KINDS, C), BF),
            pltpu.SemaphoreType.DMA((6,)),
            pltpu.SemaphoreType.DMA((8,)),
        ),
        hbm=6,
        mib=60,
        out=HBM,
    )
    got = exchange(sent)
    mlp_grad = call(mlp_kernel, sds((C, C), F32), (features, cotangent, mlp_weight))
    got, mlp_grad = lax.optimization_barrier((got, mlp_grad))
    cells = sds((VX, VY, Z, C), BF)
    voxels, near, far, divisor, meta = call(
        voxel_kernel,
        (cells, FACE, FACE, sds((CELLS, C), F32), sds((KINDS, SLOTS), F32)),
        (spot, got),
        smem=1,
    )
    far = chips(far)
    near = swap(near)
    matrix, grad_out = call(
        spread_kernel, (sds((CELLS, SLOTS), BF), sds((CELLS, C), F32)), (got, meta)
    )
    near, far, matrix, grad_out = lax.optimization_barrier((near, far, matrix, grad_out))
    even, odd = edges(spot, near, voxels, far)
    spread = sds((VX + 2, VY + 2, Z, 3 * C), BF)
    inner, hidden = call(
        inner_kernel,
        (spread, sds((VX, VY, Z, C), F32)),
        (spot, voxels, near, far, conv_weight),
        smem=1,
    )
    wide = pltpu.VMEM((VX + 2, VY + 2, Z, 3 * C), BF)
    block = sds((GY, ROWS, C), BF)
    rows = sds((GY, CAP, C), BF)
    half = sds((HALF, C, C), BF)
    send, full, turned, act, grad_hidden, near, far = call(
        conv_kernel,
        (half, spread, sds((C, CELLS), BF), sds((CELLS, C), BF), cells, FACE, FACE),
        (spot, inner, hidden, even, odd, conv_weight, grad_out, mlp_grad),
        scratch=(pltpu.VMEM((VX, VY, Z, C), F32),),
        smem=1,
    )
    arrived = swap(send)
    keep = call(keep_kernel, sds((HALF, C, C), F32), (spot, full, turned, mlp_grad), smem=1)
    filled = call(sample_kernel, rows, (matrix, act))
    sending = (pltpu.VMEM(block.shape, BF), pltpu.SemaphoreType.DMA((4,)))
    joined = call(join_kernel, block, (keep, arrived, filled), scratch=sending, out=HBM)
    first = exchange(joined)
    far = chips(far)
    near = swap(near)
    grad_faces = (near, far) + edges(spot, near, grad_hidden, far)
    first, grad_faces = lax.optimization_barrier((first, grad_faces))
    filled = call(
        back_kernel,
        rows,
        (spot, grad_hidden) + grad_faces + (conv_weight, meta, divisor),
        scratch=(wide,),
        smem=1,
    )
    share = call(share_kernel, sds((SHARE, C), BF), (first,), mib=4)
    others = tuple(across(share, [y ^ k for y in range(4)]) for k in (1, 2, 3))
    joined = call(
        deal_kernel,
        block,
        (spot, share) + others + (filled,),
        scratch=(pltpu.VMEM((4, SHARE, C), F32),) + sending,
        smem=1,
        out=HBM,
    )
    second = exchange(joined)
    output, position, back = call(
        forward_kernel,
        (sds((PTS, C), BF), sds((PTS, C), jnp.int32), sds((PTS, C), F32)),
        (first, slab, features, cotangent, mlp_weight),
    )
    second, back = lax.optimization_barrier((second, back))
    mine = call(take_kernel, sds((HALF, C, C), BF), (second,), mib=4)
    other = swap(mine)
    grad_features = call(backward_kernel, sds((PTS, C), BF), (second, position, back))
    grad_conv, grad_mlp = call(
        weights_kernel,
        (sds((27, C, C), F32), sds((C, C), F32)),
        (spot, mine, other),
        scratch=(
            pltpu.VMEM((27, C, C), F32),
            pltpu.VMEM((C, C), F32),
            pltpu.SemaphoreType.DMA((4,)),
        ),
        smem=1,
        out=HBM,
    )
    return (output, grad_features, grad_conv, grad_mlp)


def solution(mesh):
    fine = Mesh(mesh.devices.reshape(4, 2, 4, 8), ("y", "c", "x", "z"))
    rows = ("y", "c", "x", "z")
    in_specs = (P(rows, None), P(rows, None), P(rows), P(rows), P(None, rows), P(), P(), P(rows, None))
    out_specs = (P(rows, None), P(rows, None), P(), P())
    return jax.shard_map(body, mesh=fine, in_specs=in_specs, out_specs=out_specs, check_vma=False)
```
